128 devices in a mesh: loader: 4 (over z_hi, core), centers: 32 (over y, z_lo, x).
Axes of the slice: x: 4, y: 4, z: 4 (z_hi: 2, z_lo: 2; z = z_hi * 2 + z_lo), core: 2. Of those that a mesh axis runs over, the one named last changes fastest.
Arguments:
- pool: bfloat16 [32768, 256], P('loader'), may hold values from -6 to 6
- batch_index: int32 [2048], replicated, may hold values from 0 to 32767
- targets: float32 [16, 2048], replicated, may hold values from -6 to 6
- centers: bfloat16 [1048576, 256], P(('loader', 'centers')), may hold values from -6 to 6
- weights: float32 [16, 1048576], P(None, ('loader', 'centers')), may hold values from -1.8 to 1.8
- nys_index: int32 [8192], P(('loader', 'centers')), may hold values from 0 to 8191, as said below
- eigvecs: float32 [8192, 128], P(('loader', 'centers')), may hold values from -0.0625 to 0.0625
- damping: float32 [128], replicated, may hold values from 1 to 30
Outputs:
- new_weights: float32 [16, 1048576], P(None, ('loader', 'centers'))
- predictions: float32 [16, 2048], replicated
The draws below stay inside these ranges and needn't reach their ends.
Inputs may be any that keep to these rules, and one draw needn't show every extreme that they name: `nys_index`: each device's block of 64 entries names distinct local rows of that device's own 8192 centers; entry k lies in [k * 128, (k + 1) * 128); the first is 0 and the last 8191.
All inputs are finite; a program needn't handle non-finite values.
Results may differ from the reference program's by a relative error of at most 0.0049.
Values may be sent and summed in bfloat16 or wider, within the bound.
No kernel may reach another device: no remote copies, remote signals or barrier semaphores. Data moves between devices by JAX's collectives and lax.ppermute only.
A program may use at most 256 MiB of HBM per device.

```python
import math
import jax
import jax.numpy as jnp
from jax import lax

D = 256
OUT = 16
EIG_TOP = 128
C_DEV = 8192
BATCH = 2048
NYS_DEV = 64
CENTERS = 1048576
POOL = 32768
NYS = 8192
N_LOADER = 4
N_CENTERS = 32


def draw_nys_index(key, part):
    blocks = NYS // NYS_DEV
    stride = C_DEV // NYS_DEV
    offsets = jax.random.randint(key, (blocks, NYS_DEV), 0, stride)
    base = jnp.arange(NYS_DEV, dtype=jnp.int32) * stride
    picked = base[None, :] + offsets
    picked = picked.at[:, 0].set(0)
    picked = picked.at[:, NYS_DEV - 1].set(C_DEV - 1)
    return picked.reshape(-1).astype(jnp.int32)


def place_ends(values, key, least, largest):
    longest = values.shape.index(max(values.shape))
    spots = []
    for shift in (0, 1):
        where = [jax.random.randint(jax.random.fold_in(key, axis), (), 0, length) for axis, length in enumerate(values.shape)]
        where[longest] = (where[longest] + shift) % values.shape[longest]
        spots.append(tuple(where))
    return values.at[spots[0]].set(least).at[spots[1]].set(largest)


def shard_levels(stream_key, shape, split, low, largest):
    level = 1.0
    for position, shards_of in split:
        steps = jax.random.uniform(jax.random.fold_in(jax.random.fold_in(stream_key, 6), position), (shards_of,), jnp.float32, low / len(split), largest / len(split))
        level = level * jnp.repeat(jnp.exp(steps), shape[position] // shards_of).reshape((-1,) + (1,) * (len(shape) - 1 - position))
    return level


def noise(key, shape, deviation, most, split=(), held_as=jnp.bfloat16):
    array = jax.random.normal(key, shape, jnp.float32) * deviation
    if len(split) > 0:
        array = shard_levels(key, shape, split, -0.22, 0.18) * array
    return jnp.clip(array, min=-most, max=most).astype(held_as)


def setup_inputs(seed: int = 0) -> dict:
    key_list = jax.random.split(jax.random.key(seed), 9)
    return {
        "pool": noise(key_list[0], (POOL, D), 1.0, 6.0, ((0, 4),)),
        "batch_index": place_ends(jax.random.randint(key_list[1], (BATCH,), 0, POOL), jax.random.fold_in(key_list[1], 1), 0, POOL - 1).astype(jnp.int32),
        "targets": noise(key_list[2], (OUT, BATCH), 1.0, 6.0, (), jnp.float32),
        "centers": noise(key_list[3], (CENTERS, D), 1.0, 6.0, ((0, 128),)),
        "weights": noise(key_list[4], (OUT, CENTERS), 0.3, 1.8, ((1, 128),), jnp.float32),
        "nys_index": draw_nys_index(jax.random.fold_in(key_list[8], 71), 0),
        "eigvecs": noise(key_list[6], (NYS, EIG_TOP), NYS ** -0.5, 0.0625, ((0, 128),), jnp.float32),
        "damping": jnp.clip(jnp.exp(jax.random.uniform(key_list[7], (EIG_TOP,), jnp.float32, math.log(1.0), math.log(30.0))), 1.0, 30.0),
    }


def kernel_tile(rows, block):
    row_sq = lax.optimization_barrier(jnp.sum(rows.astype(jnp.float32) * rows.astype(jnp.float32), axis=1))
    cen_sq = lax.optimization_barrier(jnp.sum(block.astype(jnp.float32) * block.astype(jnp.float32), axis=1))
    cross = jnp.dot(rows, block.T, preferred_element_type=jnp.float32)
    dist_sq = row_sq[:, None] + cen_sq[None, :] - 2.0 * cross
    return jnp.exp(-4.0 * jnp.sqrt(dist_sq) / math.sqrt(D)).astype(jnp.bfloat16)

def reference(pool, batch_index, targets, centers, weights, nys_index, eigvecs, damping):
    shards = N_LOADER * N_CENTERS
    batch = pool[batch_index.astype(jnp.int32)]
    cen_blocks = centers.reshape(shards, C_DEV, D)
    w_blocks = jnp.transpose(weights.reshape(OUT, shards, C_DEV), (1, 0, 2))
    idx_blocks = nys_index.reshape(shards, NYS_DEV).astype(jnp.int32)
    eig_blocks = eigvecs.reshape(shards, NYS_DEV, EIG_TOP)

    def pred_step(total, pair):
        block, w_block = pair
        kern = kernel_tile(batch, block)
        w_half = w_block.astype(jnp.bfloat16)
        return (total + jnp.dot(w_half, kern.T, preferred_element_type=jnp.float32), None)
    predictions, _ = lax.scan(pred_step, jnp.zeros((OUT, BATCH), jnp.float32), (cen_blocks, w_blocks))
    resid = (predictions - targets).astype(jnp.bfloat16)

    def grad_step(total, trio):
        block, idx, eig = trio
        kern = kernel_tile(batch, block)
        grad = jnp.dot(resid, kern, preferred_element_type=jnp.float32)
        grad_nys = grad[:, idx]
        part = jnp.dot(grad_nys, eig, precision=lax.Precision.HIGHEST, preferred_element_type=jnp.float32)
        return (total + part, grad)
    coeff, grads = lax.scan(grad_step, jnp.zeros((OUT, EIG_TOP), jnp.float32), (cen_blocks, idx_blocks, eig_blocks))

    def update(w_block, grad, idx, eig):
        delta = jnp.dot(coeff * damping[None, :], eig.T, precision=lax.Precision.HIGHEST, preferred_element_type=jnp.float32)
        fresh = w_block - 2.0 * grad
        return fresh.at[:, idx].add(2.0 * delta)
    new_blocks = jax.vmap(update)(w_blocks, grads, idx_blocks, eig_blocks)
    new_weights = jnp.transpose(new_blocks, (1, 0, 2)).reshape(OUT, shards * C_DEV)
    return (new_weights, predictions)
```

```python
import math

import jax
import jax.numpy as jnp
from jax import lax
from jax.experimental import pallas as pl
from jax.experimental.pallas import tpu as pltpu
from jax.sharding import Mesh
from jax.sharding import PartitionSpec as P

f32, bf16 = jnp.float32, jnp.bfloat16
MIB = 2**20
LOADER = ("zh", "core")
CENTERS = ("y", "zl", "x")
ALL = LOADER + CENTERS
D = 256
CHUNKS = 2
LANES = 128
RATE = -4.0 / math.sqrt(D) * math.log2(math.e)
VMEM = pl.BlockSpec(memory_space=pltpu.VMEM)
SMEM = pl.BlockSpec(memory_space=pltpu.SMEM)
NT = (((1,), (1,)), ((), ()))


def laplacian(dist_sq):
    safe = jnp.maximum(dist_sq, 1e-30)
    return jnp.exp2(safe * lax.rsqrt(safe) * RATE).astype(bf16)


def load_rows(core_ref, own_ref, other_ref, rows_ref, sq_ref):
    half = own_ref.shape[0]
    for ref, place in ((own_ref, core_ref[0]), (other_ref, 1 - core_ref[0])):
        at = pl.ds(pl.multiple_of(place * half, half), half)
        rows = ref[...]
        wide = rows.astype(f32)
        rows_ref[at, :] = rows * (-2)
        sq_ref[at, :] = jnp.broadcast_to(jnp.sum(wide * wide, axis=1, keepdims=True), (half, LANES))


def values_kernel(core_ref, w_ref, cen_ref, own_ref, other_ref, cen_sq_ref, kern_ref, pred_ref, rows_ref, sq_ref, acc_ref):
    batch, count = kern_ref.shape
    col, row = 2048, 256
    load_rows(core_ref, own_ref, other_ref, rows_ref, sq_ref)
    acc_ref[...] = jnp.zeros_like(acc_ref)

    def step(i, carry):
        cols = pl.ds(pl.multiple_of(i * col, col), col)
        cen = cen_ref[cols, :]
        w = w_ref[:, cols]
        cen_sq = cen_sq_ref[:, cols]
        for j in range(batch // row):
            at = slice(j * row, (j + 1) * row)
            cross = lax.dot_general(rows_ref[at, :], cen, NT, preferred_element_type=f32)
            row_sq = jnp.concatenate([sq_ref[at, :]] * (col // LANES), axis=1)
            kern = laplacian((cross + row_sq) + cen_sq)
            kern_ref[at, cols] = kern
            acc_ref[:, at] += lax.dot_general(w, kern, NT, preferred_element_type=f32)
        return carry

    lax.fori_loop(0, count // col, step, 0)
    for r in range(batch // LANES):
        pred_ref[:, r, :] = acc_ref[:, r * LANES : (r + 1) * LANES]


def kernel_values(core, w_half, centers, own, other, cen_sq):
    batch, count = 2 * own.shape[0], centers.shape[0]
    return pl.pallas_call(
        values_kernel,
        in_specs=[SMEM] + [VMEM] * 5,
        out_specs=[VMEM, VMEM],
        out_shape=[
            pltpu.VMEM((batch, count), bf16),
            jax.ShapeDtypeStruct((w_half.shape[0], batch // LANES, LANES), f32),
        ],
        scratch_shapes=[
            pltpu.VMEM((batch, D), bf16),
            pltpu.VMEM((batch, LANES), f32),
            pltpu.VMEM((w_half.shape[0], batch), f32),
        ],
        compiler_params=pltpu.CompilerParams(vmem_limit_bytes=16 * MIB),
        cost_estimate=pl.CostEstimate(
            flops=8 * batch * count * D, bytes_accessed=2 * batch * count, transcendentals=2 * batch * count
        ),
        name="kernel_values",
    )(core, w_half, centers, own, other, cen_sq)


def nystrom_kernel(core_ref, cen_ref, sq_ref, hi_ref, lo_ref, *refs):
    pieces, (out_ref, acc_ref) = refs[:-2], refs[-2:]
    cen = cen_ref[...]
    half = pieces[0].shape[0]
    for n, ref in enumerate(pieces):
        place = core_ref[0] if n % 2 == 0 else 1 - core_ref[0]
        first = (n // 2 * 2 + place) * (half // LANES)
        rows = ref[...]
        wide = rows.astype(f32)
        cross = lax.dot_general(rows * (-2), cen, NT, preferred_element_type=f32)
        kern = laplacian((cross + jnp.sum(wide * wide, axis=1, keepdims=True)) + sq_ref[...])
        part = lax.dot_general(hi_ref[...], kern, NT, preferred_element_type=f32)
        part += lax.dot_general(lo_ref[...], kern, NT, preferred_element_type=f32)
        for r in range(half // LANES):
            acc_ref[:, pl.ds(first + r, 1), :] = part[:, None, r * LANES : (r + 1) * LANES]
    out_ref[...] = acc_ref[...].astype(bf16)


def nystrom_terms(core, nys_cen, eigvecs, pieces):
    wide = nys_cen.astype(f32)
    nys_sq = jnp.sum(wide * wide, axis=1)[None, :]
    eig_t = eigvecs.T
    hi = eig_t.astype(bf16)
    lo = (eig_t - hi.astype(f32)).astype(bf16)
    blocks = sum(p.shape[0] for p in pieces) // LANES
    shape = (eig_t.shape[0], blocks, LANES)
    return pl.pallas_call(
        nystrom_kernel,
        in_specs=[SMEM] + [VMEM] * (4 + len(pieces)),
        out_specs=VMEM,
        out_shape=jax.ShapeDtypeStruct(shape, bf16),
        scratch_shapes=[pltpu.VMEM(shape, f32)],
        compiler_params=pltpu.CompilerParams(vmem_limit_bytes=12 * MIB),
        cost_estimate=pl.CostEstimate(flops=2 * 10**9, bytes_accessed=2**20, transcendentals=2**18),
        name="nystrom_terms",
    )(core, nys_cen, nys_sq, hi, lo, *pieces)


def grad_kernel(pred_ref, tgt_ref, kern_ref, out_pred_ref, resid_ref, out_ref):
    count = kern_ref.shape[1]
    col = 1024
    for r in range(pred_ref.shape[1]):
        at = slice(r * LANES, (r + 1) * LANES)
        pred = pred_ref[:, r, :]
        out_pred_ref[:, at] = pred
        resid_ref[:, at] = (pred - tgt_ref[:, at]).astype(bf16)
    resid = resid_ref[...]
    for i in range(count // col):
        at = slice(i * col, (i + 1) * col)
        out_ref[:, at] = jnp.dot(resid, kern_ref[:, at], preferred_element_type=f32)


def grad_terms(pred, targets, kern):
    outs, count = targets.shape[0], kern.shape[1]
    return pl.pallas_call(
        grad_kernel,
        in_specs=[VMEM] * 3,
        out_specs=[VMEM] * 3,
        out_shape=[
            jax.ShapeDtypeStruct(targets.shape, f32),
            jax.ShapeDtypeStruct(targets.shape, bf16),
            jax.ShapeDtypeStruct((outs, count), f32),
        ],
        compiler_params=pltpu.CompilerParams(vmem_limit_bytes=8 * MIB),
        cost_estimate=pl.CostEstimate(flops=32 * kern.size, bytes_accessed=2 * kern.size, transcendentals=0),
        name="grad_terms",
    )(pred, targets, kern)


def update_kernel(idx_ref, damp_ref, eig_ref, w_ref, *refs):
    n = (len(refs) - 1) // 3
    grads, resids, moments, out_ref = refs[:n], refs[n : 2 * n], refs[2 * n : 3 * n], refs[-1]
    coeff = 0.0
    for resid_ref, moment_ref in zip(resids, moments):
        for r in range(moment_ref.shape[0]):
            at = slice(r * LANES, (r + 1) * LANES)
            coeff += lax.dot_general(resid_ref[:, at], moment_ref[r], NT, preferred_element_type=f32)
    delta = lax.dot_general(
        coeff * damp_ref[...], eig_ref[...], NT, precision=lax.Precision.HIGHEST, preferred_element_type=f32
    )
    lane = lax.broadcasted_iota(jnp.int32, (w_ref.shape[0], LANES), 1)
    for k in range(delta.shape[1]):
        at = slice(k * LANES, (k + 1) * LANES)
        total = grads[0][:, at]
        for grad_ref in grads[1:]:
            total += grad_ref[:, at]
        shift = jnp.where(lane == idx_ref[k] - k * LANES, 2.0 * delta[:, k : k + 1], 0.0)
        out_ref[:, at] = (w_ref[:, at] - 2.0 * total) + shift


def update(nys_index, damping, eigvecs, weights, grads, resids, moments):
    return pl.pallas_call(
        update_kernel,
        in_specs=[SMEM] + [VMEM] * (3 + 3 * len(grads)),
        out_specs=VMEM,
        out_shape=jax.ShapeDtypeStruct(weights.shape, f32),
        compiler_params=pltpu.CompilerParams(vmem_limit_bytes=12 * MIB),
        name="update",
    )(nys_index, damping[None, :], eigvecs, weights, *grads, *resids, *moments)


def pick_rows(pool, wanted):
    held = pool.shape[0]
    local = wanted - lax.axis_index(LOADER) * held
    owned = (local >= 0) & (local < held)
    rows = pool[jnp.clip(local, 0, held - 1)]
    return jnp.where(owned[:, None], rows, jnp.zeros_like(rows))


def swap(x, axis):
    return lax.ppermute(x, axis, [(0, 1), (1, 0)])


def exchange(x, axes):
    return lax.all_to_all(x, axes, split_axis=0, concat_axis=0, tiled=True)


def spread(x, axes):
    return exchange(jnp.broadcast_to(x[None], (lax.axis_size(axes),) + x.shape), axes)


def body(pool, batch_index, targets, centers, weights, nys_index, eigvecs, damping):
    outs, total = targets.shape
    core = lax.axis_index("core")
    groups = lax.axis_size(CENTERS)
    share = total // (CHUNKS * 2 * groups)
    mine = lax.dynamic_index_in_dim(
        batch_index.reshape(CHUNKS * 2, groups, share), lax.axis_index(CENTERS), 1, keepdims=False
    )
    rows = pick_rows(pool, mine.reshape(-1)).reshape(CHUNKS, 2, share, D)
    keep = lax.dynamic_index_in_dim(rows, core, 1, keepdims=False)
    give = lax.dynamic_index_in_dim(rows, 1 - core, 1, keepdims=False)
    rows = keep + swap(give, "core")
    rows = rows + swap(rows, "zh")
    own = [spread(rows[q], CENTERS).reshape(groups * share, D) for q in range(CHUNKS)]
    other = [swap(x, "core") for x in own]

    wide = centers.astype(f32)
    cen_sq = jnp.sum(wide * wide, axis=1)[None, :]
    w_half = weights.astype(bf16)
    where = core.astype(jnp.int32)[None]

    pieces = [p for pair in zip(own, other) for p in pair]
    moment = nystrom_terms(where, centers[nys_index], eigvecs, pieces)
    moment = jnp.sum(exchange(moment, ALL).astype(f32), axis=0).astype(bf16)
    moment = jnp.transpose(spread(moment, ALL), (1, 0, 2))

    preds, grads, resids, moments = [], [], [], []
    width = total // CHUNKS
    for q in range(CHUNKS):
        kern, pred = kernel_values(where, w_half, centers, own[q], other[q], cen_sq)
        shape = pred.shape
        pred = jnp.sum(exchange(pred.reshape(-1, 1, LANES), ALL), axis=0)
        pred = spread(pred, ALL).reshape(shape)
        pred, resid, grad = grad_terms(pred, targets[:, q * width : (q + 1) * width], kern)
        preds.append(pred)
        resids.append(resid)
        grads.append(grad)
        moments.append(moment[q * (width // LANES) : (q + 1) * (width // LANES)])
    fresh = update(nys_index, damping, eigvecs, weights, grads, resids, moments)
    return fresh, jnp.concatenate(preds, axis=1)


def solution(mesh):
    fine = Mesh(mesh.devices.reshape(2, 2, 4, 2, 4), ALL)
    return jax.shard_map(
        body,
        mesh=fine,
        in_specs=(
            P(LOADER, None),
            P(),
            P(),
            P(ALL, None),
            P(None, ALL),
            P(ALL),
            P(ALL, None),
            P(),
        ),
        out_specs=(P(None, ALL), P()),
        check_vma=False,
    )
```

```python
import functools
import math

import jax
import jax.numpy as jnp
from jax import lax
from jax.experimental import pallas as pl
from jax.experimental.pallas import tpu as pltpu
from jax.sharding import Mesh
from jax.sharding import PartitionSpec as P

f32, bf16 = jnp.float32, jnp.bfloat16
MIB = 2**20
LOADER = ("zh", "core")
CENTERS = ("y", "zl", "x")
ALL = LOADER + CENTERS
CHIPS = ("zh",) + CENTERS
PACK = 24
D = 256
LANES = 128
RATE = -4.0 / math.sqrt(D) * math.log2(math.e)
VMEM = pl.BlockSpec(memory_space=pltpu.VMEM)
SMEM = pl.BlockSpec(memory_space=pltpu.SMEM)
ANY = pl.BlockSpec(memory_space=pl.ANY)
HBM = pl.BlockSpec(memory_space=pltpu.HBM)
NT = (((1,), (1,)), ((), ()))


def laplacian(dist_sq):
    safe = jnp.maximum(dist_sq, 1e-30)
    return jnp.exp2(safe * lax.rsqrt(safe) * RATE).astype(bf16)


def pick_kernel(place_ref, index_ref, pool_ref, keep_ref, give_ref, held_ref, sems):
    share = keep_ref.shape[0]
    group = held_ref.shape[1]
    total = index_ref.shape[0]
    mine, core, first = place_ref[0], place_ref[1], place_ref[2]
    rows = pool_ref.shape[0]

    def local(n):
        half = core if n < share else 1 - core
        return index_ref[half * (total // 2) + first + n % share] - mine * rows

    def copy(n):
        at = jnp.clip(local(n), 0, rows - 1) // group * group
        return pltpu.make_async_copy(pool_ref.at[pl.ds(pl.multiple_of(at, group), group), :], held_ref.at[n], sems.at[n])

    for n in range(2 * share):
        copy(n).start()
    line = lax.broadcasted_iota(jnp.int32, (group, D), 0)
    for ref, base in ((keep_ref, 0), (give_ref, share)):
        picked = []
        for n in range(base, base + share):
            copy(n).wait()
            here = local(n)
            owned = jnp.logical_and(here >= 0, here < rows)
            spot = jnp.where(owned, lax.rem(jnp.clip(here, 0, rows - 1), group), -1)
            block = held_ref[n].astype(f32)
            picked.append(jnp.sum(jnp.where(line == spot, block, 0.0), axis=0, keepdims=True))
        ref[...] = jnp.concatenate(picked, axis=0).astype(bf16)


def pick_rows(place, batch_index, pool, share):
    group = 16
    return pl.pallas_call(
        pick_kernel,
        in_specs=[SMEM, SMEM, ANY],
        out_specs=[VMEM, VMEM],
        out_shape=[jax.ShapeDtypeStruct((share, D), bf16)] * 2,
        scratch_shapes=[pltpu.VMEM((2 * share, group, D), bf16), pltpu.SemaphoreType.DMA((2 * share,))],
        compiler_params=pltpu.CompilerParams(vmem_limit_bytes=4 * MIB),
        name="pick_rows",
    )(place, batch_index, pool)


def values_kernel(core_ref, w_ref, batch_ref, cen_sq_ref, cen_ref, *refs, first):
    n_out = 2 if first else 3
    outs_ref, (rows_ref, sq_ref, acc_ref, held_ref, sems) = refs[-5 - n_out : -5], refs[-5:]
    kern_ref = outs_ref[0]
    batch, count = kern_ref.shape
    col, row = held_ref.shape[1], 256
    steps = count // col

    def fetch(i):
        return pltpu.make_async_copy(cen_ref.at[pl.ds(pl.multiple_of(i * col, col), col), :], held_ref.at[i], sems.at[i])

    for i in range(steps):
        fetch(i).start()
    rows = batch_ref[...]
    wide = rows.astype(f32)
    rows_ref[...] = rows * (-2)
    sq_ref[...] = jnp.broadcast_to(jnp.sum(wide * wide, axis=1, keepdims=True), (batch, LANES))
    acc_ref[...] = jnp.zeros_like(acc_ref)

    def step(i, carry):
        fetch(i).wait()
        cols = pl.ds(pl.multiple_of(i * col, col), col)
        cen = held_ref[i]
        w = w_ref[:, cols]
        cen_sq = cen_sq_ref[:, cols]
        for j in range(batch // row):
            at = slice(j * row, (j + 1) * row)
            cross = lax.dot_general(rows_ref[at, :], cen, NT, preferred_element_type=f32)
            row_sq = jnp.concatenate([sq_ref[at, :]] * (col // LANES), axis=1)
            kern = laplacian((cross + row_sq) + cen_sq)
            kern_ref[at, cols] = kern
            acc_ref[:, at] += lax.dot_general(w, kern, NT, preferred_element_type=f32)
        return carry

    lax.fori_loop(0, steps, step, 0)
    blocks = batch // LANES
    if first:
        for r in range(blocks):
            outs_ref[1][:, r, :] = acc_ref[:, r * LANES : (r + 1) * LANES]
        return
    before_ref, keep_ref, give_ref = refs[0], outs_ref[1], outs_ref[2]
    core = core_ref[0]
    outs = keep_ref.shape[0]
    for ref, half in ((keep_ref, core), (give_ref, 1 - core)):
        at = pl.ds(pl.multiple_of(half * outs, outs), outs)
        ref[:, pl.ds(pl.multiple_of(core * blocks, blocks), blocks), :] = before_ref[at, :, :]
        for r in range(blocks):
            ref[:, pl.ds((1 - core) * blocks + r, 1), :] = acc_ref[at, r * LANES : (r + 1) * LANES][:, None, :]


def kernel_values(core, w_half, centers, batch, cen_sq, after, before=None):
    half, count, outs = batch.shape[0], centers.shape[0], w_half.shape[0]
    col, blocks = 2048, half // LANES
    first = before is None
    terms = [(outs, blocks, LANES)] if first else [(outs // 2, 2 * blocks, LANES)] * 2
    extra = [] if first else [before]
    return pl.pallas_call(
        functools.partial(values_kernel, first=first),
        in_specs=[SMEM] + [VMEM] * 3 + [HBM] + [VMEM] * len(extra) + [ANY] * len(after),
        out_specs=[VMEM] * (1 + len(terms)),
        out_shape=[pltpu.VMEM((half, count), bf16)] + [jax.ShapeDtypeStruct(t, f32) for t in terms],
        scratch_shapes=[
            pltpu.VMEM((half, D), bf16),
            pltpu.VMEM((half, LANES), f32),
            pltpu.VMEM((outs, half), f32),
            pltpu.VMEM((count // col, col, D), bf16),
            pltpu.SemaphoreType.DMA((count // col,)),
        ],
        compiler_params=pltpu.CompilerParams(vmem_limit_bytes=12 * MIB),
        cost_estimate=pl.CostEstimate(
            flops=8 * half * count * D, bytes_accessed=2 * half * count, transcendentals=2 * half * count
        ),
        name="kernel_values",
    )(core, w_half, batch, cen_sq, centers, *extra, *after)


def nystrom_kernel(core_ref, cen_ref, sq_ref, hi_ref, lo_ref, own_ref, other_ref, keep_ref, give_ref, acc_ref):
    cen = cen_ref[...]
    core = core_ref[0]
    half = own_ref.shape[0]
    for ref, place in ((own_ref, core), (other_ref, 1 - core)):
        rows = ref[...]
        wide = rows.astype(f32)
        cross = lax.dot_general(rows * (-2), cen, NT, preferred_element_type=f32)
        kern = laplacian((cross + jnp.sum(wide * wide, axis=1, keepdims=True)) + sq_ref[...])
        part = lax.dot_general(hi_ref[...], kern, NT, preferred_element_type=f32)
        part += lax.dot_general(lo_ref[...], kern, NT, preferred_element_type=f32)
        for r in range(half // LANES):
            at = pl.ds(place * (half // LANES) + r, 1)
            acc_ref[:, at, :] = part[:, None, r * LANES : (r + 1) * LANES]
    vectors = keep_ref.shape[0]
    keep_ref[...] = acc_ref[pl.ds(core * vectors, vectors), :, :].astype(bf16)
    give_ref[...] = acc_ref[pl.ds((1 - core) * vectors, vectors), :, :].astype(bf16)


def nystrom_terms(core, nys, own, other):
    vectors, blocks = nys[2].shape[0], 2 * own.shape[0] // LANES
    return pl.pallas_call(
        nystrom_kernel,
        in_specs=[SMEM] + [VMEM] * 6,
        out_specs=[VMEM, VMEM],
        out_shape=[jax.ShapeDtypeStruct((vectors // 2, blocks, LANES), bf16)] * 2,
        scratch_shapes=[pltpu.VMEM((vectors, blocks, LANES), f32)],
        compiler_params=pltpu.CompilerParams(vmem_limit_bytes=12 * MIB),
        cost_estimate=pl.CostEstimate(flops=2 * 10**9, bytes_accessed=2**20, transcendentals=2**18),
        name="nystrom_terms",
    )(core, *nys, own, other)


def split3(x):
    hi = x.astype(bf16).astype(f32)
    mid = (x - hi).astype(bf16).astype(f32)
    return hi, mid, (x - hi) - mid


def pack_kernel(moment_ref, moment_in_ref, pred_ref, pred_in_ref, out_ref, acc_ref):
    vectors, blocks, _ = moment_ref.shape
    acc_ref[:, :blocks, :] = moment_ref[...].astype(f32) + moment_in_ref[...].astype(f32)
    acc_ref[:, blocks:, :] = jnp.zeros((vectors, PACK - blocks, LANES), f32)
    pred = pred_ref[...] + pred_in_ref[...]
    parts = split3(pred)
    for j in range(vectors):
        o, r = j // (blocks // 2), j % (blocks // 2) * 2
        for n, part in enumerate(parts):
            acc_ref[j, blocks + 2 * n : blocks + 2 * n + 2, :] = part[o, r : r + 2, :]
    out_ref[...] = acc_ref[...].astype(bf16)


def pack(moment, moment_in, pred, pred_in):
    shape = (moment.shape[0], PACK, LANES)
    return pl.pallas_call(
        pack_kernel,
        in_specs=[VMEM] * 4,
        out_specs=VMEM,
        out_shape=jax.ShapeDtypeStruct(shape, bf16),
        scratch_shapes=[pltpu.VMEM(shape, f32)],
        compiler_params=pltpu.CompilerParams(vmem_limit_bytes=8 * MIB),
        name="pack",
    )(moment, moment_in, pred, pred_in)


def sum_kernel(part_ref, out_ref, acc_ref):
    blocks = 16
    acc_ref[...] = jnp.sum(part_ref[...].astype(f32), axis=0)
    pred = (acc_ref[blocks : blocks + 2, :] + acc_ref[blocks + 2 : blocks + 4, :]) + acc_ref[blocks + 4 : blocks + 6, :]
    for n, part in enumerate(split3(pred)):
        acc_ref[blocks + 2 * n : blocks + 2 * n + 2, :] = part
    out_ref[...] = jnp.broadcast_to(acc_ref[...].astype(bf16)[None], out_ref.shape)


def sum_chips(parts):
    return pl.pallas_call(
        sum_kernel,
        in_specs=[VMEM],
        out_specs=VMEM,
        out_shape=jax.ShapeDtypeStruct(parts.shape, bf16),
        scratch_shapes=[pltpu.VMEM(parts.shape[1:], f32)],
        compiler_params=pltpu.CompilerParams(vmem_limit_bytes=8 * MIB),
        name="sum_chips",
    )(parts)


def finish_kernel(
    core_ref, idx_ref, mine_ref, got_ref, tgt_ref, damp_ref, eig_ref, w_ref, own_ref, other_ref, out_ref, out_pred_ref, resid_ref, sum_ref
):
    half, count = own_ref.shape
    core = core_ref[0]
    chips = mine_ref.shape[0]
    blocks = tgt_ref.shape[1] // LANES
    outs = tgt_ref.shape[0] // 2
    sum_ref[pl.ds(core * chips, chips), :, :] = mine_ref[...].astype(f32)
    sum_ref[pl.ds((1 - core) * chips, chips), :, :] = got_ref[...].astype(f32)
    coeff = 0.0
    for r in range(blocks):
        at = slice(r * LANES, (r + 1) * LANES)
        halves = []
        for h in range(2):
            chip = pl.ds(h * chips + r // 2, outs, stride=chips // outs)
            line = blocks + r % 2
            halves.append((sum_ref[chip, line, :] + sum_ref[chip, line + 2, :]) + sum_ref[chip, line + 4, :])
        pred = jnp.concatenate(halves, axis=0)
        out_pred_ref[:, at] = pred
        resid = (pred - tgt_ref[:, at]).astype(bf16)
        resid_ref[:, at] = resid
        coeff += lax.dot_general(resid, sum_ref[:, r, :].astype(bf16), NT, preferred_element_type=f32)
    delta = 2.0 * lax.dot_general(
        coeff * damp_ref[...], eig_ref[...], NT, precision=lax.Precision.HIGHEST, preferred_element_type=f32
    )
    own = resid_ref[:, pl.ds(pl.multiple_of(core * half, half), half)]
    other = resid_ref[:, pl.ds(pl.multiple_of((1 - core) * half, half), half)]
    lane = lax.broadcasted_iota(jnp.int32, (w_ref.shape[0], LANES), 1)
    col = 1024
    for i in range(count // col):
        at = slice(i * col, (i + 1) * col)
        grad = jnp.dot(own, own_ref[:, at], preferred_element_type=f32)
        grad += jnp.dot(other, other_ref[:, at], preferred_element_type=f32)
        shifts = []
        for k in range(i * (col // LANES), (i + 1) * (col // LANES)):
            shifts.append(jnp.where(lane == idx_ref[k] - k * LANES, delta[:, k : k + 1], 0.0))
        out_ref[:, at] = (w_ref[:, at] - 2.0 * grad) + jnp.concatenate(shifts, axis=1)


def finish(core, nys_index, mine, got, targets, damping, eigvecs, weights, own, other):
    own = pltpu.with_memory_space_constraint(own, pltpu.VMEM)
    other = pltpu.with_memory_space_constraint(other, pltpu.VMEM)
    return pl.pallas_call(
        finish_kernel,
        in_specs=[SMEM] * 2 + [VMEM] * 8,
        out_specs=[VMEM, VMEM],
        out_shape=[jax.ShapeDtypeStruct(weights.shape, f32), jax.ShapeDtypeStruct(targets.shape, f32)],
        scratch_shapes=[
            pltpu.VMEM(targets.shape, bf16),
            pltpu.VMEM((2 * mine.shape[0],) + mine.shape[1:], f32),
        ],
        compiler_params=pltpu.CompilerParams(vmem_limit_bytes=12 * MIB),
        name="finish",
    )(core, nys_index, mine, got, targets, damping[None, :], eigvecs, weights, own, other)


def swap(x, axis):
    return lax.ppermute(x, axis, [(0, 1), (1, 0)])


def exchange(x, axes):
    return lax.all_to_all(x, axes, split_axis=0, concat_axis=0, tiled=True)


def spread(x, axes):
    return exchange(jnp.broadcast_to(x[None], (lax.axis_size(axes),) + x.shape), axes)


def body(pool, batch_index, targets, centers, weights, nys_index, eigvecs, damping):
    total = targets.shape[1]
    core = lax.axis_index("core").astype(jnp.int32)
    groups = lax.axis_size(CENTERS)
    share = total // (2 * groups)
    place = jnp.stack([lax.axis_index(LOADER), core, lax.axis_index(CENTERS) * share]).astype(jnp.int32)
    keep, give = pick_rows(place, batch_index, pool, share)
    rows = keep + swap(give, "core")
    rows = rows + swap(rows, "zh")
    own = spread(rows, CENTERS).reshape(groups * share, D)
    other = swap(own, "core")

    wide = centers.astype(f32)
    cen_sq = jnp.sum(wide * wide, axis=1)[None, :]
    w_half = weights.astype(bf16)
    core = core[None]

    nys_cen = centers[nys_index]
    nys_wide = nys_cen.astype(f32)
    eig_t = eigvecs.T
    eig_hi = eig_t.astype(bf16)
    eig_lo = (eig_t - eig_hi.astype(f32)).astype(bf16)
    nys = (nys_cen, jnp.sum(nys_wide * nys_wide, axis=1)[None, :], eig_hi, eig_lo)

    kern_own, pred = kernel_values(core, w_half, centers, own, cen_sq, nys)
    moment, give = nystrom_terms(core, nys, own, other)
    kern_other, pred, pred_give = kernel_values(core, w_half, centers, other, cen_sq, (give,), pred)
    packed = pack(moment, swap(give, "core"), pred, swap(pred_give, "core"))
    mine = exchange(sum_chips(exchange(packed, CHIPS)), CHIPS)
    return tuple(
        finish(core, nys_index, mine, swap(mine, "core"), targets, damping, eigvecs, weights, kern_own, kern_other)
    )


def solution(mesh):
    fine = Mesh(mesh.devices.reshape(2, 2, 4, 2, 4), ALL)
    return jax.shard_map(
        body,
        mesh=fine,
        in_specs=(
            P(LOADER, None),
            P(),
            P(),
            P(ALL, None),
            P(None, ALL),
            P(ALL),
            P(ALL, None),
            P(),
        ),
        out_specs=(P(None, ALL), P()),
        check_vma=False,
    )
```

```python
import functools
import math

import jax
import jax.numpy as jnp
from jax import lax
from jax.experimental import pallas as pl
from jax.experimental.pallas import tpu as pltpu
from jax.sharding import Mesh
from jax.sharding import PartitionSpec as P

f32, bf16 = jnp.float32, jnp.bfloat16
MIB = 2**20
LOADER = ("zh", "core")
CENTERS = ("y", "zl", "x")
ALL = LOADER + CENTERS
CHIPS = ("zh",) + CENTERS
PACK = 24
D = 256
LANES = 128
RATE = -4.0 / math.sqrt(D) * math.log2(math.e)
VMEM = pl.BlockSpec(memory_space=pltpu.VMEM)
SMEM = pl.BlockSpec(memory_space=pltpu.SMEM)
ANY = pl.BlockSpec(memory_space=pl.ANY)
HBM = pl.BlockSpec(memory_space=pltpu.HBM)
NT = (((1,), (1,)), ((), ()))


def in_hbm(x):
    return pltpu.with_memory_space_constraint(x, pltpu.HBM)


def in_vmem(x):
    return pltpu.with_memory_space_constraint(x, pltpu.VMEM)


def laplacian(dist_sq):
    safe = jnp.maximum(dist_sq, 1e-30)
    return jnp.exp2(safe * lax.rsqrt(safe) * RATE).astype(bf16)


def pick_kernel(place_ref, wanted_ref, pool_ref, keep_ref, give_ref, held_ref, index_ref, sems, index_sem):
    share = keep_ref.shape[0]
    group = held_ref.shape[1]
    total = index_ref.shape[0]
    mine, core, first = place_ref[0], place_ref[1], place_ref[2]
    rows = pool_ref.shape[0]
    listed = pltpu.make_async_copy(wanted_ref, index_ref, index_sem)
    listed.start()
    listed.wait()

    def local(n):
        half = core if n < share else 1 - core
        return index_ref[half * (total // 2) + first + n % share] - mine * rows

    def copy(n):
        at = jnp.clip(local(n), 0, rows - 1) // group * group
        return pltpu.make_async_copy(pool_ref.at[pl.ds(pl.multiple_of(at, group), group), :], held_ref.at[n], sems.at[n])

    for n in range(2 * share):
        copy(n).start()
    line = lax.broadcasted_iota(jnp.int32, (group, D), 0)
    for ref, base in ((keep_ref, 0), (give_ref, share)):
        picked = []
        for n in range(base, base + share):
            copy(n).wait()
            here = local(n)
            owned = jnp.logical_and(here >= 0, here < rows)
            spot = jnp.where(owned, lax.rem(jnp.clip(here, 0, rows - 1), group), -1)
            block = held_ref[n].astype(f32)
            picked.append(jnp.sum(jnp.where(line == spot, block, 0.0), axis=0, keepdims=True))
        ref[...] = jnp.concatenate(picked, axis=0).astype(bf16)


def pick_rows(place, batch_index, pool, share):
    group = 16
    return pl.pallas_call(
        pick_kernel,
        in_specs=[SMEM, HBM, HBM],
        out_specs=[VMEM, VMEM],
        out_shape=[jax.ShapeDtypeStruct((share, D), bf16)] * 2,
        scratch_shapes=[
            pltpu.VMEM((2 * share, group, D), bf16),
            pltpu.SMEM(batch_index.shape, jnp.int32),
            pltpu.SemaphoreType.DMA((2 * share,)),
            pltpu.SemaphoreType.DMA,
        ],
        compiler_params=pltpu.CompilerParams(vmem_limit_bytes=4 * MIB),
        name="pick_rows",
    )(place, in_hbm(batch_index), in_hbm(pool))


def repeat_kernel(keep_ref, got_ref, out_ref):
    out_ref[...] = jnp.broadcast_to((keep_ref[...] + got_ref[...])[None], out_ref.shape)


def repeat_sum(keep, got, times):
    return pl.pallas_call(
        repeat_kernel,
        in_specs=[VMEM, VMEM],
        out_specs=VMEM,
        out_shape=jax.ShapeDtypeStruct((times,) + keep.shape, bf16),
        compiler_params=pltpu.CompilerParams(vmem_limit_bytes=4 * MIB),
        name="repeat_sum",
    )(keep, got)


def values_kernel(w_ref, batch_ref, cen_sq_ref, cen_ref, *refs):
    kern_ref, pred_ref, rows_ref, sq_ref, acc_ref, held_ref, sems = refs[-7:]
    batch, count = kern_ref.shape
    col, row, sub = held_ref.shape[1], 512, 256
    steps = count // col

    def fetch(i):
        return pltpu.make_async_copy(cen_ref.at[pl.ds(pl.multiple_of(i * col, col), col), :], held_ref.at[i], sems.at[i])

    for i in range(steps):
        fetch(i).start()
    rows = batch_ref[0] + batch_ref[1]
    wide = rows.astype(f32)
    rows_ref[...] = rows * (-2)
    sq_ref[...] = jnp.broadcast_to(jnp.sum(wide * wide, axis=1, keepdims=True), (batch, LANES))
    acc_ref[...] = jnp.zeros_like(acc_ref)

    def step(i, carry):
        fetch(i).wait()
        for j in range(batch // row):
            at = slice(j * row, (j + 1) * row)
            row_sq = jnp.concatenate([sq_ref[at, :]] * (sub // LANES), axis=1)
            acc = acc_ref[:, at]
            for n in range(col // sub):
                cols = pl.ds(pl.multiple_of(i * col + n * sub, sub), sub)
                cen = held_ref[i, n * sub : (n + 1) * sub, :]
                cross = lax.dot_general(rows_ref[at, :], cen, NT, preferred_element_type=f32)
                kern = laplacian((cross + row_sq) + cen_sq_ref[:, cols])
                kern_ref[at, cols] = kern
                acc += lax.dot_general(w_ref[:, cols], kern, NT, preferred_element_type=f32)
            acc_ref[:, at] = acc
        return carry

    lax.fori_loop(0, steps, step, 0)
    for r in range(batch // LANES):
        pred_ref[:, r, :] = acc_ref[:, r * LANES : (r + 1) * LANES]


def kernel_values(w_half, centers, batch, cen_sq, after):
    half, count, outs = batch.shape[1], centers.shape[0], w_half.shape[0]
    col = 2048
    return pl.pallas_call(
        values_kernel,
        in_specs=[VMEM] * 3 + [HBM] + [ANY] * len(after),
        out_specs=[VMEM, VMEM],
        out_shape=[pltpu.VMEM((half, count), bf16), jax.ShapeDtypeStruct((outs, half // LANES, LANES), f32)],
        scratch_shapes=[
            pltpu.VMEM((half, D), bf16),
            pltpu.VMEM((half, LANES), f32),
            pltpu.VMEM((outs, half), f32),
            pltpu.VMEM((count // col, col, D), bf16),
            pltpu.SemaphoreType.DMA((count // col,)),
        ],
        compiler_params=pltpu.CompilerParams(vmem_limit_bytes=12 * MIB),
        cost_estimate=pl.CostEstimate(
            flops=8 * half * count * D, bytes_accessed=2 * half * count, transcendentals=2 * half * count
        ),
        name="kernel_values",
    )(w_half, batch, cen_sq, in_hbm(centers), *after)


def nystrom_kernel(core_ref, cen_ref, sq_ref, hi_ref, lo_ref, own_ref, other_ref, keep_ref, give_ref, acc_ref):
    cen = cen_ref[...]
    core = core_ref[0]
    half = own_ref.shape[1]
    for ref, place in ((own_ref, core), (other_ref, 1 - core)):
        rows = ref[0] + ref[1]
        wide = rows.astype(f32)
        cross = lax.dot_general(rows * (-2), cen, NT, preferred_element_type=f32)
        kern = laplacian((cross + jnp.sum(wide * wide, axis=1, keepdims=True)) + sq_ref[...])
        part = lax.dot_general(hi_ref[...], kern, NT, preferred_element_type=f32)
        part += lax.dot_general(lo_ref[...], kern, NT, preferred_element_type=f32)
        for r in range(half // LANES):
            at = pl.ds(place * (half // LANES) + r, 1)
            acc_ref[:, at, :] = part[:, None, r * LANES : (r + 1) * LANES]
    vectors = keep_ref.shape[0]
    keep_ref[...] = acc_ref[pl.ds(core * vectors, vectors), :, :].astype(bf16)
    give_ref[...] = acc_ref[pl.ds((1 - core) * vectors, vectors), :, :].astype(bf16)


def nystrom_terms(core, nys, own, other):
    vectors, blocks = nys[2].shape[0], 2 * own.shape[1] // LANES
    return pl.pallas_call(
        nystrom_kernel,
        in_specs=[SMEM] + [VMEM] * 6,
        out_specs=[VMEM, VMEM],
        out_shape=[jax.ShapeDtypeStruct((vectors // 2, blocks, LANES), bf16)] * 2,
        scratch_shapes=[pltpu.VMEM((vectors, blocks, LANES), f32)],
        compiler_params=pltpu.CompilerParams(vmem_limit_bytes=12 * MIB),
        cost_estimate=pl.CostEstimate(flops=2 * 10**9, bytes_accessed=2**20, transcendentals=2**18),
        name="nystrom_terms",
    )(core, *nys, own, other)


def split3(x):
    hi = x.astype(bf16).astype(f32)
    mid = (x - hi).astype(bf16).astype(f32)
    return hi, mid, (x - hi) - mid


def pack_kernel(moment_ref, moment_in_ref, pred_ref, pred_in_ref, out_ref, acc_ref):
    vectors, blocks, _ = moment_ref.shape
    acc_ref[:, :blocks, :] = moment_ref[...].astype(f32) + moment_in_ref[...].astype(f32)
    acc_ref[:, blocks:, :] = jnp.zeros((vectors, PACK - blocks, LANES), f32)
    pred = pred_ref[...] + pred_in_ref[...]
    parts = split3(pred)
    per = pred.shape[1] // 2
    for j in range(vectors):
        o, r = j // per, j % per * 2
        for n, part in enumerate(parts):
            acc_ref[j, blocks + 2 * n : blocks + 2 * n + 2, :] = part[o, r : r + 2, :]
    out_ref[...] = acc_ref[...].astype(bf16)


def pack(moment, moment_in, pred, pred_in):
    shape = (moment.shape[0], PACK, LANES)
    return pl.pallas_call(
        pack_kernel,
        in_specs=[VMEM] * 4,
        out_specs=VMEM,
        out_shape=jax.ShapeDtypeStruct(shape, bf16),
        scratch_shapes=[pltpu.VMEM(shape, f32)],
        compiler_params=pltpu.CompilerParams(vmem_limit_bytes=8 * MIB),
        name="pack",
    )(moment, moment_in, pred, pred_in)


def sum_kernel(part_ref, out_ref, acc_ref):
    blocks = 16
    acc_ref[...] = jnp.sum(part_ref[...].astype(f32), axis=0)
    pred = (acc_ref[blocks : blocks + 2, :] + acc_ref[blocks + 2 : blocks + 4, :]) + acc_ref[blocks + 4 : blocks + 6, :]
    for n, part in enumerate(split3(pred)):
        acc_ref[blocks + 2 * n : blocks + 2 * n + 2, :] = part
    out_ref[...] = jnp.broadcast_to(acc_ref[...].astype(bf16)[None], out_ref.shape)


def sum_chips(parts):
    return pl.pallas_call(
        sum_kernel,
        in_specs=[VMEM],
        out_specs=VMEM,
        out_shape=jax.ShapeDtypeStruct(parts.shape, bf16),
        scratch_shapes=[pltpu.VMEM(parts.shape[1:], f32)],
        compiler_params=pltpu.CompilerParams(vmem_limit_bytes=8 * MIB),
        name="sum_chips",
    )(parts)


def read_pred(sum_ref, r, outs, blocks):
    chip = pl.ds(r // 2, outs, stride=sum_ref.shape[0] // outs)
    line = blocks + r % 2
    return (sum_ref[chip, line, :] + sum_ref[chip, line + 2, :]) + sum_ref[chip, line + 4, :]


def grad_kernel(core_ref, mine_ref, tgt_ref, kern_ref, pred_ref, resid_ref, grad_ref, sum_ref):
    half, count = kern_ref.shape
    blocks = half // LANES
    sum_ref[...] = mine_ref[...].astype(f32)
    for r in range(blocks):
        at = slice(r * LANES, (r + 1) * LANES)
        pred = read_pred(sum_ref, r, tgt_ref.shape[0], 2 * blocks)
        pred_ref[:, at] = pred
        tgt = tgt_ref[:, pl.ds(pl.multiple_of(core_ref[0] * half + r * LANES, LANES), LANES)]
        resid_ref[:, at] = (pred - tgt).astype(bf16)
    resid = resid_ref[...]
    col = 1024
    for i in range(count // col):
        at = slice(i * col, (i + 1) * col)
        grad_ref[:, at] = jnp.dot(resid, kern_ref[:, at], preferred_element_type=f32)


def own_grad(core, mine, targets, kern):
    half, count = kern.shape
    outs = targets.shape[0]
    return pl.pallas_call(
        grad_kernel,
        in_specs=[SMEM] + [VMEM] * 3,
        out_specs=[VMEM] * 3,
        out_shape=[
            jax.ShapeDtypeStruct((outs, half), f32),
            jax.ShapeDtypeStruct((outs, half), bf16),
            jax.ShapeDtypeStruct((outs, count), f32),
        ],
        scratch_shapes=[pltpu.VMEM(mine.shape, f32)],
        compiler_params=pltpu.CompilerParams(vmem_limit_bytes=8 * MIB),
        cost_estimate=pl.CostEstimate(flops=512 * half * count, bytes_accessed=2 * half * count, transcendentals=0),
        name="own_grad",
    )(core, mine, targets, in_vmem(kern))


def finish_kernel(
    core_ref, idx_ref, mine_ref, got_ref, pred_ref, resid_ref, grad_ref, tgt_ref, damp_ref, eig_ref, w_ref, kern_ref,
    out_ref, out_pred_ref, sum_ref, moment_ref,
):
    half, count = kern_ref.shape
    core = core_ref[0]
    chips = mine_ref.shape[0]
    blocks = half // LANES
    outs = tgt_ref.shape[0]
    sum_ref[...] = got_ref[...].astype(f32)
    out_pred_ref[:, pl.ds(pl.multiple_of(core * half, half), half)] = pred_ref[...]
    resids = []
    for r in range(blocks):
        at = pl.ds(pl.multiple_of((1 - core) * half + r * LANES, LANES), LANES)
        pred = read_pred(sum_ref, r, outs, 2 * blocks)
        out_pred_ref[:, at] = pred
        resids.append((pred - tgt_ref[:, at]).astype(bf16))
    other = jnp.concatenate(resids, axis=1)
    own = resid_ref[...]
    moment_ref[pl.ds(core * chips, chips), :, :] = mine_ref[:, : 2 * blocks, :].astype(f32)
    moment_ref[pl.ds((1 - core) * chips, chips), :, :] = sum_ref[:, : 2 * blocks, :]
    coeff = 0.0
    for r in range(blocks):
        at = slice(r * LANES, (r + 1) * LANES)
        for resid, place in ((own, core), (other, 1 - core)):
            line = pl.ds(place * blocks + r, 1)
            moment = moment_ref[:, line, :].reshape(2 * chips, LANES).astype(bf16)
            coeff += lax.dot_general(resid[:, at], moment, NT, preferred_element_type=f32)
    delta = 2.0 * lax.dot_general(
        coeff * damp_ref[...], eig_ref[...], NT, precision=lax.Precision.HIGHEST, preferred_element_type=f32
    )
    lane = lax.broadcasted_iota(jnp.int32, (outs, LANES), 1)
    col = 1024
    for i in range(count // col):
        at = slice(i * col, (i + 1) * col)
        grad = grad_ref[:, at] + jnp.dot(other, kern_ref[:, at], preferred_element_type=f32)
        shifts = []
        for k in range(i * (col // LANES), (i + 1) * (col // LANES)):
            shifts.append(jnp.where(lane == idx_ref[k] - k * LANES, delta[:, k : k + 1], 0.0))
        out_ref[:, at] = (w_ref[:, at] - 2.0 * grad) + jnp.concatenate(shifts, axis=1)


def finish(core, nys_index, mine, got, pred, resid, grad, targets, damping, eigvecs, weights, kern):
    chips, _, lanes = mine.shape
    return pl.pallas_call(
        finish_kernel,
        in_specs=[SMEM] * 2 + [VMEM] * 10,
        out_specs=[VMEM, VMEM],
        out_shape=[jax.ShapeDtypeStruct(weights.shape, f32), jax.ShapeDtypeStruct(targets.shape, f32)],
        scratch_shapes=[
            pltpu.VMEM(mine.shape, f32),
            pltpu.VMEM((2 * chips, 2 * kern.shape[0] // LANES, lanes), f32),
        ],
        compiler_params=pltpu.CompilerParams(vmem_limit_bytes=12 * MIB),
        name="finish",
    )(core, nys_index, mine, got, pred, resid, grad, targets, damping[None, :], eigvecs, weights, in_vmem(kern))


def swap(x, axis):
    return lax.ppermute(x, axis, [(0, 1), (1, 0)])


def exchange(x, axes):
    return lax.all_to_all(x, axes, split_axis=0, concat_axis=0, tiled=True)


def body(pool, batch_index, targets, centers, weights, nys_index, eigvecs, damping):
    total = targets.shape[1]
    core = lax.axis_index("core").astype(jnp.int32)
    groups = lax.axis_size(CENTERS)
    share = total // (2 * groups)
    place = jnp.stack([lax.axis_index(LOADER), core, lax.axis_index(CENTERS) * share]).astype(jnp.int32)
    keep, give = pick_rows(place, batch_index, pool, share)
    rows = exchange(repeat_sum(keep, swap(give, "core"), lax.axis_size(CHIPS)), CHIPS)
    wide = centers.astype(f32)
    cen_sq = jnp.sum(wide * wide, axis=1)[None, :]
    w_half = weights.astype(bf16)
    core = core[None]

    nys_cen = centers[nys_index]
    nys_wide = nys_cen.astype(f32)
    eig_t = eigvecs.T
    eig_hi = eig_t.astype(bf16)
    eig_lo = (eig_t - eig_hi.astype(f32)).astype(bf16)
    nys = (nys_cen, jnp.sum(nys_wide * nys_wide, axis=1)[None, :], eig_hi, eig_lo)

    rows, cen_sq, w_half, nys = lax.optimization_barrier((rows, cen_sq, w_half, nys))
    own = rows.reshape(2, groups * share, D)
    other = swap(own, "core")

    kern_own, pred = kernel_values(w_half, centers, own, cen_sq, nys)
    moment, give = nystrom_terms(core, nys, own, other)
    kern_other, pred_give = kernel_values(w_half, centers, other, cen_sq, (give, pred))
    packed = pack(moment, swap(give, "core"), pred, swap(pred_give, "core"))
    mine = exchange(sum_chips(exchange(packed, CHIPS)), CHIPS)
    got = swap(mine, "core")
    pred, resid, grad = own_grad(core, mine, targets, kern_own)
    return tuple(
        finish(core, nys_index, mine, got, pred, resid, grad, targets, damping, eigvecs, weights, kern_other)
    )


def solution(mesh):
    fine = Mesh(mesh.devices.reshape(2, 2, 4, 2, 4), ALL)
    return jax.shard_map(
        body,
        mesh=fine,
        in_specs=(
            P(LOADER, None),
            P(),
            P(),
            P(ALL, None),
            P(None, ALL),
            P(ALL),
            P(ALL, None),
            P(),
        ),
        out_specs=(P(None, ALL), P()),
        check_vma=False,
    )
```

```python
import functools
import math

import jax
import jax.numpy as jnp
from jax import lax
from jax.experimental import pallas as pl
from jax.experimental.pallas import tpu as pltpu
from jax.sharding import Mesh
from jax.sharding import PartitionSpec as P

f32, bf16 = jnp.float32, jnp.bfloat16
MIB = 2**20
LOADER = ("zh", "core")
CENTERS = ("y", "zl", "x")
ALL = LOADER + CENTERS
CHIPS = ("zh",) + CENTERS
PACK = 24
D = 256
LANES = 128
RATE = -4.0 / math.sqrt(D) * math.log2(math.e)
VMEM = pl.BlockSpec(memory_space=pltpu.VMEM)
SMEM = pl.BlockSpec(memory_space=pltpu.SMEM)
ANY = pl.BlockSpec(memory_space=pl.ANY)
HBM = pl.BlockSpec(memory_space=pltpu.HBM)
NT = (((1,), (1,)), ((), ()))


def in_hbm(x):
    return pltpu.with_memory_space_constraint(x, pltpu.HBM)


def in_vmem(x):
    return pltpu.with_memory_space_constraint(x, pltpu.VMEM)


def laplacian(dist_sq):
    safe = jnp.maximum(dist_sq, 1e-30)
    return jnp.exp2(safe * lax.rsqrt(safe) * RATE).astype(bf16)


def pick_kernel(place_ref, wanted_ref, pool_ref, keep_ref, give_ref, held_ref, row_ref, index_ref, sems, index_sem):
    share = keep_ref.shape[0]
    group = held_ref.shape[1]
    half = index_ref.shape[0] // 2
    mine, core, first = place_ref[0], place_ref[1], place_ref[2]
    rows = pool_ref.shape[0]
    listed = pltpu.make_async_copy(wanted_ref, index_ref, index_sem)
    listed.start()
    listed.wait()

    def local(n):
        of = jnp.where(n < share, core, 1 - core)
        return index_ref[of * half + first + jnp.where(n < share, n, n - share)] - mine * rows

    def copy(n, at):
        return pltpu.make_async_copy(pool_ref.at[pl.ds(pl.multiple_of(at, group), group), :], held_ref.at[n], sems.at[n])

    def start(n, carry):
        at = jnp.clip(local(n), 0, rows - 1)
        copy(n, at - lax.rem(at, group)).start()
        return carry

    lax.fori_loop(0, 2 * share, start, 0, unroll=4)
    line = lax.broadcasted_iota(jnp.int32, (group, D), 0)

    def select(n, carry):
        copy(n, 0).wait()
        here = local(n)
        owned = jnp.logical_and(here >= 0, here < rows)
        spot = jnp.where(owned, lax.rem(here, group), -1)
        block = held_ref[n].astype(f32)
        row_ref[pl.ds(n, 1), :] = jnp.sum(jnp.where(line == spot, block, 0.0), axis=0, keepdims=True)
        return carry

    lax.fori_loop(0, 2 * share, select, 0, unroll=4)
    keep_ref[...] = row_ref[:share, :].astype(bf16)
    give_ref[...] = row_ref[share:, :].astype(bf16)


def pick_rows(place, batch_index, pool, share):
    group = 16
    return pl.pallas_call(
        pick_kernel,
        in_specs=[SMEM, HBM, HBM],
        out_specs=[VMEM, VMEM],
        out_shape=[jax.ShapeDtypeStruct((share, D), bf16)] * 2,
        scratch_shapes=[
            pltpu.VMEM((2 * share, group, D), bf16),
            pltpu.VMEM((2 * share, D), f32),
            pltpu.SMEM(batch_index.shape, jnp.int32),
            pltpu.SemaphoreType.DMA((2 * share,)),
            pltpu.SemaphoreType.DMA,
        ],
        compiler_params=pltpu.CompilerParams(vmem_limit_bytes=4 * MIB),
        name="pick_rows",
    )(place, in_hbm(batch_index), in_hbm(pool))


def repeat_kernel(keep_ref, got_ref, out_ref):
    out_ref[...] = jnp.broadcast_to((keep_ref[...] + got_ref[...])[None], out_ref.shape)


def repeat_sum(keep, got, times):
    return pl.pallas_call(
        repeat_kernel,
        in_specs=[VMEM, VMEM],
        out_specs=VMEM,
        out_shape=jax.ShapeDtypeStruct((times,) + keep.shape, bf16),
        compiler_params=pltpu.CompilerParams(vmem_limit_bytes=4 * MIB),
        name="repeat_sum",
    )(keep, got)


def values_kernel(w_ref, batch_ref, cen_sq_ref, cen_ref, *refs):
    kern_ref, pred_ref, rows_ref, sq_ref, acc_ref, held_ref, sems = refs[-7:]
    batch, count = kern_ref.shape
    col, row, sub = held_ref.shape[1], 512, 256
    steps = count // col

    def fetch(i):
        return pltpu.make_async_copy(cen_ref.at[pl.ds(pl.multiple_of(i * col, col), col), :], held_ref.at[i], sems.at[i])

    ahead = 2
    for i in range(ahead):
        fetch(i).start()
    rows = batch_ref[...]
    wide = rows.astype(f32)
    rows_ref[...] = rows * (-2)
    sq_ref[...] = jnp.broadcast_to(jnp.sum(wide * wide, axis=1, keepdims=True), (batch, LANES))
    acc_ref[...] = jnp.zeros_like(acc_ref)

    def step(i, carry):
        @pl.when(i + ahead < steps)
        def _():
            fetch(i + ahead).start()

        fetch(i).wait()
        for j in range(batch // row):
            at = slice(j * row, (j + 1) * row)
            row_sq = jnp.concatenate([sq_ref[at, :]] * (sub // LANES), axis=1)
            acc = acc_ref[:, at]
            for n in range(col // sub):
                cols = pl.ds(pl.multiple_of(i * col + n * sub, sub), sub)
                cen = held_ref[i, n * sub : (n + 1) * sub, :]
                cross = lax.dot_general(rows_ref[at, :], cen, NT, preferred_element_type=f32)
                kern = laplacian((cross + row_sq) + cen_sq_ref[:, cols])
                kern_ref[at, cols] = kern
                acc += lax.dot_general(w_ref[:, cols], kern, NT, preferred_element_type=f32)
            acc_ref[:, at] = acc
        return carry

    lax.fori_loop(0, steps, step, 0)
    for r in range(batch // LANES):
        pred_ref[:, r, :] = acc_ref[:, r * LANES : (r + 1) * LANES]


def kernel_values(w_half, centers, batch, cen_sq, after):
    half, count, outs = batch.shape[0], centers.shape[0], w_half.shape[0]
    col = 1024
    return pl.pallas_call(
        values_kernel,
        in_specs=[VMEM] * 3 + [HBM] + [ANY] * len(after),
        out_specs=[VMEM, VMEM],
        out_shape=[pltpu.VMEM((half, count), bf16), jax.ShapeDtypeStruct((outs, half // LANES, LANES), f32)],
        scratch_shapes=[
            pltpu.VMEM((half, D), bf16),
            pltpu.VMEM((half, LANES), f32),
            pltpu.VMEM((outs, half), f32),
            pltpu.VMEM((count // col, col, D), bf16),
            pltpu.SemaphoreType.DMA((count // col,)),
        ],
        compiler_params=pltpu.CompilerParams(vmem_limit_bytes=12 * MIB),
        cost_estimate=pl.CostEstimate(
            flops=8 * half * count * D, bytes_accessed=2 * half * count, transcendentals=2 * half * count
        ),
        name="kernel_values",
    )(w_half, batch, cen_sq, in_hbm(centers), *after)


def nystrom_kernel(core_ref, cen_ref, sq_ref, hi_ref, lo_ref, own_ref, other_ref, keep_ref, give_ref, acc_ref):
    cen = cen_ref[...]
    core = core_ref[0]
    half = own_ref.shape[0]
    count, blocks = hi_ref.shape[0], keep_ref.shape[1]
    for ref, first in ((own_ref, 0), (other_ref, half // LANES)):
        rows = ref[...]
        wide = rows.astype(f32)
        cross = lax.dot_general(rows * (-2), cen, NT, preferred_element_type=f32)
        kern = laplacian((cross + jnp.sum(wide * wide, axis=1, keepdims=True)) + sq_ref[...])
        part = lax.dot_general(hi_ref[...], kern, NT, preferred_element_type=f32)
        part += lax.dot_general(lo_ref[...], kern, NT, preferred_element_type=f32)
        for r in range(half // LANES):
            acc_ref[pl.ds(first + r, count, stride=blocks), :] = part[:, r * LANES : (r + 1) * LANES]
    lines = count // 2 * blocks
    for ref, place in ((keep_ref, core), (give_ref, 1 - core)):
        part = acc_ref[pl.ds(pl.multiple_of(place * lines, lines), lines), :]
        ref[...] = part.reshape(ref.shape).astype(bf16)


def nystrom_terms(core, nys, own, other):
    vectors, blocks = nys[2].shape[0], 2 * own.shape[0] // LANES
    return pl.pallas_call(
        nystrom_kernel,
        in_specs=[SMEM] + [VMEM] * 6,
        out_specs=[VMEM, VMEM],
        out_shape=[jax.ShapeDtypeStruct((vectors // 2, blocks, LANES), bf16)] * 2,
        scratch_shapes=[pltpu.VMEM((vectors * blocks, LANES), f32)],
        compiler_params=pltpu.CompilerParams(vmem_limit_bytes=12 * MIB),
        cost_estimate=pl.CostEstimate(flops=2 * 10**9, bytes_accessed=2**20, transcendentals=2**18),
        name="nystrom_terms",
    )(core, *nys, own, other)


def split3(x):
    hi = x.astype(bf16).astype(f32)
    mid = (x - hi).astype(bf16).astype(f32)
    return hi, mid, (x - hi) - mid


def swap_halves(x, axis):
    first, last = jnp.split(x, 2, axis)
    return jnp.concatenate([last, first], axis)


def pack_kernel(moment_ref, moment_in_ref, pred_ref, pred_in_ref, out_ref, acc_ref):
    vectors, blocks, _ = moment_ref.shape
    acc_ref[:, :blocks, :] = swap_halves(moment_in_ref[...].astype(f32), 1) + moment_ref[...].astype(f32)
    acc_ref[:, blocks:, :] = jnp.zeros((vectors, PACK - blocks, LANES), f32)
    pred = pred_ref[...] + pred_in_ref[...]
    parts = split3(pred)
    per = pred.shape[1] // 2
    for j in range(vectors):
        o, r = j // per, j % per * 2
        for n, part in enumerate(parts):
            acc_ref[j, blocks + 2 * n : blocks + 2 * n + 2, :] = part[o, r : r + 2, :]
    out_ref[...] = acc_ref[...].astype(bf16)


def pack(moment, moment_in, pred, pred_in):
    shape = (moment.shape[0], PACK, LANES)
    return pl.pallas_call(
        pack_kernel,
        in_specs=[VMEM] * 4,
        out_specs=VMEM,
        out_shape=jax.ShapeDtypeStruct(shape, bf16),
        scratch_shapes=[pltpu.VMEM(shape, f32)],
        compiler_params=pltpu.CompilerParams(vmem_limit_bytes=8 * MIB),
        name="pack",
    )(moment, moment_in, pred, pred_in)


def sum_kernel(part_ref, out_ref, acc_ref):
    blocks = 16
    acc_ref[...] = jnp.sum(part_ref[...].astype(f32), axis=0)
    pred = (acc_ref[blocks : blocks + 2, :] + acc_ref[blocks + 2 : blocks + 4, :]) + acc_ref[blocks + 4 : blocks + 6, :]
    for n, part in enumerate(split3(pred)):
        acc_ref[blocks + 2 * n : blocks + 2 * n + 2, :] = part
    out_ref[...] = jnp.broadcast_to(acc_ref[...].astype(bf16)[None], out_ref.shape)


def sum_chips(parts):
    return pl.pallas_call(
        sum_kernel,
        in_specs=[VMEM],
        out_specs=VMEM,
        out_shape=jax.ShapeDtypeStruct(parts.shape, bf16),
        scratch_shapes=[pltpu.VMEM(parts.shape[1:], f32)],
        compiler_params=pltpu.CompilerParams(vmem_limit_bytes=8 * MIB),
        name="sum_chips",
    )(parts)


def read_pred(sum_ref, r, outs, blocks):
    chips = sum_ref.shape[0] // PACK

    def part(n):
        line = r // 2 * PACK + blocks + r % 2 + 2 * n
        return sum_ref[pl.ds(line, outs, stride=chips // outs * PACK), :]

    return (part(0) + part(1)) + part(2)


def grad_kernel(core_ref, mine_ref, tgt_ref, kern_ref, pred_ref, resid_ref, grad_ref, sum_ref):
    half, count = kern_ref.shape
    blocks = half // LANES
    sum_ref[...] = mine_ref[...].astype(f32).reshape(sum_ref.shape)
    for r in range(blocks):
        at = slice(r * LANES, (r + 1) * LANES)
        pred = read_pred(sum_ref, r, tgt_ref.shape[0], 2 * blocks)
        pred_ref[:, at] = pred
        tgt = tgt_ref[:, pl.ds(pl.multiple_of(core_ref[0] * half + r * LANES, LANES), LANES)]
        resid_ref[:, at] = (pred - tgt).astype(bf16)
    resid = resid_ref[...]
    col = 1024
    for i in range(count // col):
        at = slice(i * col, (i + 1) * col)
        grad_ref[:, at] = jnp.dot(resid, kern_ref[:, at], preferred_element_type=f32)


def own_grad(core, mine, targets, kern):
    half, count = kern.shape
    outs = targets.shape[0]
    return pl.pallas_call(
        grad_kernel,
        in_specs=[SMEM] + [VMEM] * 3,
        out_specs=[VMEM] * 3,
        out_shape=[
            jax.ShapeDtypeStruct((outs, half), f32),
            jax.ShapeDtypeStruct((outs, half), bf16),
            jax.ShapeDtypeStruct((outs, count), f32),
        ],
        scratch_shapes=[pltpu.VMEM((mine.shape[0] * PACK, LANES), f32)],
        compiler_params=pltpu.CompilerParams(vmem_limit_bytes=8 * MIB),
        cost_estimate=pl.CostEstimate(flops=512 * half * count, bytes_accessed=2 * half * count, transcendentals=0),
        name="own_grad",
    )(core, mine, targets, in_vmem(kern))


def finish_kernel(
    core_ref, idx_ref, mine_ref, got_ref, pred_ref, resid_ref, grad_ref, tgt_ref, damp_ref, eig_ref, w_ref, kern_ref,
    out_ref, out_pred_ref, sum_ref, moment_ref,
):
    half, count = kern_ref.shape
    core = core_ref[0]
    chips = mine_ref.shape[0]
    blocks = half // LANES
    outs = tgt_ref.shape[0]
    got = got_ref[...].astype(f32)
    sum_ref[...] = got.reshape(sum_ref.shape)
    out_pred_ref[:, pl.ds(pl.multiple_of(core * half, half), half)] = pred_ref[...]
    resids = []
    for r in range(blocks):
        at = pl.ds(pl.multiple_of((1 - core) * half + r * LANES, LANES), LANES)
        pred = read_pred(sum_ref, r, outs, 2 * blocks)
        out_pred_ref[:, at] = pred
        resids.append((pred - tgt_ref[:, at]).astype(bf16))
    other = jnp.concatenate(resids, axis=1)
    own = resid_ref[...]
    lines = chips * 2 * blocks
    for place, part in ((core, mine_ref[...].astype(f32)[:, : 2 * blocks]), (1 - core, swap_halves(got[:, : 2 * blocks], 1))):
        moment_ref[pl.ds(pl.multiple_of(place * lines, lines), lines), :] = part.reshape(lines, LANES)
    coeff = 0.0
    for n, resid in enumerate((own, other)):
        for r in range(blocks):
            moment = moment_ref[pl.ds(n * blocks + r, 2 * chips, stride=2 * blocks), :].astype(bf16)
            at = slice(r * LANES, (r + 1) * LANES)
            coeff += lax.dot_general(resid[:, at], moment, NT, preferred_element_type=f32)
    delta = 2.0 * lax.dot_general(
        coeff * damp_ref[...], eig_ref[...], NT, precision=lax.Precision.HIGHEST, preferred_element_type=f32
    )
    lane = lax.broadcasted_iota(jnp.int32, (outs, LANES), 1)
    col = 1024
    for i in range(count // col):
        at = slice(i * col, (i + 1) * col)
        grad = grad_ref[:, at] + jnp.dot(other, kern_ref[:, at], preferred_element_type=f32)
        shifts = []
        for k in range(i * (col // LANES), (i + 1) * (col // LANES)):
            shifts.append(jnp.where(lane == idx_ref[k] - k * LANES, delta[:, k : k + 1], 0.0))
        out_ref[:, at] = (w_ref[:, at] - 2.0 * grad) + jnp.concatenate(shifts, axis=1)


def finish(core, nys_index, mine, got, pred, resid, grad, targets, damping, eigvecs, weights, kern):
    chips, _, lanes = mine.shape
    return pl.pallas_call(
        finish_kernel,
        in_specs=[SMEM] * 2 + [VMEM] * 10,
        out_specs=[VMEM, VMEM],
        out_shape=[jax.ShapeDtypeStruct(weights.shape, f32), jax.ShapeDtypeStruct(targets.shape, f32)],
        scratch_shapes=[
            pltpu.VMEM((chips * PACK, lanes), f32),
            pltpu.VMEM((2 * chips * 2 * kern.shape[0] // LANES, lanes), f32),
        ],
        compiler_params=pltpu.CompilerParams(vmem_limit_bytes=12 * MIB),
        name="finish",
    )(core, nys_index, mine, got, pred, resid, grad, targets, damping[None, :], eigvecs, weights, in_vmem(kern))


def swap(x, axis):
    return lax.ppermute(x, axis, [(0, 1), (1, 0)])


def exchange(x, axes):
    return lax.all_to_all(x, axes, split_axis=0, concat_axis=0, tiled=True)


def body(pool, batch_index, targets, centers, weights, nys_index, eigvecs, damping):
    total = targets.shape[1]
    core = lax.axis_index("core").astype(jnp.int32)
    groups = lax.axis_size(CENTERS)
    share = total // (2 * groups)
    place = jnp.stack([lax.axis_index(LOADER), core, lax.axis_index(CENTERS) * share]).astype(jnp.int32)
    keep, give = pick_rows(place, batch_index, pool, share)
    rows = keep + swap(give, "core")
    rows = exchange(repeat_sum(rows, swap(rows, "zh"), groups), CENTERS)
    wide = centers.astype(f32)
    cen_sq = jnp.sum(wide * wide, axis=1)[None, :]
    w_half = weights.astype(bf16)
    core = core[None]

    nys_cen = centers[nys_index]
    nys_wide = nys_cen.astype(f32)
    eig_t = eigvecs.T
    eig_hi = eig_t.astype(bf16)
    eig_lo = (eig_t - eig_hi.astype(f32)).astype(bf16)
    nys = (nys_cen, jnp.sum(nys_wide * nys_wide, axis=1)[None, :], eig_hi, eig_lo)

    rows, cen_sq, w_half, nys = lax.optimization_barrier((rows, cen_sq, w_half, nys))
    own = rows.reshape(groups * share, D)
    other = swap(own, "core")

    kern_own, pred = kernel_values(w_half, centers, own, cen_sq, nys)
    moment, give = nystrom_terms(core, nys, own, other)
    kern_other, pred_give = kernel_values(w_half, centers, other, cen_sq, (give, pred))
    packed = pack(moment, swap(give, "core"), pred, swap(pred_give, "core"))
    mine = exchange(sum_chips(exchange(packed, CHIPS)), CHIPS)
    got = swap(mine, "core")
    pred, resid, grad = own_grad(core, mine, targets, kern_own)
    return tuple(
        finish(core, nys_index, mine, got, pred, resid, grad, targets, damping, eigvecs, weights, kern_other)
    )


def solution(mesh):
    fine = Mesh(mesh.devices.reshape(2, 2, 4, 2, 4), ALL)
    return jax.shard_map(
        body,
        mesh=fine,
        in_specs=(
            P(LOADER, None),
            P(),
            P(),
            P(ALL, None),
            P(None, ALL),
            P(ALL),
            P(ALL, None),
            P(),
        ),
        out_specs=(P(None, ALL), P()),
        check_vma=False,
    )
```

```python
import functools
import math

import jax
import jax.numpy as jnp
from jax import lax
from jax.experimental import pallas as pl
from jax.experimental.pallas import tpu as pltpu
from jax.sharding import Mesh
from jax.sharding import PartitionSpec as P

f32, bf16 = jnp.float32, jnp.bfloat16
MIB = 2**20
LOADER = ("zh", "core")
CENTERS = ("y", "zl", "x")
ALL = LOADER + CENTERS
CHIPS = ("zh",) + CENTERS
PACK = 24
D = 256
LANES = 128
RATE = -4.0 / math.sqrt(D) * math.log2(math.e)
VMEM = pl.BlockSpec(memory_space=pltpu.VMEM)
SMEM = pl.BlockSpec(memory_space=pltpu.SMEM)
ANY = pl.BlockSpec(memory_space=pl.ANY)
HBM = pl.BlockSpec(memory_space=pltpu.HBM)
NT = (((1,), (1,)), ((), ()))


def in_hbm(x):
    return pltpu.with_memory_space_constraint(x, pltpu.HBM)


def in_vmem(x):
    return pltpu.with_memory_space_constraint(x, pltpu.VMEM)


def laplacian(dist_sq):
    safe = jnp.maximum(dist_sq, 1e-30)
    return jnp.exp2(safe * lax.rsqrt(safe) * RATE).astype(bf16)


def pick_kernel(place_ref, wanted_ref, pool_ref, keep_ref, give_ref, held_ref, row_ref, index_ref, sems, index_sem):
    share = keep_ref.shape[0]
    group = held_ref.shape[1]
    half = index_ref.shape[0] // 2
    mine, core, first = place_ref[0], place_ref[1], place_ref[2]
    rows = pool_ref.shape[0]
    listed = pltpu.make_async_copy(wanted_ref, index_ref, index_sem)
    listed.start()
    listed.wait()

    def local(n):
        of = jnp.where(n < share, core, 1 - core)
        return index_ref[of * half + first + jnp.where(n < share, n, n - share)] - mine * rows

    def copy(n, at):
        return pltpu.make_async_copy(pool_ref.at[pl.ds(pl.multiple_of(at, group), group), :], held_ref.at[n], sems.at[n])

    def owned(n, act):
        here = local(n)

        @pl.when(jnp.logical_and(here >= 0, here < rows))
        def _():
            act(jnp.clip(here, 0, rows - 1))

    def start(n, carry):
        owned(n, lambda here: copy(n, here - lax.rem(here, group)).start())
        return carry

    lax.fori_loop(0, 2 * share, start, 0, unroll=4)
    row_ref[...] = jnp.zeros_like(row_ref)
    line = lax.broadcasted_iota(jnp.int32, (group, D), 0)

    def select(n, carry):
        def take(here):
            copy(n, here - lax.rem(here, group)).wait()
            block = held_ref[n].astype(f32)
            row_ref[pl.ds(n, 1), :] = jnp.sum(jnp.where(line == lax.rem(here, group), block, 0.0), axis=0, keepdims=True)

        owned(n, take)
        return carry

    lax.fori_loop(0, 2 * share, select, 0, unroll=4)
    keep_ref[...] = row_ref[:share, :].astype(bf16)
    give_ref[...] = row_ref[share:, :].astype(bf16)


def pick_rows(place, batch_index, pool, share):
    group = 16
    return pl.pallas_call(
        pick_kernel,
        in_specs=[SMEM, HBM, HBM],
        out_specs=[VMEM, VMEM],
        out_shape=[jax.ShapeDtypeStruct((share, D), bf16)] * 2,
        scratch_shapes=[
            pltpu.VMEM((2 * share, group, D), bf16),
            pltpu.VMEM((2 * share, D), f32),
            pltpu.SMEM(batch_index.shape, jnp.int32),
            pltpu.SemaphoreType.DMA((2 * share,)),
            pltpu.SemaphoreType.DMA,
        ],
        compiler_params=pltpu.CompilerParams(vmem_limit_bytes=4 * MIB),
        name="pick_rows",
    )(place, in_hbm(batch_index), in_hbm(pool))


def repeat_kernel(keep_ref, got_ref, out_ref):
    out_ref[...] = jnp.broadcast_to((keep_ref[...] + got_ref[...])[None], out_ref.shape)


def repeat_sum(keep, got, times):
    return pl.pallas_call(
        repeat_kernel,
        in_specs=[VMEM, VMEM],
        out_specs=VMEM,
        out_shape=jax.ShapeDtypeStruct((times,) + keep.shape, bf16),
        compiler_params=pltpu.CompilerParams(vmem_limit_bytes=4 * MIB),
        name="repeat_sum",
    )(keep, got)


def row_norms(rows):
    wide = rows.astype(f32)
    square = wide * wide
    hi = square.astype(bf16)
    lo = (square - hi.astype(f32)).astype(bf16)
    ones = jnp.ones((8, rows.shape[1]), bf16)
    norms = lax.dot_general(ones, hi, NT, preferred_element_type=f32)
    norms += lax.dot_general(ones, lo, NT, preferred_element_type=f32)
    return norms[:1]


def prepare_kernel(
    idx_ref, w_ref, eig_ref, cen_ref, w_half_ref, cen_sq_ref, nys_ref, nys_sq_ref, hi_ref, lo_ref, held_ref, picked_ref, sems
):
    steps, col, _ = held_ref.shape
    per = 8

    def fetch(i):
        return pltpu.make_async_copy(cen_ref.at[pl.ds(pl.multiple_of(i * col, col), col), :], held_ref.at[i], sems.at[i])

    fetch(0).start()
    fetch(1).start()
    eig_t = eig_ref[...].T
    hi = eig_t.astype(bf16)
    hi_ref[...] = hi
    lo_ref[...] = (eig_t - hi.astype(f32)).astype(bf16)
    w_half_ref[...] = w_ref[...].astype(bf16)
    row = lax.broadcasted_iota(jnp.int32, (per, col), 0)
    lane = lax.broadcasted_iota(jnp.int32, (per, col), 1)

    def step(i, carry):
        fetch(i).wait()

        @pl.when(i + 2 < steps)
        def _():
            fetch(i + 2).start()

        rows = held_ref[i]
        cen_sq_ref[:, pl.ds(pl.multiple_of(i * col, col), col)] = row_norms(rows)
        spot = jnp.full((per, col), -1, jnp.int32)
        for g in range(per):
            spot = jnp.where(row == g, idx_ref[i * per + g] - i * col, spot)
        chosen = jnp.where(lane == spot, 1.0, 0.0).astype(bf16)
        at = pl.ds(pl.multiple_of(i * per, per), per)
        picked_ref[at, :] = jnp.dot(chosen, rows, preferred_element_type=f32)
        return carry

    lax.fori_loop(0, steps, step, 0)
    nys = picked_ref[...].astype(bf16)
    nys_ref[...] = nys
    nys_sq_ref[...] = row_norms(nys)


def prepare(nys_index, weights, eigvecs, centers):
    count, points, vectors = centers.shape[0], nys_index.shape[0], eigvecs.shape[1]
    col = count // points * 8
    shapes = [
        (weights.shape, bf16),
        ((1, count), f32),
        ((points, D), bf16),
        ((1, points), f32),
        ((vectors, points), bf16),
        ((vectors, points), bf16),
    ]
    return pl.pallas_call(
        prepare_kernel,
        in_specs=[SMEM, VMEM, VMEM, HBM],
        out_specs=[VMEM] * len(shapes),
        out_shape=[jax.ShapeDtypeStruct(*shape) for shape in shapes],
        scratch_shapes=[
            pltpu.VMEM((count // col, col, D), bf16),
            pltpu.VMEM((points, D), f32),
            pltpu.SemaphoreType.DMA((count // col,)),
        ],
        compiler_params=pltpu.CompilerParams(vmem_limit_bytes=12 * MIB),
        cost_estimate=pl.CostEstimate(flops=4 * 10**9, bytes_accessed=2 * centers.size, transcendentals=0),
        name="prepare",
    )(nys_index, weights, eigvecs, in_hbm(centers))


def values_kernel(w_ref, batch_ref, cen_sq_ref, cen_ref, *refs):
    kern_ref, pred_ref, rows_ref, sq_ref, acc_ref, held_ref, sems = refs[-7:]
    batch, count = kern_ref.shape
    col, row, sub = held_ref.shape[1], 512, 256
    steps = count // col

    def fetch(i):
        return pltpu.make_async_copy(cen_ref.at[pl.ds(pl.multiple_of(i * col, col), col), :], held_ref.at[i], sems.at[i])

    fetch(0).start()
    rows = batch_ref[...]
    wide = rows.astype(f32)
    rows_ref[...] = rows * (-2)
    sq_ref[...] = jnp.broadcast_to(jnp.sum(wide * wide, axis=1, keepdims=True), (batch, LANES))
    acc_ref[...] = jnp.zeros_like(acc_ref)

    def step(i, carry):
        fetch(i).wait()

        @pl.when(i + 1 < steps)
        def _():
            fetch(i + 1).start()

        for j in range(batch // row):
            at = slice(j * row, (j + 1) * row)
            row_sq = jnp.concatenate([sq_ref[at, :]] * (sub // LANES), axis=1)
            acc = acc_ref[:, at]
            for n in range(col // sub):
                cols = pl.ds(pl.multiple_of(i * col + n * sub, sub), sub)
                cen = held_ref[i, n * sub : (n + 1) * sub, :]
                cross = lax.dot_general(rows_ref[at, :], cen, NT, preferred_element_type=f32)
                kern = laplacian((cross + row_sq) + cen_sq_ref[:, cols])
                kern_ref[at, cols] = kern
                acc += lax.dot_general(w_ref[:, cols], kern, NT, preferred_element_type=f32)
            acc_ref[:, at] = acc
        return carry

    lax.fori_loop(0, steps, step, 0)
    for r in range(batch // LANES):
        pred_ref[:, r, :] = acc_ref[:, r * LANES : (r + 1) * LANES]


def kernel_values(w_half, centers, batch, cen_sq, after):
    half, count, outs = batch.shape[0], centers.shape[0], w_half.shape[0]
    col = 2048
    return pl.pallas_call(
        values_kernel,
        in_specs=[VMEM] * 3 + [HBM] + [ANY] * len(after),
        out_specs=[VMEM, VMEM],
        out_shape=[pltpu.VMEM((half, count), bf16), jax.ShapeDtypeStruct((outs, half // LANES, LANES), f32)],
        scratch_shapes=[
            pltpu.VMEM((half, D), bf16),
            pltpu.VMEM((half, LANES), f32),
            pltpu.VMEM((outs, half), f32),
            pltpu.VMEM((count // col, col, D), bf16),
            pltpu.SemaphoreType.DMA((count // col,)),
        ],
        compiler_params=pltpu.CompilerParams(vmem_limit_bytes=12 * MIB),
        cost_estimate=pl.CostEstimate(
            flops=8 * half * count * D, bytes_accessed=2 * half * count, transcendentals=2 * half * count
        ),
        name="kernel_values",
    )(w_half, batch, cen_sq, in_hbm(centers), *after)


def nystrom_kernel(core_ref, cen_ref, sq_ref, hi_ref, lo_ref, own_ref, other_ref, keep_ref, give_ref, acc_ref):
    cen = cen_ref[...]
    core = core_ref[0]
    half = own_ref.shape[0]
    count, blocks = hi_ref.shape[0], keep_ref.shape[1]
    for ref, first in ((own_ref, 0), (other_ref, half // LANES)):
        rows = ref[...]
        wide = rows.astype(f32)
        cross = lax.dot_general(rows * (-2), cen, NT, preferred_element_type=f32)
        kern = laplacian((cross + jnp.sum(wide * wide, axis=1, keepdims=True)) + sq_ref[...])
        part = lax.dot_general(hi_ref[...], kern, NT, preferred_element_type=f32)
        part += lax.dot_general(lo_ref[...], kern, NT, preferred_element_type=f32)
        for r in range(half // LANES):
            acc_ref[pl.ds(first + r, count, stride=blocks), :] = part[:, r * LANES : (r + 1) * LANES]
    lines = count // 2 * blocks
    for ref, place in ((keep_ref, core), (give_ref, 1 - core)):
        part = acc_ref[pl.ds(pl.multiple_of(place * lines, lines), lines), :]
        ref[...] = part.reshape(ref.shape).astype(bf16)


def nystrom_terms(core, nys, own, other):
    vectors, blocks = nys[2].shape[0], 2 * own.shape[0] // LANES
    return pl.pallas_call(
        nystrom_kernel,
        in_specs=[SMEM] + [VMEM] * 6,
        out_specs=[VMEM, VMEM],
        out_shape=[jax.ShapeDtypeStruct((vectors // 2, blocks, LANES), bf16)] * 2,
        scratch_shapes=[pltpu.VMEM((vectors * blocks, LANES), f32)],
        compiler_params=pltpu.CompilerParams(vmem_limit_bytes=12 * MIB),
        cost_estimate=pl.CostEstimate(flops=2 * 10**9, bytes_accessed=2**20, transcendentals=2**18),
        name="nystrom_terms",
    )(core, *nys, own, other)


def split3(x):
    hi = x.astype(bf16).astype(f32)
    mid = (x - hi).astype(bf16).astype(f32)
    return hi, mid, (x - hi) - mid


def swap_halves(x, axis):
    first, last = jnp.split(x, 2, axis)
    return jnp.concatenate([last, first], axis)


def pack_kernel(moment_ref, moment_in_ref, pred_ref, pred_in_ref, out_ref, acc_ref):
    vectors, blocks, _ = moment_ref.shape
    acc_ref[:, :blocks, :] = swap_halves(moment_in_ref[...].astype(f32), 1) + moment_ref[...].astype(f32)
    acc_ref[:, blocks:, :] = jnp.zeros((vectors, PACK - blocks, LANES), f32)
    pred = pred_ref[...] + pred_in_ref[...]
    parts = split3(pred)
    per = pred.shape[1] // 2
    for j in range(vectors):
        o, r = j // per, j % per * 2
        for n, part in enumerate(parts):
            acc_ref[j, blocks + 2 * n : blocks + 2 * n + 2, :] = part[o, r : r + 2, :]
    out_ref[...] = acc_ref[...].astype(bf16)


def pack(moment, moment_in, pred, pred_in):
    shape = (moment.shape[0], PACK, LANES)
    return pl.pallas_call(
        pack_kernel,
        in_specs=[VMEM] * 4,
        out_specs=VMEM,
        out_shape=jax.ShapeDtypeStruct(shape, bf16),
        scratch_shapes=[pltpu.VMEM(shape, f32)],
        compiler_params=pltpu.CompilerParams(vmem_limit_bytes=8 * MIB),
        name="pack",
    )(moment, moment_in, pred, pred_in)


def sum_kernel(part_ref, out_ref, acc_ref):
    blocks = 16
    acc_ref[...] = jnp.sum(part_ref[...].astype(f32), axis=0)
    pred = (acc_ref[blocks : blocks + 2, :] + acc_ref[blocks + 2 : blocks + 4, :]) + acc_ref[blocks + 4 : blocks + 6, :]
    for n, part in enumerate(split3(pred)):
        acc_ref[blocks + 2 * n : blocks + 2 * n + 2, :] = part
    out_ref[...] = jnp.broadcast_to(acc_ref[...].astype(bf16)[None], out_ref.shape)


def sum_chips(parts):
    return pl.pallas_call(
        sum_kernel,
        in_specs=[VMEM],
        out_specs=VMEM,
        out_shape=jax.ShapeDtypeStruct(parts.shape, bf16),
        scratch_shapes=[pltpu.VMEM(parts.shape[1:], f32)],
        compiler_params=pltpu.CompilerParams(vmem_limit_bytes=8 * MIB),
        name="sum_chips",
    )(parts)


def read_pred(sum_ref, r, outs, blocks):
    chips = sum_ref.shape[0] // PACK

    def part(n):
        line = r // 2 * PACK + blocks + r % 2 + 2 * n
        return sum_ref[pl.ds(line, outs, stride=chips // outs * PACK), :]

    return (part(0) + part(1)) + part(2)


def grad_kernel(core_ref, mine_ref, tgt_ref, kern_ref, pred_ref, resid_ref, grad_ref, sum_ref):
    half, count = kern_ref.shape
    blocks = half // LANES
    sum_ref[...] = mine_ref[...].astype(f32).reshape(sum_ref.shape)
    for r in range(blocks):
        at = slice(r * LANES, (r + 1) * LANES)
        pred = read_pred(sum_ref, r, tgt_ref.shape[0], 2 * blocks)
        pred_ref[:, at] = pred
        tgt = tgt_ref[:, pl.ds(pl.multiple_of(core_ref[0] * half + r * LANES, LANES), LANES)]
        resid_ref[:, at] = (pred - tgt).astype(bf16)
    resid = resid_ref[...]
    col = 1024
    for i in range(count // col):
        at = slice(i * col, (i + 1) * col)
        grad_ref[:, at] = jnp.dot(resid, kern_ref[:, at], preferred_element_type=f32)


def own_grad(core, mine, targets, kern):
    half, count = kern.shape
    outs = targets.shape[0]
    return pl.pallas_call(
        grad_kernel,
        in_specs=[SMEM] + [VMEM] * 3,
        out_specs=[VMEM] * 3,
        out_shape=[
            jax.ShapeDtypeStruct((outs, half), f32),
            jax.ShapeDtypeStruct((outs, half), bf16),
            jax.ShapeDtypeStruct((outs, count), f32),
        ],
        scratch_shapes=[pltpu.VMEM((mine.shape[0] * PACK, LANES), f32)],
        compiler_params=pltpu.CompilerParams(vmem_limit_bytes=8 * MIB),
        cost_estimate=pl.CostEstimate(flops=512 * half * count, bytes_accessed=2 * half * count, transcendentals=0),
        name="own_grad",
    )(core, mine, targets, in_vmem(kern))


def finish_kernel(
    core_ref, idx_ref, mine_ref, got_ref, pred_ref, resid_ref, grad_ref, tgt_ref, damp_ref, eig_ref, w_ref, kern_ref,
    out_ref, out_pred_ref, sum_ref, moment_ref,
):
    half, count = kern_ref.shape
    core = core_ref[0]
    chips = mine_ref.shape[0]
    blocks = half // LANES
    outs = tgt_ref.shape[0]
    got = got_ref[...].astype(f32)
    sum_ref[...] = got.reshape(sum_ref.shape)
    out_pred_ref[:, pl.ds(pl.multiple_of(core * half, half), half)] = pred_ref[...]
    resids = []
    for r in range(blocks):
        at = pl.ds(pl.multiple_of((1 - core) * half + r * LANES, LANES), LANES)
        pred = read_pred(sum_ref, r, outs, 2 * blocks)
        out_pred_ref[:, at] = pred
        resids.append((pred - tgt_ref[:, at]).astype(bf16))
    other = jnp.concatenate(resids, axis=1)
    own = resid_ref[...]
    lines = chips * 2 * blocks
    for place, part in ((core, mine_ref[...].astype(f32)[:, : 2 * blocks]), (1 - core, swap_halves(got[:, : 2 * blocks], 1))):
        moment_ref[pl.ds(pl.multiple_of(place * lines, lines), lines), :] = part.reshape(lines, LANES)
    coeff = 0.0
    for n, resid in enumerate((own, other)):
        for r in range(blocks):
            moment = moment_ref[pl.ds(n * blocks + r, 2 * chips, stride=2 * blocks), :].astype(bf16)
            at = slice(r * LANES, (r + 1) * LANES)
            coeff += lax.dot_general(resid[:, at], moment, NT, preferred_element_type=f32)
    delta = 2.0 * lax.dot_general(
        coeff * damp_ref[...], eig_ref[...], NT, precision=lax.Precision.HIGHEST, preferred_element_type=f32
    )
    lane = lax.broadcasted_iota(jnp.int32, (outs, LANES), 1)
    col = 1024
    for i in range(count // col):
        at = slice(i * col, (i + 1) * col)
        grad = grad_ref[:, at] + jnp.dot(other, kern_ref[:, at], preferred_element_type=f32)
        shifts = []
        for k in range(i * (col // LANES), (i + 1) * (col // LANES)):
            shifts.append(jnp.where(lane == idx_ref[k] - k * LANES, delta[:, k : k + 1], 0.0))
        out_ref[:, at] = (w_ref[:, at] - 2.0 * grad) + jnp.concatenate(shifts, axis=1)


def finish(core, nys_index, mine, got, pred, resid, grad, targets, damping, eigvecs, weights, kern):
    chips, _, lanes = mine.shape
    return pl.pallas_call(
        finish_kernel,
        in_specs=[SMEM] * 2 + [VMEM] * 10,
        out_specs=[VMEM, VMEM],
        out_shape=[jax.ShapeDtypeStruct(weights.shape, f32), jax.ShapeDtypeStruct(targets.shape, f32)],
        scratch_shapes=[
            pltpu.VMEM((chips * PACK, lanes), f32),
            pltpu.VMEM((2 * chips * 2 * kern.shape[0] // LANES, lanes), f32),
        ],
        compiler_params=pltpu.CompilerParams(vmem_limit_bytes=12 * MIB),
        name="finish",
    )(core, nys_index, mine, got, pred, resid, grad, targets, damping[None, :], eigvecs, weights, in_vmem(kern))


def swap(x, axis):
    return lax.ppermute(x, axis, [(0, 1), (1, 0)])


def exchange(x, axes):
    return lax.all_to_all(x, axes, split_axis=0, concat_axis=0, tiled=True)


def body(pool, batch_index, targets, centers, weights, nys_index, eigvecs, damping):
    total = targets.shape[1]
    core = lax.axis_index("core").astype(jnp.int32)
    groups = lax.axis_size(CENTERS)
    share = total // (2 * groups)
    place = jnp.stack([lax.axis_index(LOADER), core, lax.axis_index(CENTERS) * share]).astype(jnp.int32)
    keep, give = pick_rows(place, batch_index, pool, share)
    rows = keep + swap(give, "core")
    rows = exchange(repeat_sum(rows, swap(rows, "zh"), groups), CENTERS)
    w_half, cen_sq, *nys = prepare(nys_index, weights, eigvecs, centers)
    core = core[None]

    rows, cen_sq, w_half, nys = lax.optimization_barrier((rows, cen_sq, w_half, nys))
    own = rows.reshape(groups * share, D)
    other = swap(own, "core")

    kern_own, pred = kernel_values(w_half, centers, own, cen_sq, nys)
    moment, give = nystrom_terms(core, nys, own, other)
    kern_other, pred_give = kernel_values(w_half, centers, other, cen_sq, (give, pred))
    packed = pack(moment, swap(give, "core"), pred, swap(pred_give, "core"))
    mine = exchange(sum_chips(exchange(packed, CHIPS)), CHIPS)
    got = swap(mine, "core")
    pred, resid, grad = own_grad(core, mine, targets, kern_own)
    return tuple(
        finish(core, nys_index, mine, got, pred, resid, grad, targets, damping, eigvecs, weights, kern_other)
    )


def solution(mesh):
    fine = Mesh(mesh.devices.reshape(2, 2, 4, 2, 4), ALL)
    return jax.shard_map(
        body,
        mesh=fine,
        in_specs=(
            P(LOADER, None),
            P(),
            P(),
            P(ALL, None),
            P(None, ALL),
            P(ALL),
            P(ALL, None),
            P(),
        ),
        out_specs=(P(None, ALL), P()),
        check_vma=False,
    )
```

```python
import functools
import math

import jax
import jax.numpy as jnp
from jax import lax
from jax.experimental import pallas as pl
from jax.experimental.pallas import tpu as pltpu
from jax.sharding import Mesh
from jax.sharding import PartitionSpec as P

f32, bf16 = jnp.float32, jnp.bfloat16
MIB = 2**20
LOADER = ("zh", "core")
CENTERS = ("y", "zl", "x")
ALL = LOADER + CENTERS
CHIPS = ("zh",) + CENTERS
PACK = 24
D = 256
LANES = 128
RATE = -4.0 / math.sqrt(D) * math.log2(math.e)
VMEM = pl.BlockSpec(memory_space=pltpu.VMEM)
SMEM = pl.BlockSpec(memory_space=pltpu.SMEM)
ANY = pl.BlockSpec(memory_space=pl.ANY)
HBM = pl.BlockSpec(memory_space=pltpu.HBM)
NT = (((1,), (1,)), ((), ()))


def in_hbm(x):
    return pltpu.with_memory_space_constraint(x, pltpu.HBM)


def in_vmem(x):
    return pltpu.with_memory_space_constraint(x, pltpu.VMEM)


def laplacian(dist_sq):
    safe = jnp.maximum(dist_sq, 1e-30)
    return jnp.exp2(safe * lax.rsqrt(safe) * RATE).astype(bf16)


def pick_kernel(place_ref, wanted_ref, pool_ref, keep_ref, give_ref, held_ref, row_ref, index_ref, sems, index_sem):
    share = keep_ref.shape[0]
    group = held_ref.shape[1]
    half = index_ref.shape[0] // 2
    mine, core, first = place_ref[0], place_ref[1], place_ref[2]
    rows = pool_ref.shape[0]
    listed = pltpu.make_async_copy(wanted_ref, index_ref, index_sem)
    listed.start()
    listed.wait()

    def local(n):
        of = jnp.where(n < share, core, 1 - core)
        return index_ref[of * half + first + jnp.where(n < share, n, n - share)] - mine * rows

    def copy(n, at):
        return pltpu.make_async_copy(pool_ref.at[pl.ds(pl.multiple_of(at, group), group), :], held_ref.at[n], sems.at[n])

    def owned(n, act):
        here = local(n)

        @pl.when(jnp.logical_and(here >= 0, here < rows))
        def _():
            act(jnp.clip(here, 0, rows - 1))

    def start(n, carry):
        owned(n, lambda here: copy(n, here - lax.rem(here, group)).start())
        return carry

    lax.fori_loop(0, 2 * share, start, 0, unroll=4)
    row_ref[...] = jnp.zeros_like(row_ref)
    line = lax.broadcasted_iota(jnp.int32, (group, D), 0)

    def select(n, carry):
        def take(here):
            copy(n, here - lax.rem(here, group)).wait()
            block = held_ref[n].astype(f32)
            row_ref[pl.ds(n, 1), :] = jnp.sum(jnp.where(line == lax.rem(here, group), block, 0.0), axis=0, keepdims=True)

        owned(n, take)
        return carry

    lax.fori_loop(0, 2 * share, select, 0, unroll=4)
    keep_ref[...] = row_ref[:share, :].astype(bf16)
    give_ref[...] = row_ref[share:, :].astype(bf16)


def pick_rows(place, batch_index, pool, share):
    group = 16
    return pl.pallas_call(
        pick_kernel,
        in_specs=[SMEM, HBM, HBM],
        out_specs=[VMEM, VMEM],
        out_shape=[jax.ShapeDtypeStruct((share, D), bf16)] * 2,
        scratch_shapes=[
            pltpu.VMEM((2 * share, group, D), bf16),
            pltpu.VMEM((2 * share, D), f32),
            pltpu.SMEM(batch_index.shape, jnp.int32),
            pltpu.SemaphoreType.DMA((2 * share,)),
            pltpu.SemaphoreType.DMA,
        ],
        compiler_params=pltpu.CompilerParams(vmem_limit_bytes=4 * MIB),
        name="pick_rows",
    )(place, in_hbm(batch_index), in_hbm(pool))


def repeat_kernel(keep_ref, got_ref, out_ref):
    out_ref[...] = jnp.broadcast_to((keep_ref[...] + got_ref[...])[None], out_ref.shape)


def repeat_sum(keep, got, times):
    return pl.pallas_call(
        repeat_kernel,
        in_specs=[VMEM, VMEM],
        out_specs=VMEM,
        out_shape=jax.ShapeDtypeStruct((times,) + keep.shape, bf16),
        compiler_params=pltpu.CompilerParams(vmem_limit_bytes=4 * MIB),
        name="repeat_sum",
    )(keep, got)


def row_norms(rows):
    wide = rows.astype(f32)
    square = wide * wide
    hi = square.astype(bf16)
    lo = (square - hi.astype(f32)).astype(bf16)
    ones = jnp.ones((8, rows.shape[1]), bf16)
    norms = lax.dot_general(ones, hi, NT, preferred_element_type=f32)
    norms += lax.dot_general(ones, lo, NT, preferred_element_type=f32)
    return norms[:1]


def prepare_kernel(
    idx_hbm, w_hbm, eig_hbm, cen_ref, w_half_ref, cen_sq_ref, nys_ref, nys_sq_ref, hi_ref, lo_ref,
    held_ref, picked_ref, idx_ref, w_ref, eig_ref, sems, side_sems,
):
    steps, col, _ = held_ref.shape
    per = 8

    def fetch(i):
        return pltpu.make_async_copy(cen_ref.at[pl.ds(pl.multiple_of(i * col, col), col), :], held_ref.at[i], sems.at[i])

    side = [
        pltpu.make_async_copy(*refs, side_sems.at[n])
        for n, refs in enumerate(((idx_hbm, idx_ref), (eig_hbm, eig_ref), (w_hbm, w_ref)))
    ]
    side[0].start()
    fetch(0).start()
    fetch(1).start()
    side[1].start()
    side[2].start()
    side[0].wait()
    row = lax.broadcasted_iota(jnp.int32, (per, col), 0)
    lane = lax.broadcasted_iota(jnp.int32, (per, col), 1)

    def step(i, carry):
        fetch(i).wait()

        @pl.when(i + 2 < steps)
        def _():
            fetch(i + 2).start()

        rows = held_ref[i]
        cen_sq_ref[:, pl.ds(pl.multiple_of(i * col, col), col)] = row_norms(rows)
        spot = jnp.full((per, col), -1, jnp.int32)
        for g in range(per):
            spot = jnp.where(row == g, idx_ref[i * per + g] - i * col, spot)
        chosen = jnp.where(lane == spot, 1.0, 0.0).astype(bf16)
        at = pl.ds(pl.multiple_of(i * per, per), per)
        picked_ref[at, :] = jnp.dot(chosen, rows, preferred_element_type=f32)
        return carry

    lax.fori_loop(0, steps, step, 0, unroll=2)
    side[1].wait()
    eig_t = eig_ref[...].T
    hi = eig_t.astype(bf16)
    hi_ref[...] = hi
    lo_ref[...] = (eig_t - hi.astype(f32)).astype(bf16)
    side[2].wait()
    w_half_ref[...] = w_ref[...].astype(bf16)
    nys = picked_ref[...].astype(bf16)
    nys_ref[...] = nys
    nys_sq_ref[...] = row_norms(nys)


def prepare(nys_index, weights, eigvecs, centers):
    count, points, vectors = centers.shape[0], nys_index.shape[0], eigvecs.shape[1]
    col = count // points * 8
    shapes = [
        (weights.shape, bf16),
        ((1, count), f32),
        ((points, D), bf16),
        ((1, points), f32),
        ((vectors, points), bf16),
        ((vectors, points), bf16),
    ]
    return pl.pallas_call(
        prepare_kernel,
        in_specs=[HBM] * 4,
        out_specs=[VMEM] * len(shapes),
        out_shape=[jax.ShapeDtypeStruct(*shape) for shape in shapes],
        scratch_shapes=[
            pltpu.VMEM((count // col, col, D), bf16),
            pltpu.VMEM((points, D), f32),
            pltpu.SMEM(nys_index.shape, jnp.int32),
            pltpu.VMEM(weights.shape, f32),
            pltpu.VMEM(eigvecs.shape, f32),
            pltpu.SemaphoreType.DMA((count // col,)),
            pltpu.SemaphoreType.DMA((3,)),
        ],
        compiler_params=pltpu.CompilerParams(vmem_limit_bytes=12 * MIB),
        cost_estimate=pl.CostEstimate(flops=4 * 10**9, bytes_accessed=2 * centers.size, transcendentals=0),
        name="prepare",
    )(in_hbm(nys_index), in_hbm(weights), in_hbm(eigvecs), in_hbm(centers))


def values_kernel(w_ref, batch_ref, cen_sq_ref, cen_ref, *refs, first):
    if first:
        kern_ref, pred_ref, held_ref, rows_ref, sq_ref, acc_ref, sems = refs[-7:]
    else:
        kern_ref, pred_ref, rows_ref, sq_ref, acc_ref = refs[-5:]
        held_ref = cen_ref
    batch, count = kern_ref.shape
    col, row, sub = 2048, 512, 256
    steps = count // col

    def fetch(i):
        at = pl.ds(pl.multiple_of(i * col, col), col)
        return pltpu.make_async_copy(cen_ref.at[at, :], held_ref.at[at, :], sems.at[i])

    if first:
        fetch(0).start()
    rows = batch_ref[...]
    wide = rows.astype(f32)
    rows_ref[...] = rows * (-2)
    sq_ref[...] = jnp.broadcast_to(jnp.sum(wide * wide, axis=1, keepdims=True), (batch, LANES))
    acc_ref[...] = jnp.zeros_like(acc_ref)

    def step(i, carry):
        if first:
            fetch(i).wait()

            @pl.when(i + 1 < steps)
            def _():
                fetch(i + 1).start()

        for j in range(batch // row):
            at = slice(j * row, (j + 1) * row)
            row_sq = jnp.concatenate([sq_ref[at, :]] * (sub // LANES), axis=1)
            acc = acc_ref[:, at]
            for n in range(col // sub):
                cols = pl.ds(pl.multiple_of(i * col + n * sub, sub), sub)
                cross = lax.dot_general(rows_ref[at, :], held_ref[cols, :], NT, preferred_element_type=f32)
                kern = laplacian((cross + row_sq) + cen_sq_ref[:, cols])
                kern_ref[at, cols] = kern
                acc += lax.dot_general(w_ref[:, cols], kern, NT, preferred_element_type=f32)
            acc_ref[:, at] = acc
        return carry

    lax.fori_loop(0, steps, step, 0)
    for r in range(batch // LANES):
        pred_ref[:, r, :] = acc_ref[:, r * LANES : (r + 1) * LANES]


def kernel_values(w_half, centers, batch, cen_sq, after, first):
    half, count, outs = batch.shape[0], centers.shape[0], w_half.shape[0]
    col = 2048
    held = [pltpu.VMEM(centers.shape, bf16)] if first else []
    return pl.pallas_call(
        functools.partial(values_kernel, first=first),
        in_specs=[VMEM] * 3 + [HBM if first else VMEM] + [ANY] * len(after),
        out_specs=[VMEM] * (2 + len(held)),
        out_shape=[pltpu.VMEM((half, count), bf16), jax.ShapeDtypeStruct((outs, half // LANES, LANES), f32)] + held,
        scratch_shapes=[
            pltpu.VMEM((half, D), bf16),
            pltpu.VMEM((half, LANES), f32),
            pltpu.VMEM((outs, half), f32),
        ]
        + [pltpu.SemaphoreType.DMA((count // col,))] * len(held),
        compiler_params=pltpu.CompilerParams(vmem_limit_bytes=8 * MIB),
        cost_estimate=pl.CostEstimate(
            flops=8 * half * count * D, bytes_accessed=2 * half * count, transcendentals=2 * half * count
        ),
        name="kernel_values",
    )(w_half, batch, cen_sq, in_hbm(centers) if first else in_vmem(centers), *after)


def nystrom_kernel(core_ref, cen_ref, sq_ref, hi_ref, lo_ref, own_ref, other_ref, keep_ref, give_ref, acc_ref):
    cen = cen_ref[...]
    core = core_ref[0]
    half = own_ref.shape[0]
    count, blocks = hi_ref.shape[0], keep_ref.shape[1]
    for ref, first in ((own_ref, 0), (other_ref, half // LANES)):
        rows = ref[...]
        wide = rows.astype(f32)
        cross = lax.dot_general(rows * (-2), cen, NT, preferred_element_type=f32)
        kern = laplacian((cross + jnp.sum(wide * wide, axis=1, keepdims=True)) + sq_ref[...])
        part = lax.dot_general(hi_ref[...], kern, NT, preferred_element_type=f32)
        part += lax.dot_general(lo_ref[...], kern, NT, preferred_element_type=f32)
        for r in range(half // LANES):
            acc_ref[pl.ds(first + r, count, stride=blocks), :] = part[:, r * LANES : (r + 1) * LANES]
    lines = count // 2 * blocks
    for ref, place in ((keep_ref, core), (give_ref, 1 - core)):
        part = acc_ref[pl.ds(pl.multiple_of(place * lines, lines), lines), :]
        ref[...] = part.reshape(ref.shape).astype(bf16)


def nystrom_terms(core, nys, own, other):
    vectors, blocks = nys[2].shape[0], 2 * own.shape[0] // LANES
    return pl.pallas_call(
        nystrom_kernel,
        in_specs=[SMEM] + [VMEM] * 6,
        out_specs=[VMEM, VMEM],
        out_shape=[jax.ShapeDtypeStruct((vectors // 2, blocks, LANES), bf16)] * 2,
        scratch_shapes=[pltpu.VMEM((vectors * blocks, LANES), f32)],
        compiler_params=pltpu.CompilerParams(vmem_limit_bytes=12 * MIB),
        cost_estimate=pl.CostEstimate(flops=2 * 10**9, bytes_accessed=2**20, transcendentals=2**18),
        name="nystrom_terms",
    )(core, *nys, own, other)


def split3(x):
    hi = x.astype(bf16).astype(f32)
    mid = (x - hi).astype(bf16).astype(f32)
    return hi, mid, (x - hi) - mid


def swap_halves(x, axis):
    first, last = jnp.split(x, 2, axis)
    return jnp.concatenate([last, first], axis)


def pack_kernel(moment_ref, moment_in_ref, pred_ref, pred_in_ref, out_ref, acc_ref):
    vectors, blocks, _ = moment_ref.shape
    acc_ref[:, :blocks, :] = swap_halves(moment_in_ref[...].astype(f32), 1) + moment_ref[...].astype(f32)
    acc_ref[:, blocks:, :] = jnp.zeros((vectors, PACK - blocks, LANES), f32)
    pred = pred_ref[...] + pred_in_ref[...]
    parts = split3(pred)
    per = pred.shape[1] // 2
    for j in range(vectors):
        o, r = j // per, j % per * 2
        for n, part in enumerate(parts):
            acc_ref[j, blocks + 2 * n : blocks + 2 * n + 2, :] = part[o, r : r + 2, :]
    out_ref[...] = acc_ref[...].astype(bf16)


def pack(moment, moment_in, pred, pred_in):
    shape = (moment.shape[0], PACK, LANES)
    return pl.pallas_call(
        pack_kernel,
        in_specs=[VMEM] * 4,
        out_specs=VMEM,
        out_shape=jax.ShapeDtypeStruct(shape, bf16),
        scratch_shapes=[pltpu.VMEM(shape, f32)],
        compiler_params=pltpu.CompilerParams(vmem_limit_bytes=8 * MIB),
        name="pack",
    )(moment, moment_in, pred, pred_in)


def sum_kernel(part_ref, out_ref, acc_ref):
    blocks = 16
    acc_ref[...] = jnp.sum(part_ref[...].astype(f32), axis=0)
    pred = (acc_ref[blocks : blocks + 2, :] + acc_ref[blocks + 2 : blocks + 4, :]) + acc_ref[blocks + 4 : blocks + 6, :]
    for n, part in enumerate(split3(pred)):
        acc_ref[blocks + 2 * n : blocks + 2 * n + 2, :] = part
    out_ref[...] = jnp.broadcast_to(acc_ref[...].astype(bf16)[None], out_ref.shape)


def sum_chips(parts):
    return pl.pallas_call(
        sum_kernel,
        in_specs=[VMEM],
        out_specs=VMEM,
        out_shape=jax.ShapeDtypeStruct(parts.shape, bf16),
        scratch_shapes=[pltpu.VMEM(parts.shape[1:], f32)],
        compiler_params=pltpu.CompilerParams(vmem_limit_bytes=8 * MIB),
        name="sum_chips",
    )(parts)


def read_pred(sum_ref, r, outs, blocks):
    chips = sum_ref.shape[0] // PACK

    def part(n):
        line = r // 2 * PACK + blocks + r % 2 + 2 * n
        return sum_ref[pl.ds(line, outs, stride=chips // outs * PACK), :]

    return (part(0) + part(1)) + part(2)


def grad_kernel(core_ref, mine_ref, tgt_ref, kern_ref, pred_ref, resid_ref, grad_ref, sum_ref):
    half, count = kern_ref.shape
    blocks = half // LANES
    sum_ref[...] = mine_ref[...].astype(f32).reshape(sum_ref.shape)
    for r in range(blocks):
        at = slice(r * LANES, (r + 1) * LANES)
        pred = read_pred(sum_ref, r, tgt_ref.shape[0], 2 * blocks)
        pred_ref[:, at] = pred
        tgt = tgt_ref[:, pl.ds(pl.multiple_of(core_ref[0] * half + r * LANES, LANES), LANES)]
        resid_ref[:, at] = (pred - tgt).astype(bf16)
    resid = resid_ref[...]
    col = 1024
    for i in range(count // col):
        at = slice(i * col, (i + 1) * col)
        grad_ref[:, at] = jnp.dot(resid, kern_ref[:, at], preferred_element_type=f32)


def own_grad(core, mine, targets, kern):
    half, count = kern.shape
    outs = targets.shape[0]
    return pl.pallas_call(
        grad_kernel,
        in_specs=[SMEM] + [VMEM] * 3,
        out_specs=[VMEM] * 3,
        out_shape=[
            jax.ShapeDtypeStruct((outs, half), f32),
            jax.ShapeDtypeStruct((outs, half), bf16),
            jax.ShapeDtypeStruct((outs, count), f32),
        ],
        scratch_shapes=[pltpu.VMEM((mine.shape[0] * PACK, LANES), f32)],
        compiler_params=pltpu.CompilerParams(vmem_limit_bytes=8 * MIB),
        cost_estimate=pl.CostEstimate(flops=512 * half * count, bytes_accessed=2 * half * count, transcendentals=0),
        name="own_grad",
    )(core, mine, targets, in_vmem(kern))


def finish_kernel(
    core_ref, idx_ref, mine_ref, got_ref, pred_ref, resid_ref, grad_ref, tgt_ref, damp_ref, eig_ref, w_ref, kern_ref,
    out_hbm, out_pred_ref, sum_ref, moment_ref, out_ref, sems,
):
    half, count = kern_ref.shape
    core = core_ref[0]
    chips = mine_ref.shape[0]
    blocks = half // LANES
    outs = tgt_ref.shape[0]
    got = got_ref[...].astype(f32)
    sum_ref[...] = got.reshape(sum_ref.shape)
    out_pred_ref[:, pl.ds(pl.multiple_of(core * half, half), half)] = pred_ref[...]
    resids = []
    for r in range(blocks):
        at = pl.ds(pl.multiple_of((1 - core) * half + r * LANES, LANES), LANES)
        pred = read_pred(sum_ref, r, outs, 2 * blocks)
        out_pred_ref[:, at] = pred
        resids.append((pred - tgt_ref[:, at]).astype(bf16))
    other = jnp.concatenate(resids, axis=1)
    own = resid_ref[...]
    lines = chips * 2 * blocks
    for place, part in ((core, mine_ref[...].astype(f32)[:, : 2 * blocks]), (1 - core, swap_halves(got[:, : 2 * blocks], 1))):
        moment_ref[pl.ds(pl.multiple_of(place * lines, lines), lines), :] = part.reshape(lines, LANES)
    coeff = 0.0
    for n, resid in enumerate((own, other)):
        for r in range(blocks):
            moment = moment_ref[pl.ds(n * blocks + r, 2 * chips, stride=2 * blocks), :].astype(bf16)
            at = slice(r * LANES, (r + 1) * LANES)
            coeff += lax.dot_general(resid[:, at], moment, NT, preferred_element_type=f32)
    delta = 2.0 * lax.dot_general(
        coeff * damp_ref[...], eig_ref[...], NT, precision=lax.Precision.HIGHEST, preferred_element_type=f32
    )
    lane = lax.broadcasted_iota(jnp.int32, (outs, LANES), 1)
    col = 1024

    def leave(i):
        at = slice(i * col, (i + 1) * col)
        return pltpu.make_async_copy(out_ref.at[:, at], out_hbm.at[:, at], sems.at[i])

    for i in range(count // col):
        at = slice(i * col, (i + 1) * col)
        grad = grad_ref[:, at] + jnp.dot(other, kern_ref[:, at], preferred_element_type=f32)
        shifts = []
        for k in range(i * (col // LANES), (i + 1) * (col // LANES)):
            shifts.append(jnp.where(lane == idx_ref[k] - k * LANES, delta[:, k : k + 1], 0.0))
        out_ref[:, at] = (w_ref[:, at] - 2.0 * grad) + jnp.concatenate(shifts, axis=1)
        leave(i).start()
    for i in range(count // col):
        leave(i).wait()


def finish(core, nys_index, mine, got, pred, resid, grad, targets, damping, eigvecs, weights, kern):
    chips, _, lanes = mine.shape
    return pl.pallas_call(
        finish_kernel,
        in_specs=[SMEM] * 2 + [VMEM] * 10,
        out_specs=[HBM, VMEM],
        out_shape=[jax.ShapeDtypeStruct(weights.shape, f32), jax.ShapeDtypeStruct(targets.shape, f32)],
        scratch_shapes=[
            pltpu.VMEM((chips * PACK, lanes), f32),
            pltpu.VMEM((2 * chips * 2 * kern.shape[0] // LANES, lanes), f32),
            pltpu.VMEM(weights.shape, f32),
            pltpu.SemaphoreType.DMA((8,)),
        ],
        compiler_params=pltpu.CompilerParams(vmem_limit_bytes=12 * MIB),
        name="finish",
    )(core, nys_index, mine, got, pred, resid, grad, targets, damping[None, :], eigvecs, weights, in_vmem(kern))


def swap(x, axis):
    return lax.ppermute(x, axis, [(0, 1), (1, 0)])


def exchange(x, axes):
    return lax.all_to_all(x, axes, split_axis=0, concat_axis=0, tiled=True)


def body(pool, batch_index, targets, centers, weights, nys_index, eigvecs, damping):
    total = targets.shape[1]
    core = lax.axis_index("core").astype(jnp.int32)
    groups = lax.axis_size(CENTERS)
    share = total // (2 * groups)
    place = jnp.stack([lax.axis_index(LOADER), core, lax.axis_index(CENTERS) * share]).astype(jnp.int32)
    keep, give = pick_rows(place, batch_index, pool, share)
    rows = keep + swap(give, "core")
    rows = exchange(repeat_sum(rows, swap(rows, "zh"), groups), CENTERS)
    w_half, cen_sq, *nys = prepare(nys_index, weights, eigvecs, centers)
    core = core[None]

    rows, cen_sq, w_half, nys = lax.optimization_barrier((rows, cen_sq, w_half, nys))
    own = rows.reshape(groups * share, D)
    other = swap(own, "core")

    kern_own, pred, held = kernel_values(w_half, centers, own, cen_sq, nys, True)
    moment, give = nystrom_terms(core, nys, own, other)
    kern_other, pred_give = kernel_values(w_half, held, other, cen_sq, (give, pred), False)
    packed = pack(moment, swap(give, "core"), pred, swap(pred_give, "core"))
    mine = exchange(sum_chips(exchange(packed, CHIPS)), CHIPS)
    got = swap(mine, "core")
    pred, resid, grad = own_grad(core, mine, targets, kern_own)
    return tuple(
        finish(core, nys_index, mine, got, pred, resid, grad, targets, damping, eigvecs, weights, kern_other)
    )


def solution(mesh):
    fine = Mesh(mesh.devices.reshape(2, 2, 4, 2, 4), ALL)
    return jax.shard_map(
        body,
        mesh=fine,
        in_specs=(
            P(LOADER, None),
            P(),
            P(),
            P(ALL, None),
            P(None, ALL),
            P(ALL),
            P(ALL, None),
            P(),
        ),
        out_specs=(P(None, ALL), P()),
        check_vma=False,
    )
```

```python
import functools
import math

import jax
import jax.numpy as jnp
from jax import lax
from jax.experimental import pallas as pl
from jax.experimental.pallas import tpu as pltpu
from jax.sharding import Mesh
from jax.sharding import PartitionSpec as P

f32, bf16 = jnp.float32, jnp.bfloat16
MIB = 2**20
LOADER = ("zh", "core")
CENTERS = ("y", "zl", "x")
ALL = LOADER + CENTERS
CHIPS = ("zh",) + CENTERS
PACK = 24
STEP = 2048
D = 256
LANES = 128
RATE = -4.0 / math.sqrt(D) * math.log2(math.e)
VMEM = pl.BlockSpec(memory_space=pltpu.VMEM)
SMEM = pl.BlockSpec(memory_space=pltpu.SMEM)
ANY = pl.BlockSpec(memory_space=pl.ANY)
HBM = pl.BlockSpec(memory_space=pltpu.HBM)
NT = (((1,), (1,)), ((), ()))


def in_hbm(x):
    return pltpu.with_memory_space_constraint(x, pltpu.HBM)


def in_vmem(x):
    return pltpu.with_memory_space_constraint(x, pltpu.VMEM)


def laplacian(dist_sq):
    safe = jnp.maximum(dist_sq, 1e-30)
    return jnp.exp2(safe * lax.rsqrt(safe) * RATE).astype(bf16)


def pick_kernel(place_ref, wanted_ref, pool_ref, keep_ref, give_ref, held_ref, row_ref, index_ref, sems, index_sem):
    share = keep_ref.shape[0]
    group = held_ref.shape[1]
    half = index_ref.shape[0] // 2
    mine, core, first = place_ref[0], place_ref[1], place_ref[2]
    rows = pool_ref.shape[0]
    listed = pltpu.make_async_copy(wanted_ref, index_ref, index_sem)
    listed.start()
    listed.wait()

    def local(n):
        of = jnp.where(n < share, core, 1 - core)
        return index_ref[of * half + first + jnp.where(n < share, n, n - share)] - mine * rows

    def copy(n, at):
        return pltpu.make_async_copy(pool_ref.at[pl.ds(pl.multiple_of(at, group), group), :], held_ref.at[n], sems.at[n])

    def owned(n, act):
        here = local(n)

        @pl.when(jnp.logical_and(here >= 0, here < rows))
        def _():
            act(jnp.clip(here, 0, rows - 1))

    def start(n, carry):
        owned(n, lambda here: copy(n, here - lax.rem(here, group)).start())
        return carry

    lax.fori_loop(0, 2 * share, start, 0, unroll=4)
    row_ref[...] = jnp.zeros_like(row_ref)
    line = lax.broadcasted_iota(jnp.int32, (group, D), 0)

    def select(n, carry):
        def take(here):
            copy(n, here - lax.rem(here, group)).wait()
            block = held_ref[n].astype(f32)
            row_ref[pl.ds(n, 1), :] = jnp.sum(jnp.where(line == lax.rem(here, group), block, 0.0), axis=0, keepdims=True)

        owned(n, take)
        return carry

    lax.fori_loop(0, 2 * share, select, 0, unroll=4)
    keep_ref[...] = row_ref[:share, :].astype(bf16)
    give_ref[...] = row_ref[share:, :].astype(bf16)


def pick_rows(place, batch_index, pool, share):
    group = 16
    return pl.pallas_call(
        pick_kernel,
        in_specs=[SMEM, HBM, HBM],
        out_specs=[VMEM, VMEM],
        out_shape=[jax.ShapeDtypeStruct((share, D), bf16)] * 2,
        scratch_shapes=[
            pltpu.VMEM((2 * share, group, D), bf16),
            pltpu.VMEM((2 * share, D), f32),
            pltpu.SMEM(batch_index.shape, jnp.int32),
            pltpu.SemaphoreType.DMA((2 * share,)),
            pltpu.SemaphoreType.DMA,
        ],
        compiler_params=pltpu.CompilerParams(vmem_limit_bytes=4 * MIB),
        name="pick_rows",
    )(place, in_hbm(batch_index), in_hbm(pool))


def repeat_kernel(keep_ref, got_ref, out_ref):
    out_ref[...] = jnp.broadcast_to((keep_ref[...] + got_ref[...])[None], out_ref.shape)


def repeat_sum(keep, got, times):
    return pl.pallas_call(
        repeat_kernel,
        in_specs=[VMEM, VMEM],
        out_specs=VMEM,
        out_shape=jax.ShapeDtypeStruct((times,) + keep.shape, bf16),
        compiler_params=pltpu.CompilerParams(vmem_limit_bytes=4 * MIB),
        name="repeat_sum",
    )(keep, got)


def row_norms(rows):
    wide = rows.astype(f32)
    square = wide * wide
    hi = square.astype(bf16)
    lo = (square - hi.astype(f32)).astype(bf16)
    ones = jnp.ones((8, rows.shape[1]), bf16)
    norms = lax.dot_general(ones, hi, NT, preferred_element_type=f32)
    norms += lax.dot_general(ones, lo, NT, preferred_element_type=f32)
    return norms[:1]


def prepare_kernel(
    idx_hbm, w_hbm, eig_hbm, cen_ref, w_half_ref, cen_sq_ref, head_ref, nys_ref, nys_sq_ref, hi_ref, lo_ref,
    held_ref, picked_ref, idx_ref, w_ref, eig_ref, sems, side_sems,
):
    steps, col, _ = held_ref.shape
    per = 8

    def fetch(i):
        return pltpu.make_async_copy(cen_ref.at[pl.ds(pl.multiple_of(i * col, col), col), :], held_ref.at[i], sems.at[i])

    side = [
        pltpu.make_async_copy(*refs, side_sems.at[n])
        for n, refs in enumerate(((idx_hbm, idx_ref), (eig_hbm, eig_ref), (w_hbm, w_ref)))
    ]
    side[0].start()
    fetch(0).start()
    fetch(1).start()
    side[1].start()
    side[2].start()
    side[0].wait()
    row = lax.broadcasted_iota(jnp.int32, (per, col), 0)
    lane = lax.broadcasted_iota(jnp.int32, (per, col), 1)

    def step(i, carry):
        fetch(i).wait()

        @pl.when(i + 2 < steps)
        def _():
            fetch(i + 2).start()

        rows = held_ref[i]
        cen_sq_ref[:, pl.ds(pl.multiple_of(i * col, col), col)] = row_norms(rows)
        spot = jnp.full((per, col), -1, jnp.int32)
        for g in range(per):
            spot = jnp.where(row == g, idx_ref[i * per + g] - i * col, spot)
        chosen = jnp.where(lane == spot, 1.0, 0.0).astype(bf16)
        at = pl.ds(pl.multiple_of(i * per, per), per)
        picked_ref[at, :] = jnp.dot(chosen, rows, preferred_element_type=f32)
        return carry

    lax.fori_loop(0, steps, step, 0, unroll=2)
    side[1].wait()
    for n in range(head_ref.shape[0] // col):
        head_ref[n * col : (n + 1) * col, :] = held_ref[n]
    eig_t = eig_ref[...].T
    hi = eig_t.astype(bf16)
    hi_ref[...] = hi
    lo_ref[...] = (eig_t - hi.astype(f32)).astype(bf16)
    side[2].wait()
    w_half_ref[...] = w_ref[...].astype(bf16)
    nys = picked_ref[...].astype(bf16)
    nys_ref[...] = nys
    nys_sq_ref[...] = row_norms(nys)


def prepare(nys_index, weights, eigvecs, centers):
    count, points, vectors = centers.shape[0], nys_index.shape[0], eigvecs.shape[1]
    col = count // points * 8
    shapes = [
        (weights.shape, bf16),
        ((1, count), f32),
        ((STEP, D), bf16),
        ((points, D), bf16),
        ((1, points), f32),
        ((vectors, points), bf16),
        ((vectors, points), bf16),
    ]
    return pl.pallas_call(
        prepare_kernel,
        in_specs=[HBM] * 4,
        out_specs=[VMEM] * len(shapes),
        out_shape=[pltpu.VMEM(*shape) if n == 2 else jax.ShapeDtypeStruct(*shape) for n, shape in enumerate(shapes)],
        scratch_shapes=[
            pltpu.VMEM((count // col, col, D), bf16),
            pltpu.VMEM((points, D), f32),
            pltpu.SMEM(nys_index.shape, jnp.int32),
            pltpu.VMEM(weights.shape, f32),
            pltpu.VMEM(eigvecs.shape, f32),
            pltpu.SemaphoreType.DMA((count // col,)),
            pltpu.SemaphoreType.DMA((3,)),
        ],
        compiler_params=pltpu.CompilerParams(vmem_limit_bytes=12 * MIB),
        cost_estimate=pl.CostEstimate(flops=4 * 10**9, bytes_accessed=2 * centers.size, transcendentals=0),
        name="prepare",
    )(in_hbm(nys_index), in_hbm(weights), in_hbm(eigvecs), in_hbm(centers))


def values_kernel(w_ref, batch_ref, cen_sq_ref, cen_ref, *refs, first):
    if first:
        kern_ref, pred_ref, held_ref, rows_ref, sq_ref, acc_ref, sems = refs[-7:]
    else:
        kern_ref, pred_ref, rows_ref, sq_ref, acc_ref = refs[-5:]
        held_ref = cen_ref
    batch, count = kern_ref.shape
    col, row, sub = STEP, 512, 256
    steps = count // col

    def fetch(i):
        at = pl.ds(pl.multiple_of(i * col, col), col)
        return pltpu.make_async_copy(cen_ref.at[at, :], held_ref.at[at, :], sems.at[i])

    if first:
        fetch(1).start()
        held_ref[:col, :] = refs[0][...]
    rows = batch_ref[...]
    wide = rows.astype(f32)
    rows_ref[...] = rows * (-2)
    sq_ref[...] = jnp.broadcast_to(jnp.sum(wide * wide, axis=1, keepdims=True), (batch, LANES))
    acc_ref[...] = jnp.zeros_like(acc_ref)

    def step(i, carry):
        if first:

            @pl.when(i > 0)
            def _():
                fetch(i).wait()

            @pl.when(jnp.logical_and(i > 0, i + 1 < steps))
            def _():
                fetch(i + 1).start()

        for j in range(batch // row):
            at = slice(j * row, (j + 1) * row)
            row_sq = jnp.concatenate([sq_ref[at, :]] * (sub // LANES), axis=1)
            acc = acc_ref[:, at]
            for n in range(col // sub):
                cols = pl.ds(pl.multiple_of(i * col + n * sub, sub), sub)
                cross = lax.dot_general(rows_ref[at, :], held_ref[cols, :], NT, preferred_element_type=f32)
                kern = laplacian((cross + row_sq) + cen_sq_ref[:, cols])
                kern_ref[at, cols] = kern
                acc += lax.dot_general(w_ref[:, cols], kern, NT, preferred_element_type=f32)
            acc_ref[:, at] = acc
        return carry

    lax.fori_loop(0, steps, step, 0)
    for r in range(batch // LANES):
        pred_ref[:, r, :] = acc_ref[:, r * LANES : (r + 1) * LANES]


def kernel_values(w_half, centers, batch, cen_sq, after, head=None):
    half, count, outs = batch.shape[0], centers.shape[0], w_half.shape[0]
    first = head is not None
    heads = [in_vmem(head)] if first else []
    held = [pltpu.VMEM(centers.shape, bf16)] if first else []
    return pl.pallas_call(
        functools.partial(values_kernel, first=first),
        in_specs=[VMEM] * 3 + [HBM if first else VMEM] + [VMEM] * len(heads) + [ANY] * len(after),
        out_specs=[VMEM] * (2 + len(held)),
        out_shape=[pltpu.VMEM((half, count), bf16), jax.ShapeDtypeStruct((outs, half // LANES, LANES), f32)] + held,
        scratch_shapes=[
            pltpu.VMEM((half, D), bf16),
            pltpu.VMEM((half, LANES), f32),
            pltpu.VMEM((outs, half), f32),
        ]
        + [pltpu.SemaphoreType.DMA((count // STEP,))] * len(held),
        compiler_params=pltpu.CompilerParams(vmem_limit_bytes=8 * MIB),
        cost_estimate=pl.CostEstimate(
            flops=8 * half * count * D, bytes_accessed=2 * half * count, transcendentals=2 * half * count
        ),
        name="kernel_values",
    )(w_half, batch, cen_sq, in_hbm(centers) if first else in_vmem(centers), *heads, *after)


def nystrom_kernel(core_ref, cen_ref, sq_ref, hi_ref, lo_ref, own_ref, other_ref, keep_ref, give_ref, acc_ref):
    cen = cen_ref[...]
    core = core_ref[0]
    half = own_ref.shape[0]
    count, blocks = hi_ref.shape[0], keep_ref.shape[1]
    for ref, first in ((own_ref, 0), (other_ref, half // LANES)):
        rows = ref[...]
        wide = rows.astype(f32)
        cross = lax.dot_general(rows * (-2), cen, NT, preferred_element_type=f32)
        kern = laplacian((cross + jnp.sum(wide * wide, axis=1, keepdims=True)) + sq_ref[...])
        part = lax.dot_general(hi_ref[...], kern, NT, preferred_element_type=f32)
        part += lax.dot_general(lo_ref[...], kern, NT, preferred_element_type=f32)
        for r in range(half // LANES):
            acc_ref[pl.ds(first + r, count, stride=blocks), :] = part[:, r * LANES : (r + 1) * LANES]
    lines = count // 2 * blocks
    for ref, place in ((keep_ref, core), (give_ref, 1 - core)):
        part = acc_ref[pl.ds(pl.multiple_of(place * lines, lines), lines), :]
        ref[...] = part.reshape(ref.shape).astype(bf16)


def nystrom_terms(core, nys, own, other):
    vectors, blocks = nys[2].shape[0], 2 * own.shape[0] // LANES
    return pl.pallas_call(
        nystrom_kernel,
        in_specs=[SMEM] + [VMEM] * 6,
        out_specs=[VMEM, VMEM],
        out_shape=[jax.ShapeDtypeStruct((vectors // 2, blocks, LANES), bf16)] * 2,
        scratch_shapes=[pltpu.VMEM((vectors * blocks, LANES), f32)],
        compiler_params=pltpu.CompilerParams(vmem_limit_bytes=12 * MIB),
        cost_estimate=pl.CostEstimate(flops=2 * 10**9, bytes_accessed=2**20, transcendentals=2**18),
        name="nystrom_terms",
    )(core, *nys, own, other)


def split3(x):
    hi = x.astype(bf16).astype(f32)
    mid = (x - hi).astype(bf16).astype(f32)
    return hi, mid, (x - hi) - mid


def swap_halves(x, axis):
    first, last = jnp.split(x, 2, axis)
    return jnp.concatenate([last, first], axis)


def pack_kernel(moment_ref, moment_in_ref, pred_ref, pred_in_ref, out_ref, acc_ref):
    vectors, blocks, _ = moment_ref.shape
    acc_ref[:, :blocks, :] = swap_halves(moment_in_ref[...].astype(f32), 1) + moment_ref[...].astype(f32)
    acc_ref[:, blocks:, :] = jnp.zeros((vectors, PACK - blocks, LANES), f32)
    pred = pred_ref[...] + pred_in_ref[...]
    parts = split3(pred)
    per = pred.shape[1] // 2
    for j in range(vectors):
        o, r = j // per, j % per * 2
        for n, part in enumerate(parts):
            acc_ref[j, blocks + 2 * n : blocks + 2 * n + 2, :] = part[o, r : r + 2, :]
    out_ref[...] = acc_ref[...].astype(bf16)


def pack(moment, moment_in, pred, pred_in):
    shape = (moment.shape[0], PACK, LANES)
    return pl.pallas_call(
        pack_kernel,
        in_specs=[VMEM] * 4,
        out_specs=VMEM,
        out_shape=jax.ShapeDtypeStruct(shape, bf16),
        scratch_shapes=[pltpu.VMEM(shape, f32)],
        compiler_params=pltpu.CompilerParams(vmem_limit_bytes=8 * MIB),
        name="pack",
    )(moment, moment_in, pred, pred_in)


def sum_kernel(part_ref, out_ref, acc_ref):
    blocks = 16
    acc_ref[...] = jnp.sum(part_ref[...].astype(f32), axis=0)
    pred = (acc_ref[blocks : blocks + 2, :] + acc_ref[blocks + 2 : blocks + 4, :]) + acc_ref[blocks + 4 : blocks + 6, :]
    for n, part in enumerate(split3(pred)):
        acc_ref[blocks + 2 * n : blocks + 2 * n + 2, :] = part
    out_ref[...] = jnp.broadcast_to(acc_ref[...].astype(bf16)[None], out_ref.shape)


def sum_chips(parts):
    return pl.pallas_call(
        sum_kernel,
        in_specs=[VMEM],
        out_specs=VMEM,
        out_shape=jax.ShapeDtypeStruct(parts.shape, bf16),
        scratch_shapes=[pltpu.VMEM(parts.shape[1:], f32)],
        compiler_params=pltpu.CompilerParams(vmem_limit_bytes=8 * MIB),
        name="sum_chips",
    )(parts)


def read_pred(sum_ref, r, outs, blocks):
    chips = sum_ref.shape[0] // PACK

    def part(n):
        line = r // 2 * PACK + blocks + r % 2 + 2 * n
        return sum_ref[pl.ds(line, outs, stride=chips // outs * PACK), :]

    return (part(0) + part(1)) + part(2)


def grad_kernel(core_ref, mine_ref, tgt_ref, kern_ref, pred_ref, resid_ref, grad_ref, sum_ref):
    half, count = kern_ref.shape
    blocks = half // LANES
    sum_ref[...] = mine_ref[...].astype(f32).reshape(sum_ref.shape)
    for r in range(blocks):
        at = slice(r * LANES, (r + 1) * LANES)
        pred = read_pred(sum_ref, r, tgt_ref.shape[0], 2 * blocks)
        pred_ref[:, at] = pred
        tgt = tgt_ref[:, pl.ds(pl.multiple_of(core_ref[0] * half + r * LANES, LANES), LANES)]
        resid_ref[:, at] = (pred - tgt).astype(bf16)
    resid = resid_ref[...]
    col = 1024
    for i in range(count // col):
        at = slice(i * col, (i + 1) * col)
        grad_ref[:, at] = jnp.dot(resid, kern_ref[:, at], preferred_element_type=f32)


def own_grad(core, mine, targets, kern):
    half, count = kern.shape
    outs = targets.shape[0]
    return pl.pallas_call(
        grad_kernel,
        in_specs=[SMEM] + [VMEM] * 3,
        out_specs=[VMEM] * 3,
        out_shape=[
            jax.ShapeDtypeStruct((outs, half), f32),
            jax.ShapeDtypeStruct((outs, half), bf16),
            jax.ShapeDtypeStruct((outs, count), f32),
        ],
        scratch_shapes=[pltpu.VMEM((mine.shape[0] * PACK, LANES), f32)],
        compiler_params=pltpu.CompilerParams(vmem_limit_bytes=8 * MIB),
        cost_estimate=pl.CostEstimate(flops=512 * half * count, bytes_accessed=2 * half * count, transcendentals=0),
        name="own_grad",
    )(core, mine, targets, in_vmem(kern))


def finish_kernel(
    core_ref, idx_ref, mine_ref, got_ref, pred_ref, resid_ref, grad_ref, tgt_ref, damp_ref, eig_ref, w_ref, kern_ref,
    out_ref, out_pred_ref, sum_ref, moment_ref,
):
    half, count = kern_ref.shape
    core = core_ref[0]
    chips = mine_ref.shape[0]
    blocks = half // LANES
    outs = tgt_ref.shape[0]
    got = got_ref[...].astype(f32)
    sum_ref[...] = got.reshape(sum_ref.shape)
    out_pred_ref[:, pl.ds(pl.multiple_of(core * half, half), half)] = pred_ref[...]
    resids = []
    for r in range(blocks):
        at = pl.ds(pl.multiple_of((1 - core) * half + r * LANES, LANES), LANES)
        pred = read_pred(sum_ref, r, outs, 2 * blocks)
        out_pred_ref[:, at] = pred
        resids.append((pred - tgt_ref[:, at]).astype(bf16))
    other = jnp.concatenate(resids, axis=1)
    own = resid_ref[...]
    lines = chips * 2 * blocks
    for place, part in ((core, mine_ref[...].astype(f32)[:, : 2 * blocks]), (1 - core, swap_halves(got[:, : 2 * blocks], 1))):
        moment_ref[pl.ds(pl.multiple_of(place * lines, lines), lines), :] = part.reshape(lines, LANES)
    col = 1024
    turns = count // col
    products = [(n, r) for n in range(2) for r in range(blocks)]
    per = 2 * len(products) // turns
    coeff, delta = 0.0, None
    for i in range(turns):
        at = slice(i * col, (i + 1) * col)
        grad = grad_ref[:, at] + jnp.dot(other, kern_ref[:, at], preferred_element_type=f32)
        out_ref[:, at] = w_ref[:, at] - 2.0 * grad
        for n, r in products[i * per : (i + 1) * per]:
            moment = moment_ref[pl.ds(n * blocks + r, 2 * chips, stride=2 * blocks), :].astype(bf16)
            resid = (own, other)[n][:, r * LANES : (r + 1) * LANES]
            coeff += lax.dot_general(resid, moment, NT, preferred_element_type=f32)
        if (i + 1) * per == len(products):
            delta = 2.0 * lax.dot_general(
                coeff * damp_ref[...], eig_ref[...], NT, precision=lax.Precision.HIGHEST, preferred_element_type=f32
            )
    lane = lax.broadcasted_iota(jnp.int32, (outs, LANES), 1)
    for k in range(delta.shape[1]):
        at = slice(k * LANES, (k + 1) * LANES)
        out_ref[:, at] += jnp.where(lane == idx_ref[k] - k * LANES, delta[:, k : k + 1], 0.0)


def finish(core, nys_index, mine, got, pred, resid, grad, targets, damping, eigvecs, weights, kern):
    chips, _, lanes = mine.shape
    return pl.pallas_call(
        finish_kernel,
        in_specs=[SMEM] * 2 + [VMEM] * 10,
        out_specs=[VMEM, VMEM],
        out_shape=[jax.ShapeDtypeStruct(weights.shape, f32), jax.ShapeDtypeStruct(targets.shape, f32)],
        scratch_shapes=[
            pltpu.VMEM((chips * PACK, lanes), f32),
            pltpu.VMEM((2 * chips * 2 * kern.shape[0] // LANES, lanes), f32),
        ],
        compiler_params=pltpu.CompilerParams(vmem_limit_bytes=12 * MIB),
        name="finish",
    )(core, nys_index, mine, got, pred, resid, grad, targets, damping[None, :], eigvecs, weights, in_vmem(kern))


def swap(x, axis):
    return lax.ppermute(x, axis, [(0, 1), (1, 0)])


def exchange(x, axes):
    return lax.all_to_all(x, axes, split_axis=0, concat_axis=0, tiled=True)


def body(pool, batch_index, targets, centers, weights, nys_index, eigvecs, damping):
    total = targets.shape[1]
    core = lax.axis_index("core").astype(jnp.int32)
    groups = lax.axis_size(CENTERS)
    share = total // (2 * groups)
    place = jnp.stack([lax.axis_index(LOADER), core, lax.axis_index(CENTERS) * share]).astype(jnp.int32)
    keep, give = pick_rows(place, batch_index, pool, share)
    rows = keep + swap(give, "core")
    rows = exchange(repeat_sum(rows, swap(rows, "zh"), groups), CENTERS)
    w_half, cen_sq, head, *nys = prepare(nys_index, weights, eigvecs, centers)
    core = core[None]

    rows, cen_sq, w_half, head, nys = lax.optimization_barrier((rows, cen_sq, w_half, head, nys))
    own = rows.reshape(groups * share, D)
    other = swap(own, "core")

    kern_own, pred, held = kernel_values(w_half, centers, own, cen_sq, nys, head)
    moment, give = nystrom_terms(core, nys, own, other)
    kern_other, pred_give = kernel_values(w_half, held, other, cen_sq, (give, pred))
    packed = pack(moment, swap(give, "core"), pred, swap(pred_give, "core"))
    mine = exchange(sum_chips(exchange(packed, CHIPS)), CHIPS)
    got = swap(mine, "core")
    pred, resid, grad = own_grad(core, mine, targets, kern_own)
    return tuple(
        finish(core, nys_index, mine, got, pred, resid, grad, targets, damping, eigvecs, weights, kern_other)
    )


def solution(mesh):
    fine = Mesh(mesh.devices.reshape(2, 2, 4, 2, 4), ALL)
    return jax.shard_map(
        body,
        mesh=fine,
        in_specs=(
            P(LOADER, None),
            P(),
            P(),
            P(ALL, None),
            P(None, ALL),
            P(ALL),
            P(ALL, None),
            P(),
        ),
        out_specs=(P(None, ALL), P()),
        check_vma=False,
    )
```

```python
import functools
import math

import jax
import jax.numpy as jnp
from jax import lax
from jax.experimental import pallas as pl
from jax.experimental.pallas import tpu as pltpu
from jax.sharding import Mesh
from jax.sharding import PartitionSpec as P

f32, bf16 = jnp.float32, jnp.bfloat16
MIB = 2**20
LOADER = ("zh", "core")
CENTERS = ("y", "zl", "x")
ALL = LOADER + CENTERS
CHIPS = ("zh",) + CENTERS
PACK = 24
STEP = 2048
D = 256
LANES = 128
RATE = -4.0 / math.sqrt(D) * math.log2(math.e)
VMEM = pl.BlockSpec(memory_space=pltpu.VMEM)
SMEM = pl.BlockSpec(memory_space=pltpu.SMEM)
ANY = pl.BlockSpec(memory_space=pl.ANY)
HBM = pl.BlockSpec(memory_space=pltpu.HBM)
NT = (((1,), (1,)), ((), ()))


def in_hbm(x):
    return pltpu.with_memory_space_constraint(x, pltpu.HBM)


def in_vmem(x):
    return pltpu.with_memory_space_constraint(x, pltpu.VMEM)


def laplacian(dist_sq):
    safe = jnp.maximum(dist_sq, 1e-30)
    return jnp.exp2(safe * lax.rsqrt(safe) * RATE).astype(bf16)


def pick_kernel(place_ref, wanted_ref, pool_ref, keep_ref, give_ref, held_ref, row_ref, index_ref, sems, index_sem):
    share = keep_ref.shape[0]
    group = held_ref.shape[1]
    half = index_ref.shape[0] // 2
    mine, core, first = place_ref[0], place_ref[1], place_ref[2]
    rows = pool_ref.shape[0]
    listed = pltpu.make_async_copy(wanted_ref, index_ref, index_sem)
    listed.start()
    listed.wait()

    def local(n):
        of = jnp.where(n < share, core, 1 - core)
        return index_ref[of * half + first + jnp.where(n < share, n, n - share)] - mine * rows

    def copy(n, at):
        return pltpu.make_async_copy(pool_ref.at[pl.ds(pl.multiple_of(at, group), group), :], held_ref.at[n], sems.at[n])

    def owned(n, act):
        here = local(n)

        @pl.when(jnp.logical_and(here >= 0, here < rows))
        def _():
            act(jnp.clip(here, 0, rows - 1))

    def start(n, carry):
        owned(n, lambda here: copy(n, here - lax.rem(here, group)).start())
        return carry

    lax.fori_loop(0, 2 * share, start, 0, unroll=4)
    row_ref[...] = jnp.zeros_like(row_ref)
    line = lax.broadcasted_iota(jnp.int32, (group, D), 0)

    def select(n, carry):
        def take(here):
            copy(n, here - lax.rem(here, group)).wait()
            block = held_ref[n].astype(f32)
            row_ref[pl.ds(n, 1), :] = jnp.sum(jnp.where(line == lax.rem(here, group), block, 0.0), axis=0, keepdims=True)

        owned(n, take)
        return carry

    lax.fori_loop(0, 2 * share, select, 0, unroll=4)
    keep_ref[...] = row_ref[:share, :].astype(bf16)
    give_ref[...] = row_ref[share:, :].astype(bf16)


def pick_rows(place, batch_index, pool, share):
    group = 16
    return pl.pallas_call(
        pick_kernel,
        in_specs=[SMEM, HBM, HBM],
        out_specs=[VMEM, VMEM],
        out_shape=[jax.ShapeDtypeStruct((share, D), bf16)] * 2,
        scratch_shapes=[
            pltpu.VMEM((2 * share, group, D), bf16),
            pltpu.VMEM((2 * share, D), f32),
            pltpu.SMEM(batch_index.shape, jnp.int32),
            pltpu.SemaphoreType.DMA((2 * share,)),
            pltpu.SemaphoreType.DMA,
        ],
        compiler_params=pltpu.CompilerParams(vmem_limit_bytes=4 * MIB),
        name="pick_rows",
    )(place, in_hbm(batch_index), in_hbm(pool))


def repeat_kernel(keep_ref, got_ref, out_ref):
    out_ref[...] = jnp.broadcast_to((keep_ref[...] + got_ref[...])[None], out_ref.shape)


def repeat_sum(keep, got, times):
    return pl.pallas_call(
        repeat_kernel,
        in_specs=[VMEM, VMEM],
        out_specs=VMEM,
        out_shape=jax.ShapeDtypeStruct((times,) + keep.shape, bf16),
        compiler_params=pltpu.CompilerParams(vmem_limit_bytes=4 * MIB),
        name="repeat_sum",
    )(keep, got)


def row_norms(rows):
    wide = rows.astype(f32)
    square = wide * wide
    hi = square.astype(bf16)
    lo = (square - hi.astype(f32)).astype(bf16)
    ones = jnp.ones((8, rows.shape[1]), bf16)
    norms = lax.dot_general(ones, hi, NT, preferred_element_type=f32)
    norms += lax.dot_general(ones, lo, NT, preferred_element_type=f32)
    return norms[:1]


def prepare_kernel(
    idx_hbm, w_hbm, eig_hbm, cen_ref, w_half_ref, cen_sq_ref, head_ref, nys_ref, nys_sq_ref, hi_ref, lo_ref,
    held_ref, picked_ref, idx_ref, w_ref, eig_ref, sems, side_sems,
):
    steps, col, _ = held_ref.shape
    per = 8

    def fetch(i):
        return pltpu.make_async_copy(cen_ref.at[pl.ds(pl.multiple_of(i * col, col), col), :], held_ref.at[i], sems.at[i])

    side = [
        pltpu.make_async_copy(*refs, side_sems.at[n])
        for n, refs in enumerate(((idx_hbm, idx_ref), (eig_hbm, eig_ref), (w_hbm, w_ref)))
    ]
    side[0].start()
    fetch(0).start()
    fetch(1).start()
    side[1].start()
    side[2].start()
    side[0].wait()
    row = lax.broadcasted_iota(jnp.int32, (per, col), 0)
    lane = lax.broadcasted_iota(jnp.int32, (per, col), 1)

    def step(i, carry):
        fetch(i).wait()

        @pl.when(i + 2 < steps)
        def _():
            fetch(i + 2).start()

        rows = held_ref[i]
        cen_sq_ref[:, pl.ds(pl.multiple_of(i * col, col), col)] = row_norms(rows)
        spot = jnp.full((per, col), -1, jnp.int32)
        for g in range(per):
            spot = jnp.where(row == g, idx_ref[i * per + g] - i * col, spot)
        chosen = jnp.where(lane == spot, 1.0, 0.0).astype(bf16)
        at = pl.ds(pl.multiple_of(i * per, per), per)
        picked_ref[at, :] = jnp.dot(chosen, rows, preferred_element_type=f32)
        return carry

    lax.fori_loop(0, steps, step, 0, unroll=2)
    side[1].wait()
    for n in range(head_ref.shape[0] // col):
        head_ref[n * col : (n + 1) * col, :] = held_ref[n]
    eig_t = eig_ref[...].T
    hi = eig_t.astype(bf16)
    hi_ref[...] = hi
    lo_ref[...] = (eig_t - hi.astype(f32)).astype(bf16)
    side[2].wait()
    w_half_ref[...] = w_ref[...].astype(bf16)
    nys = picked_ref[...].astype(bf16)
    nys_ref[...] = nys
    nys_sq_ref[...] = row_norms(nys)


def prepare(nys_index, weights, eigvecs, centers):
    count, points, vectors = centers.shape[0], nys_index.shape[0], eigvecs.shape[1]
    col = count // points * 8
    shapes = [
        (weights.shape, bf16),
        ((1, count), f32),
        ((STEP, D), bf16),
        ((points, D), bf16),
        ((1, points), f32),
        ((vectors, points), bf16),
        ((vectors, points), bf16),
    ]
    return pl.pallas_call(
        prepare_kernel,
        in_specs=[HBM] * 4,
        out_specs=[VMEM] * len(shapes),
        out_shape=[pltpu.VMEM(*shape) if n == 2 else jax.ShapeDtypeStruct(*shape) for n, shape in enumerate(shapes)],
        scratch_shapes=[
            pltpu.VMEM((count // col, col, D), bf16),
            pltpu.VMEM((points, D), f32),
            pltpu.SMEM(nys_index.shape, jnp.int32),
            pltpu.VMEM(weights.shape, f32),
            pltpu.VMEM(eigvecs.shape, f32),
            pltpu.SemaphoreType.DMA((count // col,)),
            pltpu.SemaphoreType.DMA((3,)),
        ],
        compiler_params=pltpu.CompilerParams(vmem_limit_bytes=12 * MIB),
        cost_estimate=pl.CostEstimate(flops=4 * 10**9, bytes_accessed=2 * centers.size, transcendentals=0),
        name="prepare",
    )(in_hbm(nys_index), in_hbm(weights), in_hbm(eigvecs), in_hbm(centers))


def values_kernel(w_ref, batch_ref, cen_sq_ref, cen_ref, *refs, first):
    if first:
        kern_ref, pred_ref, held_ref, rows_ref, sq_ref, acc_ref, sems = refs[-7:]
    else:
        kern_ref, pred_ref, rows_ref, sq_ref, acc_ref = refs[-5:]
        held_ref = cen_ref
    batch, count = kern_ref.shape
    col, row, sub = STEP, 512, 256
    steps = count // col

    def fetch(i):
        at = pl.ds(pl.multiple_of(i * col, col), col)
        return pltpu.make_async_copy(cen_ref.at[at, :], held_ref.at[at, :], sems.at[i])

    if first:
        fetch(1).start()
        held_ref[:col, :] = refs[0][...]
    rows = batch_ref[...]
    wide = rows.astype(f32)
    rows_ref[...] = rows * (-2)
    sq_ref[...] = jnp.broadcast_to(jnp.sum(wide * wide, axis=1, keepdims=True), (batch, LANES))
    acc_ref[...] = jnp.zeros_like(acc_ref)

    def step(i, carry):
        if first:

            @pl.when(i > 0)
            def _():
                fetch(i).wait()

            @pl.when(jnp.logical_and(i > 0, i + 1 < steps))
            def _():
                fetch(i + 1).start()

        for j in range(batch // row):
            at = slice(j * row, (j + 1) * row)
            row_sq = jnp.concatenate([sq_ref[at, :]] * (sub // LANES), axis=1)
            acc = acc_ref[:, at]
            for n in range(col // sub):
                cols = pl.ds(pl.multiple_of(i * col + n * sub, sub), sub)
                cross = lax.dot_general(rows_ref[at, :], held_ref[cols, :], NT, preferred_element_type=f32)
                kern = laplacian((cross + row_sq) + cen_sq_ref[:, cols])
                kern_ref[at, cols] = kern
                acc += lax.dot_general(w_ref[:, cols], kern, NT, preferred_element_type=f32)
            acc_ref[:, at] = acc
        return carry

    lax.fori_loop(0, steps, step, 0)
    for r in range(batch // LANES):
        pred_ref[:, r, :] = acc_ref[:, r * LANES : (r + 1) * LANES]


def kernel_values(w_half, centers, batch, cen_sq, after, head=None):
    half, count, outs = batch.shape[0], centers.shape[0], w_half.shape[0]
    first = head is not None
    heads = [in_vmem(head)] if first else []
    held = [pltpu.VMEM(centers.shape, bf16)] if first else []
    return pl.pallas_call(
        functools.partial(values_kernel, first=first),
        in_specs=[VMEM] * 3 + [HBM if first else VMEM] + [VMEM] * len(heads) + [ANY] * len(after),
        out_specs=[VMEM] * (2 + len(held)),
        out_shape=[pltpu.VMEM((half, count), bf16), jax.ShapeDtypeStruct((outs, half // LANES, LANES), f32)] + held,
        scratch_shapes=[
            pltpu.VMEM((half, D), bf16),
            pltpu.VMEM((half, LANES), f32),
            pltpu.VMEM((outs, half), f32),
        ]
        + [pltpu.SemaphoreType.DMA((count // STEP,))] * len(held),
        compiler_params=pltpu.CompilerParams(vmem_limit_bytes=8 * MIB),
        cost_estimate=pl.CostEstimate(
            flops=8 * half * count * D, bytes_accessed=2 * half * count, transcendentals=2 * half * count
        ),
        name="kernel_values",
    )(w_half, batch, cen_sq, in_hbm(centers) if first else in_vmem(centers), *heads, *after)


def nystrom_kernel(core_ref, cen_ref, sq_ref, hi_ref, lo_ref, own_ref, other_ref, keep_ref, give_ref, acc_ref):
    cen = cen_ref[...]
    core = core_ref[0]
    half = own_ref.shape[0]
    count, blocks = hi_ref.shape[0], keep_ref.shape[1]
    for ref, first in ((own_ref, 0), (other_ref, half // LANES)):
        rows = ref[...]
        wide = rows.astype(f32)
        cross = lax.dot_general(rows * (-2), cen, NT, preferred_element_type=f32)
        kern = laplacian((cross + jnp.sum(wide * wide, axis=1, keepdims=True)) + sq_ref[...])
        part = lax.dot_general(hi_ref[...], kern, NT, preferred_element_type=f32)
        part += lax.dot_general(lo_ref[...], kern, NT, preferred_element_type=f32)
        for r in range(half // LANES):
            acc_ref[pl.ds(first + r, count, stride=blocks), :] = part[:, r * LANES : (r + 1) * LANES]
    lines = count // 2 * blocks
    for ref, place in ((keep_ref, core), (give_ref, 1 - core)):
        part = acc_ref[pl.ds(pl.multiple_of(place * lines, lines), lines), :]
        ref[...] = part.reshape(ref.shape).astype(bf16)


def nystrom_terms(core, nys, own, other):
    vectors, blocks = nys[2].shape[0], 2 * own.shape[0] // LANES
    return pl.pallas_call(
        nystrom_kernel,
        in_specs=[SMEM] + [VMEM] * 6,
        out_specs=[VMEM, VMEM],
        out_shape=[jax.ShapeDtypeStruct((vectors // 2, blocks, LANES), bf16)] * 2,
        scratch_shapes=[pltpu.VMEM((vectors * blocks, LANES), f32)],
        compiler_params=pltpu.CompilerParams(vmem_limit_bytes=12 * MIB),
        cost_estimate=pl.CostEstimate(flops=2 * 10**9, bytes_accessed=2**20, transcendentals=2**18),
        name="nystrom_terms",
    )(core, *nys, own, other)


def split3(x):
    hi = x.astype(bf16).astype(f32)
    mid = (x - hi).astype(bf16).astype(f32)
    return hi, mid, (x - hi) - mid


def swap_halves(x, axis):
    first, last = jnp.split(x, 2, axis)
    return jnp.concatenate([last, first], axis)


def pack_kernel(moment_ref, moment_in_ref, pred_ref, pred_in_ref, out_ref, acc_ref):
    vectors, blocks, _ = moment_ref.shape
    acc_ref[:, :blocks, :] = swap_halves(moment_in_ref[...].astype(f32), 1) + moment_ref[...].astype(f32)
    acc_ref[:, blocks:, :] = jnp.zeros((vectors, PACK - blocks, LANES), f32)
    pred = pred_ref[...] + pred_in_ref[...]
    parts = split3(pred)
    per = pred.shape[1] // 2
    for j in range(vectors):
        o, r = j // per, j % per * 2
        for n, part in enumerate(parts):
            acc_ref[j, blocks + 2 * n : blocks + 2 * n + 2, :] = part[o, r : r + 2, :]
    out_ref[...] = acc_ref[...].astype(bf16)


def pack(moment, moment_in, pred, pred_in):
    shape = (moment.shape[0], PACK, LANES)
    return pl.pallas_call(
        pack_kernel,
        in_specs=[VMEM] * 4,
        out_specs=VMEM,
        out_shape=jax.ShapeDtypeStruct(shape, bf16),
        scratch_shapes=[pltpu.VMEM(shape, f32)],
        compiler_params=pltpu.CompilerParams(vmem_limit_bytes=8 * MIB),
        name="pack",
    )(moment, moment_in, pred, pred_in)


def sum_kernel(part_ref, out_ref, acc_ref):
    blocks = 16
    acc_ref[...] = jnp.sum(part_ref[...].astype(f32), axis=0)
    pred = (acc_ref[blocks : blocks + 2, :] + acc_ref[blocks + 2 : blocks + 4, :]) + acc_ref[blocks + 4 : blocks + 6, :]
    for n, part in enumerate(split3(pred)):
        acc_ref[blocks + 2 * n : blocks + 2 * n + 2, :] = part
    out_ref[...] = jnp.broadcast_to(acc_ref[...].astype(bf16)[None], out_ref.shape)


def sum_chips(parts):
    return pl.pallas_call(
        sum_kernel,
        in_specs=[VMEM],
        out_specs=VMEM,
        out_shape=jax.ShapeDtypeStruct(parts.shape, bf16),
        scratch_shapes=[pltpu.VMEM(parts.shape[1:], f32)],
        compiler_params=pltpu.CompilerParams(vmem_limit_bytes=8 * MIB),
        name="sum_chips",
    )(parts)


def read_pred(sum_ref, r, outs, blocks):
    chips = sum_ref.shape[0] // PACK

    def part(n):
        line = r // 2 * PACK + blocks + r % 2 + 2 * n
        return sum_ref[pl.ds(line, outs, stride=chips // outs * PACK), :]

    return (part(0) + part(1)) + part(2)


def grad_kernel(core_ref, mine_ref, tgt_ref, kern_ref, pred_ref, resid_ref, grad_ref, sum_ref):
    half, count = kern_ref.shape
    blocks = half // LANES
    sum_ref[...] = mine_ref[...].astype(f32).reshape(sum_ref.shape)
    for r in range(blocks):
        at = slice(r * LANES, (r + 1) * LANES)
        pred = read_pred(sum_ref, r, tgt_ref.shape[0], 2 * blocks)
        pred_ref[:, at] = pred
        tgt = tgt_ref[:, pl.ds(pl.multiple_of(core_ref[0] * half + r * LANES, LANES), LANES)]
        resid_ref[:, at] = (pred - tgt).astype(bf16)
    resid = resid_ref[...]
    col = 1024
    for i in range(count // col):
        at = slice(i * col, (i + 1) * col)
        grad_ref[:, at] = jnp.dot(resid, kern_ref[:, at], preferred_element_type=f32)


def own_grad(core, mine, targets, kern):
    half, count = kern.shape
    outs = targets.shape[0]
    return pl.pallas_call(
        grad_kernel,
        in_specs=[SMEM] + [VMEM] * 3,
        out_specs=[VMEM] * 3,
        out_shape=[
            jax.ShapeDtypeStruct((outs, half), f32),
            jax.ShapeDtypeStruct((outs, half), bf16),
            jax.ShapeDtypeStruct((outs, count), f32),
        ],
        scratch_shapes=[pltpu.VMEM((mine.shape[0] * PACK, LANES), f32)],
        compiler_params=pltpu.CompilerParams(vmem_limit_bytes=8 * MIB),
        cost_estimate=pl.CostEstimate(flops=512 * half * count, bytes_accessed=2 * half * count, transcendentals=0),
        name="own_grad",
    )(core, mine, targets, in_vmem(kern))


def finish_kernel(
    core_ref, idx_ref, mine_ref, got_ref, pred_ref, resid_ref, grad_ref, tgt_ref, damp_ref, eig_ref, w_ref, kern_ref,
    out_ref, out_pred_ref, sum_ref, moment_ref, other_ref,
):
    half, count = kern_ref.shape
    core = core_ref[0]
    chips = mine_ref.shape[0]
    blocks = half // LANES
    outs = tgt_ref.shape[0]
    got = got_ref[...].astype(f32)
    sum_ref[...] = got.reshape(sum_ref.shape)
    out_pred_ref[:, pl.ds(pl.multiple_of(core * half, half), half)] = pred_ref[...]
    for r in range(blocks):
        at = pl.ds(pl.multiple_of((1 - core) * half + r * LANES, LANES), LANES)
        pred = read_pred(sum_ref, r, outs, 2 * blocks)
        out_pred_ref[:, at] = pred
        other_ref[:, r * LANES : (r + 1) * LANES] = (pred - tgt_ref[:, at]).astype(bf16)
    lines = chips * 2 * blocks
    for place, part in ((core, mine_ref[...].astype(f32)[:, : 2 * blocks]), (1 - core, swap_halves(got[:, : 2 * blocks], 1))):
        moment_ref[pl.ds(pl.multiple_of(place * lines, lines), lines), :] = part.reshape(lines, LANES)
    col = 2048

    def step(i, carry):
        at = pl.ds(pl.multiple_of(i * col, col), col)
        grad = grad_ref[:, at] + jnp.dot(other_ref[...], kern_ref[:, at], preferred_element_type=f32)
        out_ref[:, at] = w_ref[:, at] - 2.0 * grad
        return carry

    lax.fori_loop(0, count // col, step, 0)
    coeff = 0.0
    for n, ref in enumerate((resid_ref, other_ref)):
        for r in range(blocks):
            moment = moment_ref[pl.ds(n * blocks + r, 2 * chips, stride=2 * blocks), :].astype(bf16)
            at = slice(r * LANES, (r + 1) * LANES)
            coeff += lax.dot_general(ref[:, at], moment, NT, preferred_element_type=f32)
    delta = 2.0 * lax.dot_general(
        coeff * damp_ref[...], eig_ref[...], NT, precision=lax.Precision.HIGHEST, preferred_element_type=f32
    )
    lane = lax.broadcasted_iota(jnp.int32, (outs, LANES), 1)
    for k in range(delta.shape[1]):
        at = slice(k * LANES, (k + 1) * LANES)
        out_ref[:, at] += jnp.where(lane == idx_ref[k] - k * LANES, delta[:, k : k + 1], 0.0)


def finish(core, nys_index, mine, got, pred, resid, grad, targets, damping, eigvecs, weights, kern):
    chips, _, lanes = mine.shape
    return pl.pallas_call(
        finish_kernel,
        in_specs=[SMEM] * 2 + [VMEM] * 10,
        out_specs=[VMEM, VMEM],
        out_shape=[jax.ShapeDtypeStruct(weights.shape, f32), jax.ShapeDtypeStruct(targets.shape, f32)],
        scratch_shapes=[
            pltpu.VMEM((chips * PACK, lanes), f32),
            pltpu.VMEM((2 * chips * 2 * kern.shape[0] // LANES, lanes), f32),
            pltpu.VMEM(resid.shape, bf16),
        ],
        compiler_params=pltpu.CompilerParams(vmem_limit_bytes=12 * MIB),
        name="finish",
    )(core, nys_index, mine, got, pred, resid, grad, targets, damping[None, :], eigvecs, weights, in_vmem(kern))


def swap(x, axis):
    return lax.ppermute(x, axis, [(0, 1), (1, 0)])


def exchange(x, axes):
    return lax.all_to_all(x, axes, split_axis=0, concat_axis=0, tiled=True)


def body(pool, batch_index, targets, centers, weights, nys_index, eigvecs, damping):
    total = targets.shape[1]
    core = lax.axis_index("core").astype(jnp.int32)
    groups = lax.axis_size(CENTERS)
    share = total // (2 * groups)
    place = jnp.stack([lax.axis_index(LOADER), core, lax.axis_index(CENTERS) * share]).astype(jnp.int32)
    keep, give = pick_rows(place, batch_index, pool, share)
    rows = keep + swap(give, "core")
    rows = exchange(repeat_sum(rows, swap(rows, "zh"), groups), CENTERS)
    w_half, cen_sq, head, *nys = prepare(nys_index, weights, eigvecs, centers)
    core = core[None]

    rows, cen_sq, w_half, head, nys = lax.optimization_barrier((rows, cen_sq, w_half, head, nys))
    own = rows.reshape(groups * share, D)
    other = swap(own, "core")

    kern_own, pred, held = kernel_values(w_half, centers, own, cen_sq, nys, head)
    moment, give = nystrom_terms(core, nys, own, other)
    kern_other, pred_give = kernel_values(w_half, held, other, cen_sq, (give, pred))
    packed = pack(moment, swap(give, "core"), pred, swap(pred_give, "core"))
    mine = exchange(sum_chips(exchange(packed, CHIPS)), CHIPS)
    got = swap(mine, "core")
    pred, resid, grad = own_grad(core, mine, targets, kern_own)
    return tuple(
        finish(core, nys_index, mine, got, pred, resid, grad, targets, damping, eigvecs, weights, kern_other)
    )


def solution(mesh):
    fine = Mesh(mesh.devices.reshape(2, 2, 4, 2, 4), ALL)
    return jax.shard_map(
        body,
        mesh=fine,
        in_specs=(
            P(LOADER, None),
            P(),
            P(),
            P(ALL, None),
            P(None, ALL),
            P(ALL),
            P(ALL, None),
            P(),
        ),
        out_specs=(P(None, ALL), P()),
        check_vma=False,
    )
```

```python
import functools
import math

import jax
import jax.numpy as jnp
from jax import lax
from jax.experimental import pallas as pl
from jax.experimental.pallas import tpu as pltpu
from jax.sharding import Mesh
from jax.sharding import PartitionSpec as P

f32, bf16 = jnp.float32, jnp.bfloat16
MIB = 2**20
LOADER = ("zh", "core")
CENTERS = ("y", "zl", "x")
ALL = LOADER + CENTERS
CHIPS = ("zh",) + CENTERS
PACK = 24
STEP = 2048
D = 256
LANES = 128
RATE = -4.0 / math.sqrt(D) * math.log2(math.e)
VMEM = pl.BlockSpec(memory_space=pltpu.VMEM)
SMEM = pl.BlockSpec(memory_space=pltpu.SMEM)
ANY = pl.BlockSpec(memory_space=pl.ANY)
HBM = pl.BlockSpec(memory_space=pltpu.HBM)
NT = (((1,), (1,)), ((), ()))


def in_hbm(x):
    return pltpu.with_memory_space_constraint(x, pltpu.HBM)


def in_vmem(x):
    return pltpu.with_memory_space_constraint(x, pltpu.VMEM)


def laplacian(dist_sq):
    safe = jnp.maximum(dist_sq, 1e-30)
    return jnp.exp2(safe * lax.rsqrt(safe) * RATE).astype(bf16)


def pick_kernel(place_ref, wanted_ref, pool_ref, keep_ref, give_ref, held_ref, row_ref, index_ref, sems, index_sem):
    share = keep_ref.shape[0]
    group = held_ref.shape[1]
    half = index_ref.shape[0] // 2
    mine, core, first = place_ref[0], place_ref[1], place_ref[2]
    rows = pool_ref.shape[0]
    listed = pltpu.make_async_copy(wanted_ref, index_ref, index_sem)
    listed.start()
    listed.wait()

    def local(n):
        of = jnp.where(n < share, core, 1 - core)
        return index_ref[of * half + first + jnp.where(n < share, n, n - share)] - mine * rows

    def copy(n, at):
        return pltpu.make_async_copy(pool_ref.at[pl.ds(pl.multiple_of(at, group), group), :], held_ref.at[n], sems.at[n])

    def owned(n, act):
        here = local(n)

        @pl.when(jnp.logical_and(here >= 0, here < rows))
        def _():
            act(jnp.clip(here, 0, rows - 1))

    def start(n, carry):
        owned(n, lambda here: copy(n, here - lax.rem(here, group)).start())
        return carry

    lax.fori_loop(0, 2 * share, start, 0, unroll=4)
    row_ref[...] = jnp.zeros_like(row_ref)
    line = lax.broadcasted_iota(jnp.int32, (group, D), 0)

    def select(n, carry):
        def take(here):
            copy(n, here - lax.rem(here, group)).wait()
            block = held_ref[n].astype(f32)
            row_ref[pl.ds(n, 1), :] = jnp.sum(jnp.where(line == lax.rem(here, group), block, 0.0), axis=0, keepdims=True)

        owned(n, take)
        return carry

    lax.fori_loop(0, 2 * share, select, 0, unroll=4)
    keep_ref[...] = row_ref[:share, :].astype(bf16)
    give_ref[...] = row_ref[share:, :].astype(bf16)


def pick_rows(place, batch_index, pool, share):
    group = 16
    return pl.pallas_call(
        pick_kernel,
        in_specs=[SMEM, HBM, HBM],
        out_specs=[VMEM, VMEM],
        out_shape=[jax.ShapeDtypeStruct((share, D), bf16)] * 2,
        scratch_shapes=[
            pltpu.VMEM((2 * share, group, D), bf16),
            pltpu.VMEM((2 * share, D), f32),
            pltpu.SMEM(batch_index.shape, jnp.int32),
            pltpu.SemaphoreType.DMA((2 * share,)),
            pltpu.SemaphoreType.DMA,
        ],
        compiler_params=pltpu.CompilerParams(vmem_limit_bytes=4 * MIB),
        name="pick_rows",
    )(place, in_hbm(batch_index), in_hbm(pool))


def repeat_kernel(keep_ref, got_ref, out_ref):
    out_ref[...] = jnp.broadcast_to((keep_ref[...] + got_ref[...])[None], out_ref.shape)


def repeat_sum(keep, got, times):
    return pl.pallas_call(
        repeat_kernel,
        in_specs=[VMEM, VMEM],
        out_specs=VMEM,
        out_shape=jax.ShapeDtypeStruct((times,) + keep.shape, bf16),
        compiler_params=pltpu.CompilerParams(vmem_limit_bytes=4 * MIB),
        name="repeat_sum",
    )(keep, got)


def row_norms(rows):
    wide = rows.astype(f32)
    square = wide * wide
    hi = square.astype(bf16)
    lo = (square - hi.astype(f32)).astype(bf16)
    ones = jnp.ones((8, rows.shape[1]), bf16)
    norms = lax.dot_general(ones, hi, NT, preferred_element_type=f32)
    norms += lax.dot_general(ones, lo, NT, preferred_element_type=f32)
    return norms[:1]


def prepare_kernel(
    idx_hbm, w_hbm, eig_hbm, cen_ref, w_half_ref, cen_sq_ref, head_ref, nys_ref, nys_sq_ref, hi_ref, lo_ref,
    held_ref, picked_ref, idx_ref, w_ref, eig_ref, sems, side_sems,
):
    steps, col, _ = held_ref.shape
    per = 8

    def fetch(i):
        return pltpu.make_async_copy(cen_ref.at[pl.ds(pl.multiple_of(i * col, col), col), :], held_ref.at[i], sems.at[i])

    side = [
        pltpu.make_async_copy(*refs, side_sems.at[n])
        for n, refs in enumerate(((idx_hbm, idx_ref), (eig_hbm, eig_ref), (w_hbm, w_ref)))
    ]
    side[0].start()
    fetch(0).start()
    fetch(1).start()
    side[1].start()
    side[2].start()
    side[0].wait()
    row = lax.broadcasted_iota(jnp.int32, (per, col), 0)
    lane = lax.broadcasted_iota(jnp.int32, (per, col), 1)

    def step(i, carry):
        fetch(i).wait()

        @pl.when(i + 2 < steps)
        def _():
            fetch(i + 2).start()

        rows = held_ref[i]
        cen_sq_ref[:, pl.ds(pl.multiple_of(i * col, col), col)] = row_norms(rows)
        spot = jnp.full((per, col), -1, jnp.int32)
        for g in range(per):
            spot = jnp.where(row == g, idx_ref[i * per + g] - i * col, spot)
        chosen = jnp.where(lane == spot, 1.0, 0.0).astype(bf16)
        at = pl.ds(pl.multiple_of(i * per, per), per)
        picked_ref[at, :] = jnp.dot(chosen, rows, preferred_element_type=f32)
        return carry

    lax.fori_loop(0, steps, step, 0, unroll=2)
    side[1].wait()
    for n in range(head_ref.shape[0] // col):
        head_ref[n * col : (n + 1) * col, :] = held_ref[n]
    eig_t = eig_ref[...].T
    hi = eig_t.astype(bf16)
    hi_ref[...] = hi
    lo_ref[...] = (eig_t - hi.astype(f32)).astype(bf16)
    side[2].wait()
    w_half_ref[...] = w_ref[...].astype(bf16)
    nys = picked_ref[...].astype(bf16)
    nys_ref[...] = nys
    nys_sq_ref[...] = row_norms(nys)


def prepare(nys_index, weights, eigvecs, centers):
    count, points, vectors = centers.shape[0], nys_index.shape[0], eigvecs.shape[1]
    col = count // points * 8
    shapes = [
        (weights.shape, bf16),
        ((1, count), f32),
        ((STEP, D), bf16),
        ((points, D), bf16),
        ((1, points), f32),
        ((vectors, points), bf16),
        ((vectors, points), bf16),
    ]
    return pl.pallas_call(
        prepare_kernel,
        in_specs=[HBM] * 4,
        out_specs=[VMEM] * len(shapes),
        out_shape=[pltpu.VMEM(*shape) if n == 2 else jax.ShapeDtypeStruct(*shape) for n, shape in enumerate(shapes)],
        scratch_shapes=[
            pltpu.VMEM((count // col, col, D), bf16),
            pltpu.VMEM((points, D), f32),
            pltpu.SMEM(nys_index.shape, jnp.int32),
            pltpu.VMEM(weights.shape, f32),
            pltpu.VMEM(eigvecs.shape, f32),
            pltpu.SemaphoreType.DMA((count // col,)),
            pltpu.SemaphoreType.DMA((3,)),
        ],
        compiler_params=pltpu.CompilerParams(vmem_limit_bytes=12 * MIB),
        cost_estimate=pl.CostEstimate(flops=4 * 10**9, bytes_accessed=2 * centers.size, transcendentals=0),
        name="prepare",
    )(in_hbm(nys_index), in_hbm(weights), in_hbm(eigvecs), in_hbm(centers))


def values_kernel(w_ref, batch_ref, cen_sq_ref, cen_ref, *refs, first, start, joined):
    if first:
        kern_ref, pred_ref, held_ref, rows_ref, sq_ref, acc_ref, sems = refs[-7:]
    else:
        kern_ref, pred_ref, rows_ref, sq_ref, acc_ref = refs[-5:]
        held_ref = cen_ref
    batch, count = kern_ref.shape
    col, row, sub = STEP, 512, 256
    steps = count // col

    def fetch(i):
        at = pl.ds(pl.multiple_of(i * col, col), col)
        return pltpu.make_async_copy(cen_ref.at[at, :], held_ref.at[at, :], sems.at[i])

    if first:
        fetch(1).start()
        held_ref[:col, :] = refs[0][...]
    rows = batch_ref[start : start + batch, :]
    wide = rows.astype(f32)
    rows_ref[...] = rows * (-2)
    sq_ref[...] = jnp.broadcast_to(jnp.sum(wide * wide, axis=1, keepdims=True), (batch, LANES))
    acc_ref[...] = jnp.zeros_like(acc_ref)

    def step(i, carry):
        if first:

            @pl.when(i > 0)
            def _():
                fetch(i).wait()

            @pl.when(jnp.logical_and(i > 0, i + 1 < steps))
            def _():
                fetch(i + 1).start()

        for j in range(batch // row):
            at = slice(j * row, (j + 1) * row)
            row_sq = jnp.concatenate([sq_ref[at, :]] * (sub // LANES), axis=1)
            acc = acc_ref[:, at]
            for n in range(col // sub):
                cols = pl.ds(pl.multiple_of(i * col + n * sub, sub), sub)
                cross = lax.dot_general(rows_ref[at, :], held_ref[cols, :], NT, preferred_element_type=f32)
                kern = laplacian((cross + row_sq) + cen_sq_ref[:, cols])
                kern_ref[at, cols] = kern
                acc += lax.dot_general(w_ref[:, cols], kern, NT, preferred_element_type=f32)
            acc_ref[:, at] = acc
        return carry

    lax.fori_loop(0, steps, step, 0)
    before = 0
    if joined:
        before = refs[0].shape[1]
        for r in range(before):
            pred_ref[:, r, :] = refs[0][:, r, :]
    for r in range(batch // LANES):
        pred_ref[:, before + r, :] = acc_ref[:, r * LANES : (r + 1) * LANES]


def kernel_values(w_half, centers, batch, cen_sq, after, rows, head=None, joined=None):
    half, count, outs = rows[1] - rows[0], centers.shape[0], w_half.shape[0]
    blocks = half // LANES + (0 if joined is None else joined.shape[1])
    first = head is not None
    heads = [in_vmem(head)] if first else []
    heads += [] if joined is None else [joined]
    held = [pltpu.VMEM(centers.shape, bf16)] if first else []
    return pl.pallas_call(
        functools.partial(values_kernel, first=first, start=rows[0], joined=joined is not None),
        in_specs=[VMEM] * 3 + [HBM if first else VMEM] + [VMEM] * len(heads) + [ANY] * len(after),
        out_specs=[VMEM] * (2 + len(held)),
        out_shape=[pltpu.VMEM((half, count), bf16), jax.ShapeDtypeStruct((outs, blocks, LANES), f32)] + held,
        scratch_shapes=[
            pltpu.VMEM((half, D), bf16),
            pltpu.VMEM((half, LANES), f32),
            pltpu.VMEM((outs, half), f32),
        ]
        + [pltpu.SemaphoreType.DMA((count // STEP,))] * len(held),
        compiler_params=pltpu.CompilerParams(vmem_limit_bytes=8 * MIB),
        cost_estimate=pl.CostEstimate(
            flops=8 * half * count * D, bytes_accessed=2 * half * count, transcendentals=2 * half * count
        ),
        name="kernel_values",
    )(w_half, batch, cen_sq, in_hbm(centers) if first else in_vmem(centers), *heads, *after)


def nystrom_kernel(core_ref, cen_ref, sq_ref, hi_ref, lo_ref, own_ref, other_ref, keep_ref, give_ref, acc_ref):
    cen = cen_ref[...]
    core = core_ref[0]
    half = own_ref.shape[0]
    count, blocks = hi_ref.shape[0], keep_ref.shape[1]
    for ref, first in ((own_ref, 0), (other_ref, half // LANES)):
        rows = ref[...]
        wide = rows.astype(f32)
        cross = lax.dot_general(rows * (-2), cen, NT, preferred_element_type=f32)
        kern = laplacian((cross + jnp.sum(wide * wide, axis=1, keepdims=True)) + sq_ref[...])
        part = lax.dot_general(hi_ref[...], kern, NT, preferred_element_type=f32)
        part += lax.dot_general(lo_ref[...], kern, NT, preferred_element_type=f32)
        for r in range(half // LANES):
            acc_ref[pl.ds(first + r, count, stride=blocks), :] = part[:, r * LANES : (r + 1) * LANES]
    lines = count // 2 * blocks
    for ref, place in ((keep_ref, core), (give_ref, 1 - core)):
        part = acc_ref[pl.ds(pl.multiple_of(place * lines, lines), lines), :]
        ref[...] = part.reshape(ref.shape).astype(bf16)


def nystrom_terms(core, nys, own, other):
    vectors, blocks = nys[2].shape[0], 2 * own.shape[0] // LANES
    return pl.pallas_call(
        nystrom_kernel,
        in_specs=[SMEM] + [VMEM] * 6,
        out_specs=[VMEM, VMEM],
        out_shape=[jax.ShapeDtypeStruct((vectors // 2, blocks, LANES), bf16)] * 2,
        scratch_shapes=[pltpu.VMEM((vectors * blocks, LANES), f32)],
        compiler_params=pltpu.CompilerParams(vmem_limit_bytes=12 * MIB),
        cost_estimate=pl.CostEstimate(flops=2 * 10**9, bytes_accessed=2**20, transcendentals=2**18),
        name="nystrom_terms",
    )(core, *nys, own, other)


def split3(x):
    hi = x.astype(bf16).astype(f32)
    mid = (x - hi).astype(bf16).astype(f32)
    return hi, mid, (x - hi) - mid


def swap_halves(x, axis):
    first, last = jnp.split(x, 2, axis)
    return jnp.concatenate([last, first], axis)


def pack_kernel(moment_ref, moment_in_ref, pred_ref, pred_in_ref, out_ref, acc_ref):
    vectors, blocks, _ = moment_ref.shape
    acc_ref[:, :blocks, :] = swap_halves(moment_in_ref[...].astype(f32), 1) + moment_ref[...].astype(f32)
    acc_ref[:, blocks:, :] = jnp.zeros((vectors, PACK - blocks, LANES), f32)
    pred = pred_ref[...] + pred_in_ref[...]
    parts = split3(pred)
    per = pred.shape[1] // 2
    for j in range(vectors):
        o, r = j // per, j % per * 2
        for n, part in enumerate(parts):
            acc_ref[j, blocks + 2 * n : blocks + 2 * n + 2, :] = part[o, r : r + 2, :]
    out_ref[...] = acc_ref[...].astype(bf16)


def pack(moment, moment_in, pred, pred_in):
    shape = (moment.shape[0], PACK, LANES)
    return pl.pallas_call(
        pack_kernel,
        in_specs=[VMEM] * 4,
        out_specs=VMEM,
        out_shape=jax.ShapeDtypeStruct(shape, bf16),
        scratch_shapes=[pltpu.VMEM(shape, f32)],
        compiler_params=pltpu.CompilerParams(vmem_limit_bytes=8 * MIB),
        name="pack",
    )(moment, moment_in, pred, pred_in)


def sum_kernel(part_ref, out_ref, acc_ref):
    blocks = 16
    acc_ref[...] = jnp.sum(part_ref[...].astype(f32), axis=0)
    pred = (acc_ref[blocks : blocks + 2, :] + acc_ref[blocks + 2 : blocks + 4, :]) + acc_ref[blocks + 4 : blocks + 6, :]
    for n, part in enumerate(split3(pred)):
        acc_ref[blocks + 2 * n : blocks + 2 * n + 2, :] = part
    out_ref[...] = jnp.broadcast_to(acc_ref[...].astype(bf16)[None], out_ref.shape)


def sum_chips(parts):
    return pl.pallas_call(
        sum_kernel,
        in_specs=[VMEM],
        out_specs=VMEM,
        out_shape=jax.ShapeDtypeStruct(parts.shape, bf16),
        scratch_shapes=[pltpu.VMEM(parts.shape[1:], f32)],
        compiler_params=pltpu.CompilerParams(vmem_limit_bytes=8 * MIB),
        name="sum_chips",
    )(parts)


def read_pred(sum_ref, r, outs, blocks):
    chips = sum_ref.shape[0] // PACK

    def part(n):
        line = r // 2 * PACK + blocks + r % 2 + 2 * n
        return sum_ref[pl.ds(line, outs, stride=chips // outs * PACK), :]

    return (part(0) + part(1)) + part(2)


def grad_kernel(core_ref, mine_ref, tgt_ref, kern_ref, last_ref, pred_ref, resid_ref, grad_ref, sum_ref):
    part, count = kern_ref.shape
    half = part + last_ref.shape[0]
    blocks = half // LANES
    sum_ref[...] = mine_ref[...].astype(f32).reshape(sum_ref.shape)
    for r in range(blocks):
        at = slice(r * LANES, (r + 1) * LANES)
        pred = read_pred(sum_ref, r, tgt_ref.shape[0], 2 * blocks)
        pred_ref[:, at] = pred
        tgt = tgt_ref[:, pl.ds(pl.multiple_of(core_ref[0] * half + r * LANES, LANES), LANES)]
        resid_ref[:, at] = (pred - tgt).astype(bf16)
    resid = resid_ref[...]
    col = 1024
    for i in range(count // col):
        at = slice(i * col, (i + 1) * col)
        grad = jnp.dot(resid[:, :part], kern_ref[:, at], preferred_element_type=f32)
        grad_ref[:, at] = grad + jnp.dot(resid[:, part:], last_ref[:, at], preferred_element_type=f32)


def own_grad(core, mine, targets, kern, last):
    half, count = kern.shape[0] + last.shape[0], kern.shape[1]
    outs = targets.shape[0]
    return pl.pallas_call(
        grad_kernel,
        in_specs=[SMEM] + [VMEM] * 4,
        out_specs=[VMEM] * 3,
        out_shape=[
            jax.ShapeDtypeStruct((outs, half), f32),
            jax.ShapeDtypeStruct((outs, half), bf16),
            jax.ShapeDtypeStruct((outs, count), f32),
        ],
        scratch_shapes=[pltpu.VMEM((mine.shape[0] * PACK, LANES), f32)],
        compiler_params=pltpu.CompilerParams(vmem_limit_bytes=8 * MIB),
        cost_estimate=pl.CostEstimate(flops=512 * half * count, bytes_accessed=2 * half * count, transcendentals=0),
        name="own_grad",
    )(core, mine, targets, in_vmem(kern), in_vmem(last))


def finish_kernel(
    core_ref, idx_ref, mine_ref, got_ref, pred_ref, resid_ref, grad_ref, tgt_ref, damp_ref, eig_ref, w_ref, kern_ref,
    out_ref, out_pred_ref, sum_ref, moment_ref,
):
    half, count = kern_ref.shape
    core = core_ref[0]
    chips = mine_ref.shape[0]
    blocks = half // LANES
    outs = tgt_ref.shape[0]
    got = got_ref[...].astype(f32)
    sum_ref[...] = got.reshape(sum_ref.shape)
    out_pred_ref[:, pl.ds(pl.multiple_of(core * half, half), half)] = pred_ref[...]
    resids = []
    for r in range(blocks):
        at = pl.ds(pl.multiple_of((1 - core) * half + r * LANES, LANES), LANES)
        pred = read_pred(sum_ref, r, outs, 2 * blocks)
        out_pred_ref[:, at] = pred
        resids.append((pred - tgt_ref[:, at]).astype(bf16))
    other = jnp.concatenate(resids, axis=1)
    own = resid_ref[...]
    lines = chips * 2 * blocks
    for place, part in ((core, mine_ref[...].astype(f32)[:, : 2 * blocks]), (1 - core, swap_halves(got[:, : 2 * blocks], 1))):
        moment_ref[pl.ds(pl.multiple_of(place * lines, lines), lines), :] = part.reshape(lines, LANES)
    col = 1024
    turns = count // col
    products = [(n, r) for n in range(2) for r in range(blocks)]
    per = 2 * len(products) // turns
    coeff, delta = 0.0, None
    for i in range(turns):
        at = slice(i * col, (i + 1) * col)
        grad = grad_ref[:, at] + jnp.dot(other, kern_ref[:, at], preferred_element_type=f32)
        out_ref[:, at] = w_ref[:, at] - 2.0 * grad
        for n, r in products[i * per : (i + 1) * per]:
            moment = moment_ref[pl.ds(n * blocks + r, 2 * chips, stride=2 * blocks), :].astype(bf16)
            resid = (own, other)[n][:, r * LANES : (r + 1) * LANES]
            coeff += lax.dot_general(resid, moment, NT, preferred_element_type=f32)
        if (i + 1) * per == len(products):
            delta = 2.0 * lax.dot_general(
                coeff * damp_ref[...], eig_ref[...], NT, precision=lax.Precision.HIGHEST, preferred_element_type=f32
            )
    lane = lax.broadcasted_iota(jnp.int32, (outs, LANES), 1)
    for k in range(delta.shape[1]):
        at = slice(k * LANES, (k + 1) * LANES)
        out_ref[:, at] += jnp.where(lane == idx_ref[k] - k * LANES, delta[:, k : k + 1], 0.0)


def finish(core, nys_index, mine, got, pred, resid, grad, targets, damping, eigvecs, weights, kern):
    chips, _, lanes = mine.shape
    return pl.pallas_call(
        finish_kernel,
        in_specs=[SMEM] * 2 + [VMEM] * 10,
        out_specs=[VMEM, VMEM],
        out_shape=[jax.ShapeDtypeStruct(weights.shape, f32), jax.ShapeDtypeStruct(targets.shape, f32)],
        scratch_shapes=[
            pltpu.VMEM((chips * PACK, lanes), f32),
            pltpu.VMEM((2 * chips * 2 * kern.shape[0] // LANES, lanes), f32),
        ],
        compiler_params=pltpu.CompilerParams(vmem_limit_bytes=12 * MIB),
        name="finish",
    )(core, nys_index, mine, got, pred, resid, grad, targets, damping[None, :], eigvecs, weights, in_vmem(kern))


def swap(x, axis):
    return lax.ppermute(x, axis, [(0, 1), (1, 0)])


def exchange(x, axes):
    return lax.all_to_all(x, axes, split_axis=0, concat_axis=0, tiled=True)


def body(pool, batch_index, targets, centers, weights, nys_index, eigvecs, damping):
    total = targets.shape[1]
    core = lax.axis_index("core").astype(jnp.int32)
    groups = lax.axis_size(CENTERS)
    share = total // (2 * groups)
    place = jnp.stack([lax.axis_index(LOADER), core, lax.axis_index(CENTERS) * share]).astype(jnp.int32)
    keep, give = pick_rows(place, batch_index, pool, share)
    rows = keep + swap(give, "core")
    rows = exchange(repeat_sum(rows, swap(rows, "zh"), groups), CENTERS)
    w_half, cen_sq, head, *nys = prepare(nys_index, weights, eigvecs, centers)
    core = core[None]

    rows, cen_sq, w_half, head, nys = lax.optimization_barrier((rows, cen_sq, w_half, head, nys))
    own = rows.reshape(groups * share, D)
    other = swap(own, "core")

    half = total // 2
    kern_first, pred, held = kernel_values(w_half, centers, own, cen_sq, nys, (0, half // 2), head)
    moment, give = nystrom_terms(core, nys, own, other)
    kern_other, pred_give = kernel_values(w_half, held, other, cen_sq, (give, pred), (0, half))
    kern_last, pred = kernel_values(w_half, held, own, cen_sq, (pred_give,), (half // 2, half), None, pred)
    packed = pack(moment, swap(give, "core"), pred, swap(pred_give, "core"))
    mine = exchange(sum_chips(exchange(packed, CHIPS)), CHIPS)
    got = swap(mine, "core")
    pred, resid, grad = own_grad(core, mine, targets, kern_first, kern_last)
    return tuple(
        finish(core, nys_index, mine, got, pred, resid, grad, targets, damping, eigvecs, weights, kern_other)
    )


def solution(mesh):
    fine = Mesh(mesh.devices.reshape(2, 2, 4, 2, 4), ALL)
    return jax.shard_map(
        body,
        mesh=fine,
        in_specs=(
            P(LOADER, None),
            P(),
            P(),
            P(ALL, None),
            P(None, ALL),
            P(ALL),
            P(ALL, None),
            P(),
        ),
        out_specs=(P(None, ALL), P()),
        check_vma=False,
    )
```

```python
import functools
import math

import jax
import jax.numpy as jnp
from jax import lax
from jax.experimental import pallas as pl
from jax.experimental.pallas import tpu as pltpu
from jax.sharding import Mesh
from jax.sharding import PartitionSpec as P

f32, bf16 = jnp.float32, jnp.bfloat16
MIB = 2**20
LOADER = ("zh", "core")
CENTERS = ("y", "zl", "x")
ALL = LOADER + CENTERS
CHIPS = ("zh",) + CENTERS
PACK = 24
STEP = 2048
D = 256
LANES = 128
RATE = -4.0 / math.sqrt(D) * math.log2(math.e)
VMEM = pl.BlockSpec(memory_space=pltpu.VMEM)
SMEM = pl.BlockSpec(memory_space=pltpu.SMEM)
ANY = pl.BlockSpec(memory_space=pl.ANY)
HBM = pl.BlockSpec(memory_space=pltpu.HBM)
NT = (((1,), (1,)), ((), ()))


def in_hbm(x):
    return pltpu.with_memory_space_constraint(x, pltpu.HBM)


def in_vmem(x):
    return pltpu.with_memory_space_constraint(x, pltpu.VMEM)


def laplacian(dist_sq):
    safe = jnp.maximum(dist_sq, 1e-30)
    return jnp.exp2(safe * lax.rsqrt(safe) * RATE).astype(bf16)


def pick_kernel(place_ref, wanted_ref, pool_ref, keep_ref, give_ref, held_ref, row_ref, index_ref, sems, index_sem):
    share = keep_ref.shape[0]
    group = held_ref.shape[1]
    half = index_ref.shape[0] // 2
    mine, core, first = place_ref[0], place_ref[1], place_ref[2]
    rows = pool_ref.shape[0]
    listed = pltpu.make_async_copy(wanted_ref, index_ref, index_sem)
    listed.start()
    listed.wait()

    def local(n):
        of = jnp.where(n < share, core, 1 - core)
        spot = jnp.where(n < share, n, n - share)
        spot = jnp.where(spot < share // 2, spot, spot - share // 2 + half // 2)
        return index_ref[of * half + first + spot] - mine * rows

    def copy(n, at):
        return pltpu.make_async_copy(pool_ref.at[pl.ds(pl.multiple_of(at, group), group), :], held_ref.at[n], sems.at[n])

    def owned(n, act):
        here = local(n)

        @pl.when(jnp.logical_and(here >= 0, here < rows))
        def _():
            act(jnp.clip(here, 0, rows - 1))

    def start(n, carry):
        owned(n, lambda here: copy(n, here - lax.rem(here, group)).start())
        return carry

    lax.fori_loop(0, 2 * share, start, 0, unroll=4)
    row_ref[...] = jnp.zeros_like(row_ref)
    line = lax.broadcasted_iota(jnp.int32, (group, D), 0)

    def select(n, carry):
        def take(here):
            copy(n, here - lax.rem(here, group)).wait()
            block = held_ref[n].astype(f32)
            row_ref[pl.ds(n, 1), :] = jnp.sum(jnp.where(line == lax.rem(here, group), block, 0.0), axis=0, keepdims=True)

        owned(n, take)
        return carry

    lax.fori_loop(0, 2 * share, select, 0, unroll=4)
    keep_ref[...] = row_ref[:share, :].astype(bf16)
    give_ref[...] = row_ref[share:, :].astype(bf16)


def pick_rows(place, batch_index, pool, share):
    group = 16
    return pl.pallas_call(
        pick_kernel,
        in_specs=[SMEM, HBM, HBM],
        out_specs=[VMEM, VMEM],
        out_shape=[jax.ShapeDtypeStruct((share, D), bf16)] * 2,
        scratch_shapes=[
            pltpu.VMEM((2 * share, group, D), bf16),
            pltpu.VMEM((2 * share, D), f32),
            pltpu.SMEM(batch_index.shape, jnp.int32),
            pltpu.SemaphoreType.DMA((2 * share,)),
            pltpu.SemaphoreType.DMA,
        ],
        compiler_params=pltpu.CompilerParams(vmem_limit_bytes=4 * MIB),
        name="pick_rows",
    )(place, in_hbm(batch_index), in_hbm(pool))


def repeat_kernel(keep_ref, got_ref, out_ref):
    out_ref[...] = jnp.broadcast_to((keep_ref[...] + got_ref[...])[None], out_ref.shape)


def repeat_sum(keep, got, times):
    return pl.pallas_call(
        repeat_kernel,
        in_specs=[VMEM, VMEM],
        out_specs=VMEM,
        out_shape=jax.ShapeDtypeStruct((times,) + keep.shape, bf16),
        compiler_params=pltpu.CompilerParams(vmem_limit_bytes=4 * MIB),
        name="repeat_sum",
    )(keep, got)


def row_norms(rows):
    wide = rows.astype(f32)
    square = wide * wide
    hi = square.astype(bf16)
    lo = (square - hi.astype(f32)).astype(bf16)
    ones = jnp.ones((8, rows.shape[1]), bf16)
    norms = lax.dot_general(ones, hi, NT, preferred_element_type=f32)
    norms += lax.dot_general(ones, lo, NT, preferred_element_type=f32)
    return norms[:1]


def prepare_kernel(
    idx_hbm, w_hbm, eig_hbm, cen_ref, w_half_ref, cen_sq_ref, head_ref, nys_ref, nys_sq_ref, hi_ref, lo_ref,
    held_ref, picked_ref, idx_ref, w_ref, eig_ref, sems, side_sems,
):
    steps, col, _ = held_ref.shape
    per = 8

    def fetch(i):
        return pltpu.make_async_copy(cen_ref.at[pl.ds(pl.multiple_of(i * col, col), col), :], held_ref.at[i], sems.at[i])

    side = [
        pltpu.make_async_copy(*refs, side_sems.at[n])
        for n, refs in enumerate(((idx_hbm, idx_ref), (eig_hbm, eig_ref), (w_hbm, w_ref)))
    ]
    side[0].start()
    fetch(0).start()
    fetch(1).start()
    side[1].start()
    side[2].start()
    side[0].wait()
    row = lax.broadcasted_iota(jnp.int32, (per, col), 0)
    lane = lax.broadcasted_iota(jnp.int32, (per, col), 1)

    def step(i, carry):
        fetch(i).wait()

        @pl.when(i + 2 < steps)
        def _():
            fetch(i + 2).start()

        rows = held_ref[i]
        cen_sq_ref[:, pl.ds(pl.multiple_of(i * col, col), col)] = row_norms(rows)
        spot = jnp.full((per, col), -1, jnp.int32)
        for g in range(per):
            spot = jnp.where(row == g, idx_ref[i * per + g] - i * col, spot)
        chosen = jnp.where(lane == spot, 1.0, 0.0).astype(bf16)
        at = pl.ds(pl.multiple_of(i * per, per), per)
        picked_ref[at, :] = jnp.dot(chosen, rows, preferred_element_type=f32)
        return carry

    lax.fori_loop(0, steps, step, 0, unroll=2)
    side[1].wait()
    for n in range(head_ref.shape[0] // col):
        head_ref[n * col : (n + 1) * col, :] = held_ref[n]
    eig_t = eig_ref[...].T
    hi = eig_t.astype(bf16)
    hi_ref[...] = hi
    lo_ref[...] = (eig_t - hi.astype(f32)).astype(bf16)
    side[2].wait()
    w_half_ref[...] = w_ref[...].astype(bf16)
    nys = picked_ref[...].astype(bf16)
    nys_ref[...] = nys
    nys_sq_ref[...] = row_norms(nys)


def prepare(nys_index, weights, eigvecs, centers):
    count, points, vectors = centers.shape[0], nys_index.shape[0], eigvecs.shape[1]
    col = count // points * 8
    shapes = [
        (weights.shape, bf16),
        ((1, count), f32),
        ((STEP, D), bf16),
        ((points, D), bf16),
        ((1, points), f32),
        ((vectors, points), bf16),
        ((vectors, points), bf16),
    ]
    return pl.pallas_call(
        prepare_kernel,
        in_specs=[HBM] * 4,
        out_specs=[VMEM] * len(shapes),
        out_shape=[pltpu.VMEM(*shape) if n == 2 else jax.ShapeDtypeStruct(*shape) for n, shape in enumerate(shapes)],
        scratch_shapes=[
            pltpu.VMEM((count // col, col, D), bf16),
            pltpu.VMEM((points, D), f32),
            pltpu.SMEM(nys_index.shape, jnp.int32),
            pltpu.VMEM(weights.shape, f32),
            pltpu.VMEM(eigvecs.shape, f32),
            pltpu.SemaphoreType.DMA((count // col,)),
            pltpu.SemaphoreType.DMA((3,)),
        ],
        compiler_params=pltpu.CompilerParams(vmem_limit_bytes=12 * MIB),
        cost_estimate=pl.CostEstimate(flops=4 * 10**9, bytes_accessed=2 * centers.size, transcendentals=0),
        name="prepare",
    )(in_hbm(nys_index), in_hbm(weights), in_hbm(eigvecs), in_hbm(centers))


def values_kernel(w_ref, batch_ref, cen_sq_ref, cen_ref, *refs, first):
    if first:
        kern_ref, pred_ref, held_ref, rows_ref, sq_ref, acc_ref, sems = refs[-7:]
    else:
        kern_ref, pred_ref, rows_ref, sq_ref, acc_ref = refs[-5:]
        held_ref = cen_ref
    batch, count = kern_ref.shape
    col, row, sub = STEP, 512, 256
    steps = count // col

    def fetch(i):
        at = pl.ds(pl.multiple_of(i * col, col), col)
        return pltpu.make_async_copy(cen_ref.at[at, :], held_ref.at[at, :], sems.at[i])

    if first:
        fetch(1).start()
        held_ref[:col, :] = refs[0][...]
    rows = batch_ref[...]
    wide = rows.astype(f32)
    rows_ref[...] = rows * (-2)
    sq_ref[...] = jnp.broadcast_to(jnp.sum(wide * wide, axis=1, keepdims=True), (batch, LANES))
    acc_ref[...] = jnp.zeros_like(acc_ref)

    def step(i, carry):
        if first:

            @pl.when(i > 0)
            def _():
                fetch(i).wait()

            @pl.when(jnp.logical_and(i > 0, i + 1 < steps))
            def _():
                fetch(i + 1).start()

        for j in range(batch // row):
            at = slice(j * row, (j + 1) * row)
            row_sq = jnp.concatenate([sq_ref[at, :]] * (sub // LANES), axis=1)
            acc = acc_ref[:, at]
            for n in range(col // sub):
                cols = pl.ds(pl.multiple_of(i * col + n * sub, sub), sub)
                cross = lax.dot_general(rows_ref[at, :], held_ref[cols, :], NT, preferred_element_type=f32)
                kern = laplacian((cross + row_sq) + cen_sq_ref[:, cols])
                kern_ref[at, cols] = kern
                acc += lax.dot_general(w_ref[:, cols], kern, NT, preferred_element_type=f32)
            acc_ref[:, at] = acc
        return carry

    lax.fori_loop(0, steps, step, 0)
    for r in range(batch // LANES):
        pred_ref[:, r, :] = acc_ref[:, r * LANES : (r + 1) * LANES]


def kernel_values(w_half, centers, batch, cen_sq, after, head=None):
    half, count, outs = batch.shape[0], centers.shape[0], w_half.shape[0]
    first = head is not None
    heads = [in_vmem(head)] if first else []
    held = [pltpu.VMEM(centers.shape, bf16)] if first else []
    return pl.pallas_call(
        functools.partial(values_kernel, first=first),
        in_specs=[VMEM] * 3 + [HBM if first else VMEM] + [VMEM] * len(heads) + [ANY] * len(after),
        out_specs=[VMEM] * (2 + len(held)),
        out_shape=[pltpu.VMEM((half, count), bf16), jax.ShapeDtypeStruct((outs, half // LANES, LANES), f32)] + held,
        scratch_shapes=[
            pltpu.VMEM((half, D), bf16),
            pltpu.VMEM((half, LANES), f32),
            pltpu.VMEM((outs, half), f32),
        ]
        + [pltpu.SemaphoreType.DMA((count // STEP,))] * len(held),
        compiler_params=pltpu.CompilerParams(vmem_limit_bytes=8 * MIB),
        cost_estimate=pl.CostEstimate(
            flops=8 * half * count * D, bytes_accessed=2 * half * count, transcendentals=2 * half * count
        ),
        name="kernel_values",
    )(w_half, batch, cen_sq, in_hbm(centers) if first else in_vmem(centers), *heads, *after)


def nystrom_kernel(core_ref, cen_ref, sq_ref, hi_ref, lo_ref, own_ref, other_ref, keep_ref, give_ref, acc_ref):
    cen = cen_ref[...]
    core = core_ref[0]
    half = own_ref.shape[0]
    count, blocks = hi_ref.shape[0], keep_ref.shape[1]
    for ref, first in ((own_ref, 0), (other_ref, half // LANES)):
        rows = ref[...]
        wide = rows.astype(f32)
        cross = lax.dot_general(rows * (-2), cen, NT, preferred_element_type=f32)
        kern = laplacian((cross + jnp.sum(wide * wide, axis=1, keepdims=True)) + sq_ref[...])
        part = lax.dot_general(hi_ref[...], kern, NT, preferred_element_type=f32)
        part += lax.dot_general(lo_ref[...], kern, NT, preferred_element_type=f32)
        for r in range(half // LANES):
            acc_ref[pl.ds(first + r, count, stride=blocks), :] = part[:, r * LANES : (r + 1) * LANES]
    lines = count // 2 * blocks
    for ref, place in ((keep_ref, core), (give_ref, 1 - core)):
        part = acc_ref[pl.ds(pl.multiple_of(place * lines, lines), lines), :]
        ref[...] = part.reshape(ref.shape).astype(bf16)


def nystrom_terms(core, nys, own, other):
    vectors, blocks = nys[2].shape[0], 2 * own.shape[0] // LANES
    return pl.pallas_call(
        nystrom_kernel,
        in_specs=[SMEM] + [VMEM] * 6,
        out_specs=[VMEM, VMEM],
        out_shape=[jax.ShapeDtypeStruct((vectors // 2, blocks, LANES), bf16)] * 2,
        scratch_shapes=[pltpu.VMEM((vectors * blocks, LANES), f32)],
        compiler_params=pltpu.CompilerParams(vmem_limit_bytes=12 * MIB),
        cost_estimate=pl.CostEstimate(flops=2 * 10**9, bytes_accessed=2**20, transcendentals=2**18),
        name="nystrom_terms",
    )(core, *nys, own, other)


def split3(x):
    hi = x.astype(bf16).astype(f32)
    mid = (x - hi).astype(bf16).astype(f32)
    return hi, mid, (x - hi) - mid


def swap_halves(x, axis):
    first, last = jnp.split(x, 2, axis)
    return jnp.concatenate([last, first], axis)


def pack_kernel(moment_ref, moment_in_ref, pred_ref, pred_in_ref, out_ref, acc_ref):
    vectors, blocks, _ = moment_ref.shape
    acc_ref[:, :blocks, :] = swap_halves(moment_in_ref[...].astype(f32), 1) + moment_ref[...].astype(f32)
    acc_ref[:, blocks:, :] = jnp.zeros((vectors, PACK - blocks, LANES), f32)
    pred = pred_ref[...] + pred_in_ref[...]
    parts = split3(pred)
    per = pred.shape[1] // 2
    for j in range(vectors):
        o, r = j // per, j % per * 2
        for n, part in enumerate(parts):
            acc_ref[j, blocks + 2 * n : blocks + 2 * n + 2, :] = part[o, r : r + 2, :]
    out_ref[...] = acc_ref[...].astype(bf16)


def pack(moment, moment_in, pred, pred_in):
    shape = (moment.shape[0], PACK, LANES)
    return pl.pallas_call(
        pack_kernel,
        in_specs=[VMEM] * 4,
        out_specs=VMEM,
        out_shape=jax.ShapeDtypeStruct(shape, bf16),
        scratch_shapes=[pltpu.VMEM(shape, f32)],
        compiler_params=pltpu.CompilerParams(vmem_limit_bytes=8 * MIB),
        name="pack",
    )(moment, moment_in, pred, pred_in)


def sum_kernel(part_ref, out_ref, acc_ref):
    blocks = 16
    acc_ref[...] = jnp.sum(part_ref[...].astype(f32), axis=0)
    pred = (acc_ref[blocks : blocks + 2, :] + acc_ref[blocks + 2 : blocks + 4, :]) + acc_ref[blocks + 4 : blocks + 6, :]
    for n, part in enumerate(split3(pred)):
        acc_ref[blocks + 2 * n : blocks + 2 * n + 2, :] = part
    out_ref[...] = jnp.broadcast_to(acc_ref[...].astype(bf16)[None], out_ref.shape)


def sum_chips(parts):
    return pl.pallas_call(
        sum_kernel,
        in_specs=[VMEM],
        out_specs=VMEM,
        out_shape=jax.ShapeDtypeStruct(parts.shape, bf16),
        scratch_shapes=[pltpu.VMEM(parts.shape[1:], f32)],
        compiler_params=pltpu.CompilerParams(vmem_limit_bytes=8 * MIB),
        name="sum_chips",
    )(parts)


def read_pred(sum_ref, r, outs, blocks):
    chips = sum_ref.shape[0] // PACK

    def part(n):
        line = r // 2 * PACK + blocks + r % 2 + 2 * n
        return sum_ref[pl.ds(line, outs, stride=chips // outs * PACK), :]

    return (part(0) + part(1)) + part(2)


def grad_kernel(core_ref, mine_ref, tgt_ref, kern_ref, pred_ref, resid_ref, grad_ref, sum_ref):
    half, count = kern_ref.shape
    blocks = half // LANES
    sum_ref[...] = mine_ref[...].astype(f32).reshape(sum_ref.shape)
    for r in range(blocks):
        at = slice(r * LANES, (r + 1) * LANES)
        pred = read_pred(sum_ref, r, tgt_ref.shape[0], 2 * blocks)
        pred_ref[:, at] = pred
        tgt = tgt_ref[:, pl.ds(pl.multiple_of(core_ref[0] * half + r * LANES, LANES), LANES)]
        resid_ref[:, at] = (pred - tgt).astype(bf16)
    resid = resid_ref[...]
    col = 1024
    for i in range(count // col):
        at = slice(i * col, (i + 1) * col)
        grad_ref[:, at] = jnp.dot(resid, kern_ref[:, at], preferred_element_type=f32)


def own_grad(core, mine, targets, kern):
    half, count = kern.shape
    outs = targets.shape[0]
    return pl.pallas_call(
        grad_kernel,
        in_specs=[SMEM] + [VMEM] * 3,
        out_specs=[VMEM] * 3,
        out_shape=[
            jax.ShapeDtypeStruct((outs, half), f32),
            jax.ShapeDtypeStruct((outs, half), bf16),
            jax.ShapeDtypeStruct((outs, count), f32),
        ],
        scratch_shapes=[pltpu.VMEM((mine.shape[0] * PACK, LANES), f32)],
        compiler_params=pltpu.CompilerParams(vmem_limit_bytes=8 * MIB),
        cost_estimate=pl.CostEstimate(flops=512 * half * count, bytes_accessed=2 * half * count, transcendentals=0),
        name="own_grad",
    )(core, mine, targets, in_vmem(kern))


def finish_kernel(
    core_ref, idx_ref, mine_ref, got_ref, pred_ref, resid_ref, grad_ref, tgt_ref, damp_ref, eig_ref, w_ref, kern_ref,
    out_ref, out_pred_ref, sum_ref, moment_ref,
):
    half, count = kern_ref.shape
    core = core_ref[0]
    chips = mine_ref.shape[0]
    blocks = half // LANES
    outs = tgt_ref.shape[0]
    got = got_ref[...].astype(f32)
    sum_ref[...] = got.reshape(sum_ref.shape)
    out_pred_ref[:, pl.ds(pl.multiple_of(core * half, half), half)] = pred_ref[...]
    resids = []
    for r in range(blocks):
        at = pl.ds(pl.multiple_of((1 - core) * half + r * LANES, LANES), LANES)
        pred = read_pred(sum_ref, r, outs, 2 * blocks)
        out_pred_ref[:, at] = pred
        resids.append((pred - tgt_ref[:, at]).astype(bf16))
    other = jnp.concatenate(resids, axis=1)
    own = resid_ref[...]
    lines = chips * 2 * blocks
    for place, part in ((core, mine_ref[...].astype(f32)[:, : 2 * blocks]), (1 - core, swap_halves(got[:, : 2 * blocks], 1))):
        moment_ref[pl.ds(pl.multiple_of(place * lines, lines), lines), :] = part.reshape(lines, LANES)
    col = 1024
    turns = count // col
    products = [(n, r) for n in range(2) for r in range(blocks)]
    per = 2 * len(products) // turns
    coeff, delta = 0.0, None
    for i in range(turns):
        at = slice(i * col, (i + 1) * col)
        grad = grad_ref[:, at] + jnp.dot(other, kern_ref[:, at], preferred_element_type=f32)
        out_ref[:, at] = w_ref[:, at] - 2.0 * grad
        for n, r in products[i * per : (i + 1) * per]:
            moment = moment_ref[pl.ds(n * blocks + r, 2 * chips, stride=2 * blocks), :].astype(bf16)
            resid = (own, other)[n][:, r * LANES : (r + 1) * LANES]
            coeff += lax.dot_general(resid, moment, NT, preferred_element_type=f32)
        if (i + 1) * per == len(products):
            delta = 2.0 * lax.dot_general(
                coeff * damp_ref[...], eig_ref[...], NT, precision=lax.Precision.HIGHEST, preferred_element_type=f32
            )
    lane = lax.broadcasted_iota(jnp.int32, (outs, LANES), 1)
    for k in range(delta.shape[1]):
        at = slice(k * LANES, (k + 1) * LANES)
        out_ref[:, at] += jnp.where(lane == idx_ref[k] - k * LANES, delta[:, k : k + 1], 0.0)


def finish(core, nys_index, mine, got, pred, resid, grad, targets, damping, eigvecs, weights, kern):
    chips, _, lanes = mine.shape
    return pl.pallas_call(
        finish_kernel,
        in_specs=[SMEM] * 2 + [VMEM] * 10,
        out_specs=[VMEM, VMEM],
        out_shape=[jax.ShapeDtypeStruct(weights.shape, f32), jax.ShapeDtypeStruct(targets.shape, f32)],
        scratch_shapes=[
            pltpu.VMEM((chips * PACK, lanes), f32),
            pltpu.VMEM((2 * chips * 2 * kern.shape[0] // LANES, lanes), f32),
        ],
        compiler_params=pltpu.CompilerParams(vmem_limit_bytes=12 * MIB),
        name="finish",
    )(core, nys_index, mine, got, pred, resid, grad, targets, damping[None, :], eigvecs, weights, in_vmem(kern))


def swap(x, axis):
    return lax.ppermute(x, axis, [(0, 1), (1, 0)])


def exchange(x, axes):
    return lax.all_to_all(x, axes, split_axis=0, concat_axis=0, tiled=True)


def body(pool, batch_index, targets, centers, weights, nys_index, eigvecs, damping):
    total = targets.shape[1]
    core = lax.axis_index("core").astype(jnp.int32)
    groups = lax.axis_size(CENTERS)
    share = total // (2 * groups)
    place = jnp.stack([lax.axis_index(LOADER), core, lax.axis_index(CENTERS) * (share // 2)]).astype(jnp.int32)
    keep, give = pick_rows(place, batch_index, pool, share)
    rows = keep + swap(give, "core")
    z = lax.axis_index("zh")
    mine = lax.dynamic_slice_in_dim(rows, z * (share // 2), share // 2)
    theirs = lax.dynamic_slice_in_dim(rows, (1 - z) * (share // 2), share // 2)
    rows = exchange(repeat_sum(mine, swap(theirs, "zh"), lax.axis_size(CHIPS)), CHIPS)
    w_half, cen_sq, head, *nys = prepare(nys_index, weights, eigvecs, centers)
    core = core[None]

    rows, cen_sq, w_half, head, nys = lax.optimization_barrier((rows, cen_sq, w_half, head, nys))
    own = rows.reshape(groups * share, D)
    other = swap(own, "core")

    kern_own, pred, held = kernel_values(w_half, centers, own, cen_sq, nys, head)
    moment, give = nystrom_terms(core, nys, own, other)
    kern_other, pred_give = kernel_values(w_half, held, other, cen_sq, (give, pred))
    packed = pack(moment, swap(give, "core"), pred, swap(pred_give, "core"))
    mine = exchange(sum_chips(exchange(packed, CHIPS)), CHIPS)
    got = swap(mine, "core")
    pred, resid, grad = own_grad(core, mine, targets, kern_own)
    return tuple(
        finish(core, nys_index, mine, got, pred, resid, grad, targets, damping, eigvecs, weights, kern_other)
    )


def solution(mesh):
    fine = Mesh(mesh.devices.reshape(2, 2, 4, 2, 4), ALL)
    return jax.shard_map(
        body,
        mesh=fine,
        in_specs=(
            P(LOADER, None),
            P(),
            P(),
            P(ALL, None),
            P(None, ALL),
            P(ALL),
            P(ALL, None),
            P(),
        ),
        out_specs=(P(None, ALL), P()),
        check_vma=False,
    )
```

```python
import functools
import math

import jax
import jax.numpy as jnp
from jax import lax
from jax.experimental import pallas as pl
from jax.experimental.pallas import tpu as pltpu
from jax.sharding import Mesh
from jax.sharding import PartitionSpec as P

f32, bf16 = jnp.float32, jnp.bfloat16
MIB = 2**20
LOADER = ("zh", "core")
CENTERS = ("y", "zl", "x")
PLANE = ("y", "x")
ALL = LOADER + CENTERS
CHIPS = ("zh",) + CENTERS
PACK = 24
STEP = 2048
D = 256
LANES = 128
RATE = -4.0 / math.sqrt(D) * math.log2(math.e)
VMEM = pl.BlockSpec(memory_space=pltpu.VMEM)
SMEM = pl.BlockSpec(memory_space=pltpu.SMEM)
ANY = pl.BlockSpec(memory_space=pl.ANY)
HBM = pl.BlockSpec(memory_space=pltpu.HBM)
NT = (((1,), (1,)), ((), ()))


def in_hbm(x):
    return pltpu.with_memory_space_constraint(x, pltpu.HBM)


def in_vmem(x):
    return pltpu.with_memory_space_constraint(x, pltpu.VMEM)


def laplacian(dist_sq):
    safe = jnp.maximum(dist_sq, 1e-30)
    return jnp.exp2(safe * lax.rsqrt(safe) * RATE).astype(bf16)


def pick_kernel(place_ref, wanted_ref, pool_ref, keep_ref, give_ref, held_ref, row_ref, index_ref, sems, index_sem):
    share = keep_ref.shape[0]
    group = held_ref.shape[1]
    half = index_ref.shape[0] // 2
    mine, core, first = place_ref[0], place_ref[1], place_ref[2]
    rows = pool_ref.shape[0]
    listed = pltpu.make_async_copy(wanted_ref, index_ref, index_sem)
    listed.start()
    listed.wait()

    def local(n):
        of = jnp.where(n < share, core, 1 - core)
        return index_ref[of * half + first + jnp.where(n < share, n, n - share)] - mine * rows

    def copy(n, at):
        return pltpu.make_async_copy(pool_ref.at[pl.ds(pl.multiple_of(at, group), group), :], held_ref.at[n], sems.at[n])

    def owned(n, act):
        here = local(n)

        @pl.when(jnp.logical_and(here >= 0, here < rows))
        def _():
            act(jnp.clip(here, 0, rows - 1))

    def start(n, carry):
        owned(n, lambda here: copy(n, here - lax.rem(here, group)).start())
        return carry

    lax.fori_loop(0, 2 * share, start, 0, unroll=4)
    row_ref[...] = jnp.zeros_like(row_ref)
    line = lax.broadcasted_iota(jnp.int32, (group, D), 0)

    def select(n, carry):
        def take(here):
            copy(n, here - lax.rem(here, group)).wait()
            block = held_ref[n].astype(f32)
            row_ref[pl.ds(n, 1), :] = jnp.sum(jnp.where(line == lax.rem(here, group), block, 0.0), axis=0, keepdims=True)

        owned(n, take)
        return carry

    lax.fori_loop(0, 2 * share, select, 0, unroll=4)
    keep_ref[...] = row_ref[:share, :].astype(bf16)
    give_ref[...] = row_ref[share:, :].astype(bf16)


def pick_rows(place, batch_index, pool, share):
    group = 16
    return pl.pallas_call(
        pick_kernel,
        in_specs=[SMEM, HBM, HBM],
        out_specs=[VMEM, VMEM],
        out_shape=[jax.ShapeDtypeStruct((share, D), bf16)] * 2,
        scratch_shapes=[
            pltpu.VMEM((2 * share, group, D), bf16),
            pltpu.VMEM((2 * share, D), f32),
            pltpu.SMEM(batch_index.shape, jnp.int32),
            pltpu.SemaphoreType.DMA((2 * share,)),
            pltpu.SemaphoreType.DMA,
        ],
        compiler_params=pltpu.CompilerParams(vmem_limit_bytes=4 * MIB),
        name="pick_rows",
    )(place, in_hbm(batch_index), in_hbm(pool))


def repeat_kernel(z_ref, mine_ref, far_ref, near_ref, across_ref, out_ref):
    share = mine_ref.shape[0]
    for place, refs in ((z_ref[0], (mine_ref, far_ref)), (1 - z_ref[0], (near_ref, across_ref))):
        at = pl.ds(pl.multiple_of(place * share, share), share)
        rows = refs[0][...] + refs[1][...]
        out_ref[:, at, :] = jnp.broadcast_to(rows[None], (out_ref.shape[0],) + rows.shape)


def repeat_sum(z, parts, times):
    share, width = parts[0].shape
    return pl.pallas_call(
        repeat_kernel,
        in_specs=[SMEM] + [VMEM] * 4,
        out_specs=VMEM,
        out_shape=jax.ShapeDtypeStruct((times, 2 * share, width), bf16),
        compiler_params=pltpu.CompilerParams(vmem_limit_bytes=4 * MIB),
        name="repeat_sum",
    )(z, *parts)


def row_norms(rows):
    wide = rows.astype(f32)
    square = wide * wide
    hi = square.astype(bf16)
    lo = (square - hi.astype(f32)).astype(bf16)
    ones = jnp.ones((8, rows.shape[1]), bf16)
    norms = lax.dot_general(ones, hi, NT, preferred_element_type=f32)
    norms += lax.dot_general(ones, lo, NT, preferred_element_type=f32)
    return norms[:1]


def prepare_kernel(
    idx_hbm, w_hbm, eig_hbm, cen_ref, w_half_ref, cen_sq_ref, head_ref, nys_ref, nys_sq_ref, hi_ref, lo_ref,
    held_ref, picked_ref, idx_ref, w_ref, eig_ref, sems, side_sems,
):
    steps, col, _ = held_ref.shape
    per = 8

    def fetch(i):
        return pltpu.make_async_copy(cen_ref.at[pl.ds(pl.multiple_of(i * col, col), col), :], held_ref.at[i], sems.at[i])

    side = [
        pltpu.make_async_copy(*refs, side_sems.at[n])
        for n, refs in enumerate(((idx_hbm, idx_ref), (eig_hbm, eig_ref), (w_hbm, w_ref)))
    ]
    side[0].start()
    fetch(0).start()
    fetch(1).start()
    side[1].start()
    side[2].start()
    side[0].wait()
    row = lax.broadcasted_iota(jnp.int32, (per, col), 0)
    lane = lax.broadcasted_iota(jnp.int32, (per, col), 1)

    def step(i, carry):
        fetch(i).wait()

        @pl.when(i + 2 < steps)
        def _():
            fetch(i + 2).start()

        rows = held_ref[i]
        cen_sq_ref[:, pl.ds(pl.multiple_of(i * col, col), col)] = row_norms(rows)
        spot = jnp.full((per, col), -1, jnp.int32)
        for g in range(per):
            spot = jnp.where(row == g, idx_ref[i * per + g] - i * col, spot)
        chosen = jnp.where(lane == spot, 1.0, 0.0).astype(bf16)
        at = pl.ds(pl.multiple_of(i * per, per), per)
        picked_ref[at, :] = jnp.dot(chosen, rows, preferred_element_type=f32)
        return carry

    lax.fori_loop(0, steps, step, 0, unroll=2)
    side[1].wait()
    for n in range(head_ref.shape[0] // col):
        head_ref[n * col : (n + 1) * col, :] = held_ref[n]
    eig_t = eig_ref[...].T
    hi = eig_t.astype(bf16)
    hi_ref[...] = hi
    lo_ref[...] = (eig_t - hi.astype(f32)).astype(bf16)
    side[2].wait()
    w_half_ref[...] = w_ref[...].astype(bf16)
    nys = picked_ref[...].astype(bf16)
    nys_ref[...] = nys
    nys_sq_ref[...] = row_norms(nys)


def prepare(nys_index, weights, eigvecs, centers):
    count, points, vectors = centers.shape[0], nys_index.shape[0], eigvecs.shape[1]
    col = count // points * 8
    shapes = [
        (weights.shape, bf16),
        ((1, count), f32),
        ((STEP, D), bf16),
        ((points, D), bf16),
        ((1, points), f32),
        ((vectors, points), bf16),
        ((vectors, points), bf16),
    ]
    return pl.pallas_call(
        prepare_kernel,
        in_specs=[HBM] * 4,
        out_specs=[VMEM] * len(shapes),
        out_shape=[pltpu.VMEM(*shape) if n == 2 else jax.ShapeDtypeStruct(*shape) for n, shape in enumerate(shapes)],
        scratch_shapes=[
            pltpu.VMEM((count // col, col, D), bf16),
            pltpu.VMEM((points, D), f32),
            pltpu.SMEM(nys_index.shape, jnp.int32),
            pltpu.VMEM(weights.shape, f32),
            pltpu.VMEM(eigvecs.shape, f32),
            pltpu.SemaphoreType.DMA((count // col,)),
            pltpu.SemaphoreType.DMA((3,)),
        ],
        compiler_params=pltpu.CompilerParams(vmem_limit_bytes=12 * MIB),
        cost_estimate=pl.CostEstimate(flops=4 * 10**9, bytes_accessed=2 * centers.size, transcendentals=0),
        name="prepare",
    )(in_hbm(nys_index), in_hbm(weights), in_hbm(eigvecs), in_hbm(centers))


def values_kernel(w_ref, batch_ref, cen_sq_ref, cen_ref, *refs, first):
    if first:
        kern_ref, pred_ref, held_ref, rows_ref, sq_ref, acc_ref, sems = refs[-7:]
    else:
        kern_ref, pred_ref, rows_ref, sq_ref, acc_ref = refs[-5:]
        held_ref = cen_ref
    batch, count = kern_ref.shape
    col, row, sub = STEP, 512, 256
    steps = count // col

    def fetch(i):
        at = pl.ds(pl.multiple_of(i * col, col), col)
        return pltpu.make_async_copy(cen_ref.at[at, :], held_ref.at[at, :], sems.at[i])

    if first:
        fetch(1).start()
        held_ref[:col, :] = refs[0][...]
    rows = batch_ref[...]
    wide = rows.astype(f32)
    rows_ref[...] = rows * (-2)
    sq_ref[...] = jnp.broadcast_to(jnp.sum(wide * wide, axis=1, keepdims=True), (batch, LANES))
    acc_ref[...] = jnp.zeros_like(acc_ref)

    def step(i, carry):
        if first:

            @pl.when(i > 0)
            def _():
                fetch(i).wait()

            @pl.when(jnp.logical_and(i > 0, i + 1 < steps))
            def _():
                fetch(i + 1).start()

        for j in range(batch // row):
            at = slice(j * row, (j + 1) * row)
            row_sq = jnp.concatenate([sq_ref[at, :]] * (sub // LANES), axis=1)
            acc = acc_ref[:, at]
            for n in range(col // sub):
                cols = pl.ds(pl.multiple_of(i * col + n * sub, sub), sub)
                cross = lax.dot_general(rows_ref[at, :], held_ref[cols, :], NT, preferred_element_type=f32)
                kern = laplacian((cross + row_sq) + cen_sq_ref[:, cols])
                kern_ref[at, cols] = kern
                acc += lax.dot_general(w_ref[:, cols], kern, NT, preferred_element_type=f32)
            acc_ref[:, at] = acc
        return carry

    lax.fori_loop(0, steps, step, 0)
    for r in range(batch // LANES):
        pred_ref[:, r, :] = acc_ref[:, r * LANES : (r + 1) * LANES]


def kernel_values(w_half, centers, batch, cen_sq, after, head=None):
    half, count, outs = batch.shape[0], centers.shape[0], w_half.shape[0]
    first = head is not None
    heads = [in_vmem(head)] if first else []
    held = [pltpu.VMEM(centers.shape, bf16)] if first else []
    return pl.pallas_call(
        functools.partial(values_kernel, first=first),
        in_specs=[VMEM] * 3 + [HBM if first else VMEM] + [VMEM] * len(heads) + [ANY] * len(after),
        out_specs=[VMEM] * (2 + len(held)),
        out_shape=[pltpu.VMEM((half, count), bf16), jax.ShapeDtypeStruct((outs, half // LANES, LANES), f32)] + held,
        scratch_shapes=[
            pltpu.VMEM((half, D), bf16),
            pltpu.VMEM((half, LANES), f32),
            pltpu.VMEM((outs, half), f32),
        ]
        + [pltpu.SemaphoreType.DMA((count // STEP,))] * len(held),
        compiler_params=pltpu.CompilerParams(vmem_limit_bytes=8 * MIB),
        cost_estimate=pl.CostEstimate(
            flops=8 * half * count * D, bytes_accessed=2 * half * count, transcendentals=2 * half * count
        ),
        name="kernel_values",
    )(w_half, batch, cen_sq, in_hbm(centers) if first else in_vmem(centers), *heads, *after)


def nystrom_kernel(core_ref, cen_ref, sq_ref, hi_ref, lo_ref, own_ref, other_ref, keep_ref, give_ref, acc_ref):
    cen = cen_ref[...]
    core = core_ref[0]
    half = own_ref.shape[0]
    count, blocks = hi_ref.shape[0], keep_ref.shape[1]
    for ref, first in ((own_ref, 0), (other_ref, half // LANES)):
        rows = ref[...]
        wide = rows.astype(f32)
        cross = lax.dot_general(rows * (-2), cen, NT, preferred_element_type=f32)
        kern = laplacian((cross + jnp.sum(wide * wide, axis=1, keepdims=True)) + sq_ref[...])
        part = lax.dot_general(hi_ref[...], kern, NT, preferred_element_type=f32)
        part += lax.dot_general(lo_ref[...], kern, NT, preferred_element_type=f32)
        for r in range(half // LANES):
            acc_ref[pl.ds(first + r, count, stride=blocks), :] = part[:, r * LANES : (r + 1) * LANES]
    lines = count // 2 * blocks
    for ref, place in ((keep_ref, core), (give_ref, 1 - core)):
        part = acc_ref[pl.ds(pl.multiple_of(place * lines, lines), lines), :]
        ref[...] = part.reshape(ref.shape).astype(bf16)


def nystrom_terms(core, nys, own, other):
    vectors, blocks = nys[2].shape[0], 2 * own.shape[0] // LANES
    return pl.pallas_call(
        nystrom_kernel,
        in_specs=[SMEM] + [VMEM] * 6,
        out_specs=[VMEM, VMEM],
        out_shape=[jax.ShapeDtypeStruct((vectors // 2, blocks, LANES), bf16)] * 2,
        scratch_shapes=[pltpu.VMEM((vectors * blocks, LANES), f32)],
        compiler_params=pltpu.CompilerParams(vmem_limit_bytes=12 * MIB),
        cost_estimate=pl.CostEstimate(flops=2 * 10**9, bytes_accessed=2**20, transcendentals=2**18),
        name="nystrom_terms",
    )(core, *nys, own, other)


def split3(x):
    hi = x.astype(bf16).astype(f32)
    mid = (x - hi).astype(bf16).astype(f32)
    return hi, mid, (x - hi) - mid


def swap_halves(x, axis):
    first, last = jnp.split(x, 2, axis)
    return jnp.concatenate([last, first], axis)


def pack_kernel(moment_ref, moment_in_ref, pred_ref, pred_in_ref, out_ref, acc_ref):
    vectors, blocks, _ = moment_ref.shape
    acc_ref[:, :blocks, :] = swap_halves(moment_in_ref[...].astype(f32), 1) + moment_ref[...].astype(f32)
    acc_ref[:, blocks:, :] = jnp.zeros((vectors, PACK - blocks, LANES), f32)
    pred = pred_ref[...] + pred_in_ref[...]
    parts = split3(pred)
    per = pred.shape[1] // 2
    for j in range(vectors):
        o, r = j // per, j % per * 2
        for n, part in enumerate(parts):
            acc_ref[j, blocks + 2 * n : blocks + 2 * n + 2, :] = part[o, r : r + 2, :]
    out_ref[...] = acc_ref[...].astype(bf16)


def pack(moment, moment_in, pred, pred_in):
    shape = (moment.shape[0], PACK, LANES)
    return pl.pallas_call(
        pack_kernel,
        in_specs=[VMEM] * 4,
        out_specs=VMEM,
        out_shape=jax.ShapeDtypeStruct(shape, bf16),
        scratch_shapes=[pltpu.VMEM(shape, f32)],
        compiler_params=pltpu.CompilerParams(vmem_limit_bytes=8 * MIB),
        name="pack",
    )(moment, moment_in, pred, pred_in)


def sum_kernel(part_ref, out_ref, acc_ref):
    blocks = 16
    acc_ref[...] = jnp.sum(part_ref[...].astype(f32), axis=0)
    pred = (acc_ref[blocks : blocks + 2, :] + acc_ref[blocks + 2 : blocks + 4, :]) + acc_ref[blocks + 4 : blocks + 6, :]
    for n, part in enumerate(split3(pred)):
        acc_ref[blocks + 2 * n : blocks + 2 * n + 2, :] = part
    out_ref[...] = jnp.broadcast_to(acc_ref[...].astype(bf16)[None], out_ref.shape)


def sum_chips(parts):
    return pl.pallas_call(
        sum_kernel,
        in_specs=[VMEM],
        out_specs=VMEM,
        out_shape=jax.ShapeDtypeStruct(parts.shape, bf16),
        scratch_shapes=[pltpu.VMEM(parts.shape[1:], f32)],
        compiler_params=pltpu.CompilerParams(vmem_limit_bytes=8 * MIB),
        name="sum_chips",
    )(parts)


def read_pred(sum_ref, r, outs, blocks):
    chips = sum_ref.shape[0] // PACK

    def part(n):
        line = r // 2 * PACK + blocks + r % 2 + 2 * n
        return sum_ref[pl.ds(line, outs, stride=chips // outs * PACK), :]

    return (part(0) + part(1)) + part(2)


def grad_kernel(core_ref, mine_ref, tgt_ref, kern_ref, pred_ref, resid_ref, grad_ref, sum_ref):
    half, count = kern_ref.shape
    blocks = half // LANES
    sum_ref[...] = mine_ref[...].astype(f32).reshape(sum_ref.shape)
    for r in range(blocks):
        at = slice(r * LANES, (r + 1) * LANES)
        pred = read_pred(sum_ref, r, tgt_ref.shape[0], 2 * blocks)
        pred_ref[:, at] = pred
        tgt = tgt_ref[:, pl.ds(pl.multiple_of(core_ref[0] * half + r * LANES, LANES), LANES)]
        resid_ref[:, at] = (pred - tgt).astype(bf16)
    resid = resid_ref[...]
    col = 1024
    for i in range(count // col):
        at = slice(i * col, (i + 1) * col)
        grad_ref[:, at] = jnp.dot(resid, kern_ref[:, at], preferred_element_type=f32)


def own_grad(core, mine, targets, kern):
    half, count = kern.shape
    outs = targets.shape[0]
    return pl.pallas_call(
        grad_kernel,
        in_specs=[SMEM] + [VMEM] * 3,
        out_specs=[VMEM] * 3,
        out_shape=[
            jax.ShapeDtypeStruct((outs, half), f32),
            jax.ShapeDtypeStruct((outs, half), bf16),
            jax.ShapeDtypeStruct((outs, count), f32),
        ],
        scratch_shapes=[pltpu.VMEM((mine.shape[0] * PACK, LANES), f32)],
        compiler_params=pltpu.CompilerParams(vmem_limit_bytes=8 * MIB),
        cost_estimate=pl.CostEstimate(flops=512 * half * count, bytes_accessed=2 * half * count, transcendentals=0),
        name="own_grad",
    )(core, mine, targets, in_vmem(kern))


def finish_kernel(
    core_ref, idx_ref, mine_ref, got_ref, pred_ref, resid_ref, grad_ref, tgt_ref, damp_ref, eig_ref, w_ref, kern_ref,
    out_ref, out_pred_ref, sum_ref, moment_ref,
):
    half, count = kern_ref.shape
    core = core_ref[0]
    chips = mine_ref.shape[0]
    blocks = half // LANES
    outs = tgt_ref.shape[0]
    got = got_ref[...].astype(f32)
    sum_ref[...] = got.reshape(sum_ref.shape)
    out_pred_ref[:, pl.ds(pl.multiple_of(core * half, half), half)] = pred_ref[...]
    resids = []
    for r in range(blocks):
        at = pl.ds(pl.multiple_of((1 - core) * half + r * LANES, LANES), LANES)
        pred = read_pred(sum_ref, r, outs, 2 * blocks)
        out_pred_ref[:, at] = pred
        resids.append((pred - tgt_ref[:, at]).astype(bf16))
    other = jnp.concatenate(resids, axis=1)
    own = resid_ref[...]
    lines = chips * 2 * blocks
    for place, part in ((core, mine_ref[...].astype(f32)[:, : 2 * blocks]), (1 - core, swap_halves(got[:, : 2 * blocks], 1))):
        moment_ref[pl.ds(pl.multiple_of(place * lines, lines), lines), :] = part.reshape(lines, LANES)
    col = 1024
    turns = count // col
    products = [(n, r) for n in range(2) for r in range(blocks)]
    per = 2 * len(products) // turns
    coeff, delta = 0.0, None
    for i in range(turns):
        at = slice(i * col, (i + 1) * col)
        grad = grad_ref[:, at] + jnp.dot(other, kern_ref[:, at], preferred_element_type=f32)
        out_ref[:, at] = w_ref[:, at] - 2.0 * grad
        for n, r in products[i * per : (i + 1) * per]:
            moment = moment_ref[pl.ds(n * blocks + r, 2 * chips, stride=2 * blocks), :].astype(bf16)
            resid = (own, other)[n][:, r * LANES : (r + 1) * LANES]
            coeff += lax.dot_general(resid, moment, NT, preferred_element_type=f32)
        if (i + 1) * per == len(products):
            delta = 2.0 * lax.dot_general(
                coeff * damp_ref[...], eig_ref[...], NT, precision=lax.Precision.HIGHEST, preferred_element_type=f32
            )
    lane = lax.broadcasted_iota(jnp.int32, (outs, LANES), 1)
    for k in range(delta.shape[1]):
        at = slice(k * LANES, (k + 1) * LANES)
        out_ref[:, at] += jnp.where(lane == idx_ref[k] - k * LANES, delta[:, k : k + 1], 0.0)


def finish(core, nys_index, mine, got, pred, resid, grad, targets, damping, eigvecs, weights, kern):
    chips, _, lanes = mine.shape
    return pl.pallas_call(
        finish_kernel,
        in_specs=[SMEM] * 2 + [VMEM] * 10,
        out_specs=[VMEM, VMEM],
        out_shape=[jax.ShapeDtypeStruct(weights.shape, f32), jax.ShapeDtypeStruct(targets.shape, f32)],
        scratch_shapes=[
            pltpu.VMEM((chips * PACK, lanes), f32),
            pltpu.VMEM((2 * chips * 2 * kern.shape[0] // LANES, lanes), f32),
        ],
        compiler_params=pltpu.CompilerParams(vmem_limit_bytes=12 * MIB),
        name="finish",
    )(core, nys_index, mine, got, pred, resid, grad, targets, damping[None, :], eigvecs, weights, in_vmem(kern))


def swap(x, axis):
    return lax.ppermute(x, axis, [(0, 1), (1, 0)])


def exchange(x, axes):
    return lax.all_to_all(x, axes, split_axis=0, concat_axis=0, tiled=True)


def body(pool, batch_index, targets, centers, weights, nys_index, eigvecs, damping):
    total = targets.shape[1]
    core = lax.axis_index("core").astype(jnp.int32)
    groups = lax.axis_size(CENTERS)
    share = total // (2 * groups)
    z = lax.axis_index("zl").astype(jnp.int32)
    place = jnp.stack([lax.axis_index(LOADER), core, lax.axis_index(PLANE) * 2 * share + z * share]).astype(jnp.int32)
    keep, give = pick_rows(place, batch_index, pool, share)
    rows = keep + swap(give, "core")
    across = lax.ppermute(rows, ("zh", "zl"), [(n, 3 - n) for n in range(4)])
    parts = (rows, swap(rows, "zh"), swap(rows, "zl"), across)
    rows = exchange(repeat_sum(z[None], parts, lax.axis_size(PLANE)), PLANE)
    w_half, cen_sq, head, *nys = prepare(nys_index, weights, eigvecs, centers)
    core = core[None]

    rows, cen_sq, w_half, head, nys = lax.optimization_barrier((rows, cen_sq, w_half, head, nys))
    own = rows.reshape(groups * share, D)
    other = swap(own, "core")

    kern_own, pred, held = kernel_values(w_half, centers, own, cen_sq, nys, head)
    moment, give = nystrom_terms(core, nys, own, other)
    kern_other, pred_give = kernel_values(w_half, held, other, cen_sq, (give, pred))
    packed = pack(moment, swap(give, "core"), pred, swap(pred_give, "core"))
    mine = exchange(sum_chips(exchange(packed, CHIPS)), CHIPS)
    got = swap(mine, "core")
    pred, resid, grad = own_grad(core, mine, targets, kern_own)
    return tuple(
        finish(core, nys_index, mine, got, pred, resid, grad, targets, damping, eigvecs, weights, kern_other)
    )


def solution(mesh):
    fine = Mesh(mesh.devices.reshape(2, 2, 4, 2, 4), ALL)
    return jax.shard_map(
        body,
        mesh=fine,
        in_specs=(
            P(LOADER, None),
            P(),
            P(),
            P(ALL, None),
            P(None, ALL),
            P(ALL),
            P(ALL, None),
            P(),
        ),
        out_specs=(P(None, ALL), P()),
        check_vma=False,
    )
```
